128 devices in a mesh: row: 8 (over y_lo, x), col: 8 (over z, core), seq: 2 (over y_hi).
Axes of the slice: x: 4, y: 4 (y_hi: 2, y_lo: 2; y = y_hi * 2 + y_lo), z: 4, core: 2. Of those that a mesh axis runs over, the one named last changes fastest.
Arguments:
- alignment_tensor: bfloat16 [256, 512, 256], P('seq', ('row', 'col')), may hold values from -6 to 6
- occupancy_matrix: int32 [256, 512], P(None, ('row', 'col')), may hold values from 0 to 1, as said below
- first_factor_matrix: bfloat16 [256, 32], replicated, may hold values from -0.375 to 0.375
- second_factor_matrix: bfloat16 [256, 32], replicated, may hold values from -0.375 to 0.375
- couple_factor_matrix: bfloat16 [1024, 128], replicated, may hold values from -3 to 3
- couple_increment_adjoint: bfloat16 [512, 512, 128], P(('row', 'seq'), 'col'), may hold values from -6 to 6
Outputs:
- couple_increment: bfloat16 [512, 512, 128], P(('row', 'seq'), 'col')
- alignment_adjoint: bfloat16 [256, 512, 256], P('seq', ('row', 'col'))
- first_factor_adjoint: float32 [256, 32], replicated
- second_factor_adjoint: float32 [256, 32], replicated
- couple_factor_adjoint: float32 [1024, 128], replicated
The draws below stay inside these ranges and needn't reach their ends.
Inputs may be any that keep to these rules, and one draw needn't show every extreme that they name: Row 0 of occupancy_matrix (the query) is all ones; every other sequence covers residues of one contiguous range with some gaps.
All inputs are finite; a program needn't handle non-finite values.
Results may differ from the reference program's by a relative error of at most 0.0076.
Values may be sent and summed in bfloat16 or wider, within the bound.
A program may use at most 192 MiB of HBM per device.

```python
import jax
import jax.numpy as jnp
from jax import lax

ALIGN_DIM = 256
PROJ_DIM = 32
CZ = 128
OUTER = 1024
Q = 8
NUM_HOMOLOGS = 256
NUM_AMINO = 512
N_COL = 8


def draw_occupancy_matrix(key, part):
    key = jax.random.fold_in(key, 7)
    key_start, key_length, key_keep = jax.random.split(key, 3)
    starts = jax.random.randint(key_start, (NUM_HOMOLOGS, 1), 0, NUM_AMINO)
    spans = jax.random.randint(key_length, (NUM_HOMOLOGS, 1), NUM_AMINO // 8, NUM_AMINO + 1)
    places = jnp.arange(NUM_AMINO, dtype=jnp.int32)[None, :]
    inside = (places >= starts) & (places < starts + spans)
    kept = jax.random.randint(key_keep, (NUM_HOMOLOGS, NUM_AMINO), 0, 100) < 85
    argument_tensor = (inside & kept).astype(jnp.int32)
    first = jnp.arange(NUM_HOMOLOGS, dtype=jnp.int32)[:, None] == 0
    return jnp.where(first, jnp.ones_like(argument_tensor), argument_tensor)


def steps_of(stream_key, shape, pieces, low, largest):
    loudness, own = 1.0, jax.random.fold_in(stream_key, 6)
    for dim, shards_of in pieces:
        draws = jnp.exp(jax.random.uniform(jax.random.fold_in(own, dim), (shards_of,), jnp.float32, low / len(pieces), largest / len(pieces)))
        loudness = loudness * jnp.repeat(draws, shape[dim] // shards_of).reshape([-1 if axis == dim else 1 for axis in range(len(shape))])
    return loudness


def centred(rng, extent, deviation, most, cuts=(), held_as=jnp.bfloat16):
    factor_of = steps_of(rng, extent, cuts, -0.22, 0.18) if cuts else 1.0
    drawn = jax.random.normal(rng, extent, jnp.float32) * deviation * factor_of
    return jnp.minimum(jnp.maximum(drawn, -most), most).astype(held_as)


def setup_inputs(seed: int = 0) -> dict:
    key_of = jax.random.split(jax.random.key(seed), 7)
    alignment_tensor = centred(key_of[0], (NUM_HOMOLOGS, NUM_AMINO, ALIGN_DIM), 1.0, 6.0, ((0, 2), (1, 64)))
    occupancy_matrix = draw_occupancy_matrix(jax.random.fold_in(key_of[6], 71), 0)
    first_factor_matrix = centred(key_of[2], (ALIGN_DIM, PROJ_DIM), ALIGN_DIM ** -0.5, 0.375)
    second_factor_matrix = centred(key_of[3], (ALIGN_DIM, PROJ_DIM), ALIGN_DIM ** -0.5, 0.375)
    couple_factor_matrix = centred(key_of[4], (OUTER, CZ), 0.5, 3.0)
    couple_increment_adjoint = centred(key_of[5], (NUM_AMINO, NUM_AMINO, CZ), 1.0, 6.0, ((0, 16), (1, 8)))
    return dict(alignment_tensor=alignment_tensor, occupancy_matrix=occupancy_matrix, first_factor_matrix=first_factor_matrix, second_factor_matrix=second_factor_matrix, couple_factor_matrix=couple_factor_matrix, couple_increment_adjoint=couple_increment_adjoint)


def apply_norming(alignment_tensor):
    argument_tensor = alignment_tensor.astype(jnp.float32)
    centered_input = argument_tensor - lax.optimization_barrier(jnp.mean(argument_tensor, axis=-1, keepdims=True))
    reciprocal_spread = lax.rsqrt(lax.optimization_barrier(jnp.mean(centered_input * centered_input, axis=-1, keepdims=True)) + 1e-05)
    return (centered_input * reciprocal_spread, reciprocal_spread)

def reference(alignment_tensor, occupancy_matrix, first_factor_matrix, second_factor_matrix, couple_factor_matrix, couple_increment_adjoint):
    homolog_rows, amino_positions = occupancy_matrix.shape
    block = Q * N_COL
    nblocks = amino_positions // block
    zscored_tensor, reciprocal_spread = apply_norming(alignment_tensor)
    rescaled_tensor = zscored_tensor.astype(jnp.bfloat16)
    maskf = occupancy_matrix.astype(jnp.float32)
    raveled_matrix = rescaled_tensor.reshape(-1, ALIGN_DIM)
    left = (maskf[:, :, None] * jnp.dot(raveled_matrix, first_factor_matrix, preferred_element_type=jnp.float32).reshape(homolog_rows, amino_positions, PROJ_DIM)).astype(jnp.bfloat16)
    right = (maskf[:, :, None] * jnp.dot(raveled_matrix, second_factor_matrix, preferred_element_type=jnp.float32).reshape(homolog_rows, amino_positions, PROJ_DIM)).astype(jnp.bfloat16)
    count = jnp.dot(maskf.T, maskf, precision=lax.Precision.HIGHEST)
    den = count + 0.001
    right32 = right.astype(jnp.float32)
    wo32 = couple_factor_matrix.astype(jnp.float32)

    def outer_of(index):
        lblock = lax.dynamic_slice_in_dim(left, index * block, block, 1).astype(jnp.float32)
        outer = jnp.einsum('sic,sje->ijce', lblock, right32).reshape(block, amino_positions, PROJ_DIM * PROJ_DIM)
        return (outer, lblock)

    def forward(index):
        outer, lblock = outer_of(index)
        value = jnp.dot(outer.reshape(-1, PROJ_DIM * PROJ_DIM), wo32, precision=lax.Precision.HIGHEST).reshape(block, amino_positions, CZ)
        dblock = lax.dynamic_slice_in_dim(den, index * block, block, 0)
        return (value / dblock[:, :, None]).astype(jnp.bfloat16)
    indexes = jnp.arange(nblocks, dtype=jnp.int32)
    couple_increment = lax.map(forward, indexes).reshape(amino_positions, amino_positions, CZ)

    def backward(carry, index):
        g_right, d_wo = carry
        outer, lblock = outer_of(index)
        dblock = lax.dynamic_slice_in_dim(den, index * block, block, 0)
        gblock = lax.dynamic_slice_in_dim(couple_increment_adjoint, index * block, block, 0).astype(jnp.float32)
        scaled = (gblock / dblock[:, :, None]).astype(jnp.bfloat16)
        d_outer = jnp.dot(scaled.reshape(-1, CZ), couple_factor_matrix.T, preferred_element_type=jnp.float32).astype(jnp.bfloat16)
        d_outer = d_outer.reshape(block, amino_positions, PROJ_DIM, PROJ_DIM).astype(jnp.float32)
        g_lblock = jnp.einsum('ijce,sje->sic', d_outer, right32)
        g_right = g_right + jnp.einsum('ijce,sic->sje', d_outer, lblock)
        d_wo = d_wo + jnp.dot(outer.reshape(-1, PROJ_DIM * PROJ_DIM).T, scaled.astype(jnp.float32).reshape(-1, CZ), precision=lax.Precision.HIGHEST)
        return ((g_right, d_wo), g_lblock)
    start = (jnp.zeros((homolog_rows, amino_positions, PROJ_DIM), jnp.float32), jnp.zeros((PROJ_DIM * PROJ_DIM, CZ), jnp.float32))
    (g_right, couple_factor_adjoint), g_blocks = lax.scan(backward, start, indexes)
    g_left = jnp.transpose(g_blocks, (1, 0, 2, 3)).reshape(homolog_rows, amino_positions, PROJ_DIM)
    g_left = maskf[:, :, None] * g_left
    g_right = maskf[:, :, None] * g_right
    gl_flat = g_left.reshape(-1, PROJ_DIM)
    gr_flat = g_right.reshape(-1, PROJ_DIM)
    normed32 = raveled_matrix.astype(jnp.float32)
    first_factor_adjoint = jnp.dot(normed32.T, gl_flat, precision=lax.Precision.HIGHEST)
    second_factor_adjoint = jnp.dot(normed32.T, gr_flat, precision=lax.Precision.HIGHEST)
    rescaled_adjoint = jnp.dot(gl_flat, first_factor_matrix.astype(jnp.float32).T, precision=lax.Precision.HIGHEST)
    rescaled_adjoint = rescaled_adjoint + jnp.dot(gr_flat, second_factor_matrix.astype(jnp.float32).T, precision=lax.Precision.HIGHEST)
    rescaled_adjoint = rescaled_adjoint.reshape(homolog_rows, amino_positions, ALIGN_DIM)
    addend_term = lax.optimization_barrier(jnp.mean(rescaled_adjoint * zscored_tensor, axis=-1, keepdims=True))
    alignment_adjoint = (reciprocal_spread * (rescaled_adjoint - lax.optimization_barrier(jnp.mean(rescaled_adjoint, axis=-1, keepdims=True)) - zscored_tensor * addend_term)).astype(jnp.bfloat16)
    return (couple_increment, alignment_adjoint, first_factor_adjoint, second_factor_adjoint, couple_factor_adjoint)
```

```python
import jax
import jax.numpy as jnp
from jax import lax
from jax.experimental import pallas as pl
from jax.experimental.pallas import tpu as pltpu
from jax.sharding import PartitionSpec as P

F32 = jnp.float32
BF16 = jnp.bfloat16
MESH = pl.DeviceIdType.MESH

NS = 128
NQ = 8
NCH = 256
NP = 32
NZ = 128
HALF = 512
PAIRS = 2048


def dot(a, b, ca, cb):
    return lax.dot_general(a, b, (((ca,), (cb,)), ((), ())), preferred_element_type=F32)


def both_halves(ref, rows):
    return jnp.concatenate([ref[0, rows, :], ref[1, rows, :]], axis=1)


def kernel(
    x_ref,
    occ_ref,
    w1_ref,
    w2_ref,
    wo_ref,
    cot_ref,
    inc_ref,
    aadj_ref,
    fa_ref,
    sa_ref,
    dwo_ref,
    msend,
    mrow,
    mcol,
    xh,
    rs,
    nres,
    tmp,
    lsend,
    rsend,
    lrecv,
    rrecv,
    wt,
    wsplit,
    wide,
    inv,
    s12,
    d2,
    lscr,
    rscr,
    beo,
    grsend,
    glsend,
    glrecv,
    grrecv,
    dwf,
    dwsend,
    dwrecv,
    fsend,
    frecv,
    f1,
    f1recv,
    f2,
    f2recv,
    e1,
    e1recv,
    e2,
    e2recv,
    e3,
    gown,
    oscr,
    ss_mr,
    rs_mr,
    ss_mc,
    rs_mc,
    ss_l,
    rs_l,
    ss_r,
    rs_r,
    ss_gl,
    rs_gl,
    ss_gr,
    rs_gr,
    ss_dw,
    rs_dw,
    ss_f,
    rs_f,
    ss_f1,
    rs_f1,
    ss_f2,
    rs_f2,
    ss_e1,
    rs_e1,
    ss_e2,
    rs_e2,
    ss_e3,
    rs_e3,
):
    r, c, q = lax.axis_index("row"), lax.axis_index("col"), lax.axis_index("seq")
    qd = c // 4
    other = (r, lax.rem(c + 1, 8), q)

    def far(src, dst, ssem, rsem, dev):
        return pltpu.make_async_remote_copy(
            src_ref=src, dst_ref=dst, send_sem=ssem, recv_sem=rsem, device_id=dev, device_id_type=MESH
        )

    def put(own, src, dst, ssem, rsem, dev):
        @pl.when(own)
        def _():
            pltpu.make_async_copy(src, dst, rsem).start()

        @pl.when(jnp.logical_not(own))
        def _():
            far(src, dst, ssem, rsem, dev).start()

    def arrived(slot, ssem, rsem):
        far(slot, slot, ssem, rsem, other).wait_recv()

    def sent(slot, ssem, rsem):
        far(slot, slot, ssem, rsem, other).wait_send()

    occ = occ_ref[...].astype(F32).astype(BF16)
    eye = (
        lax.broadcasted_iota(jnp.int32, (16, NQ), 0) == lax.broadcasted_iota(jnp.int32, (16, NQ), 1)
    ).astype(F32).astype(BF16)
    for h in range(2):
        msend[h] = dot(eye, occ[h * NS : (h + 1) * NS], 1, 1).astype(BF16)

    @pl.when(q == qd)
    def _():
        pltpu.make_async_copy(msend, mrow.at[lax.rem(c, 4)], rs_mr.at[lax.rem(c, 4)]).start()

        @pl.loop(1, 8)
        def _(t):
            far(
                msend, mrow.at[lax.rem(c, 4)], ss_mr.at[t], rs_mr.at[lax.rem(c, 4)], (r, lax.rem(c + t, 8), q)
            ).start()

    put(c == r, msend, mcol.at[c], ss_mc.at[0], rs_mc.at[c], (r, r, q))

    @pl.loop(1, 8)
    def _(t):
        far(msend, mcol.at[c], ss_mc.at[t], rs_mc.at[c], (lax.rem(r + t, 8), r, q)).start()

    @pl.loop(0, 8)
    def _(t):
        xb = x_ref[pl.ds(t * 16, 16)].astype(F32).reshape(128, NCH)
        xc = xb - jnp.mean(xb, axis=-1, keepdims=True)
        rstd = lax.rsqrt(jnp.mean(xc * xc, axis=-1, keepdims=True) + 1e-05)
        z = xc * rstd
        xh[0, pl.ds(t * 128, 128), :] = z[:, :128]
        xh[1, pl.ds(t * 128, 128), :] = z[:, 128:]
        rs[pl.ds(t * 128, 128), :] = jnp.broadcast_to(rstd, (128, 128))

    wt[0:NP, :] = w1_ref[...].astype(F32).T.astype(BF16)
    wt[NP:, :] = w2_ref[...].astype(F32).T.astype(BF16)
    mine = msend[q].astype(F32)
    for k in range(NQ):
        n = both_halves(xh, pl.ds(k, NS, stride=NQ)).astype(BF16)
        nres[k] = n
        p = dot(wt[...], n, 1, 1) * mine[k : k + 1, :]
        lsend[k * NP : (k + 1) * NP, :] = p[:NP].astype(BF16)
        tmp[pl.ds(k, NP, stride=NQ), :] = p[NP:]
    rsend[...] = tmp[...].astype(BF16)

    put(jnp.logical_and(c == r, True), rsend, rrecv.at[q, c], ss_r.at[0], rs_r.at[q, c], (r, r, q))

    @pl.loop(1, 16)
    def _(t):
        dev = (lax.rem(r + t // 2, 8), r, lax.rem(q + t, 2))
        far(rsend, rrecv.at[q, c], ss_r.at[t], rs_r.at[q, c], dev).start()

    put(q == qd, lsend, lrecv.at[q, lax.rem(c, 4)], ss_l.at[0], rs_l.at[q, lax.rem(c, 4)], (r, c, qd))

    @pl.loop(1, 8)
    def _(t):
        dev = (r, lax.rem(c + t, 8), qd)
        far(lsend, lrecv.at[q, lax.rem(c, 4)], ss_l.at[t], rs_l.at[q, lax.rem(c, 4)], dev).start()

    wide[...] = wo_ref[...].astype(F32)
    for e in range(NP):
        wsplit[e % 2, (e // 2) * NP : (e // 2 + 1) * NP, :] = wide[pl.ds(e, NP, stride=NP), :].astype(BF16)

    for m in range(4):
        arrived(mrow.at[m], ss_mr.at[m], rs_mr.at[m])
    for m in range(8):
        arrived(mcol.at[m], ss_mc.at[m], rs_mc.at[m])
    count = jnp.zeros((64, 32), F32)
    for h in range(2):
        rows = jnp.concatenate([mrow[m, h].astype(F32)[:NQ] for m in range(4)], axis=0).astype(BF16)
        cols = jnp.concatenate([mcol[m, h].astype(F32)[:NQ] for m in range(8)], axis=0).astype(BF16)
        count = count + dot(cols, rows, 1, 1)
    over = 1.0 / (count + 0.001)
    for k in range(16):
        parts = []
        for i in (k, k + 16):
            column = jnp.broadcast_to(over[:, i : i + 1], (64, NZ))
            inv[i] = column
            parts.append((cot_ref[i].astype(F32) * column).astype(BF16))
        s12[0, k * 128 : k * 128 + 64, :] = parts[0]
        s12[0, k * 128 + 64 : (k + 1) * 128, :] = parts[1]
        s12[1, k * 128 : k * 128 + 64, :] = parts[1]
        s12[1, k * 128 + 64 : (k + 1) * 128, :] = parts[0]

    low = lax.broadcasted_iota(jnp.int32, (NP, 128), 1) < 64

    @pl.loop(0, 8)
    def _(t):
        here = pl.ds(pl.multiple_of(t * 256, 256), 256)
        de = dot(wsplit[0], s12[0, here, :], 1, 1)
        do = dot(wsplit[1], s12[1, here, :], 1, 1)
        for u in range(2):
            at = pl.multiple_of((t * 2 + u) * NP, NP)
            for p in range(16):
                a = de[p * NP : (p + 1) * NP, u * 128 : (u + 1) * 128]
                b = do[p * NP : (p + 1) * NP, u * 128 : (u + 1) * 128]
                d2[0, pl.ds(at, NP), p * 128 : (p + 1) * 128] = jnp.where(low, a, b).astype(BF16)
                d2[1, pl.ds(at, NP), p * 128 : (p + 1) * 128] = jnp.where(low, b, a).astype(BF16)

    for h in range(2):
        for m in range(4):
            arrived(lrecv.at[h, m], ss_l.at[m], rs_l.at[h, m])
            lscr[m // 2, (m % 2) * 256 : (m % 2 + 1) * 256, h * NS : (h + 1) * NS] = lrecv[h, m]

    @pl.loop(0, 8)
    def _(t):
        here = pl.ds(pl.multiple_of(t * 256, 256), 256)
        a = dot(lscr[0], d2[0, :, here], 0, 0)
        b = dot(lscr[1], d2[1, :, here], 0, 0)
        for u in range(2):
            lanes = slice(u * 128, (u + 1) * 128)
            g = a[:, lanes] + pltpu.roll(b[:, lanes], 64, 1)
            for h in range(2):
                gt = g[h * NS : (h + 1) * NS].T
                at = pl.multiple_of((t * 2 + u) * 16, 16)
                for m in range(8):
                    both = jnp.concatenate([gt[m * 8 : m * 8 + 8], gt[64 + m * 8 : 72 + m * 8]], axis=0)
                    grsend[m, h, pl.ds(at, 16), :] = both.astype(BF16)

    put(
        r == c,
        grsend.at[c, q],
        grrecv.at[r, q],
        ss_gr.at[0],
        rs_gr.at[r, q],
        (c, c, q),
    )

    @pl.loop(1, 16)
    def _(t):
        m, h = lax.rem(c + t // 2, 8), lax.rem(q + t, 2)
        far(grsend.at[m, h], grrecv.at[r, q], ss_gr.at[t], rs_gr.at[r, q], (c, m, h)).start()

    for h in range(2):
        for m in range(8):
            arrived(rrecv.at[h, m], ss_r.at[m], rs_r.at[h, m])

    @pl.loop(0, 16)
    def _(p):
        rows = pl.ds(pl.multiple_of(p * 16, 16), 16)
        for h in range(2):
            got = [rrecv[h, m, rows, :].astype(F32) for m in range(8)]
            one = jnp.concatenate([g[:NQ] for g in got], axis=0).astype(BF16)
            two = jnp.concatenate([g[NQ:] for g in got], axis=0).astype(BF16)
            lanes = slice(h * NS, (h + 1) * NS)
            first = pl.ds(pl.multiple_of(p * 128, 128), 64)
            second = pl.ds(pl.multiple_of(p * 128 + 64, 64), 64)
            rscr[0, first, lanes] = one
            rscr[0, second, lanes] = two
            rscr[1, first, lanes] = two
            rscr[1, second, lanes] = one

    @pl.loop(0, 4)
    def _(t):
        m = lax.rem(c + t, 4)
        rows = pl.ds(pl.multiple_of(lax.rem(m, 2) * 256, 256), 256)
        g = dot(d2[m // 2, rows, :], rscr[m // 2], 1, 0)
        for h in range(2):
            glsend[m, h] = g[:, h * NS : (h + 1) * NS].astype(BF16)
            put(
                jnp.logical_and(4 * q + m == c, q == h),
                glsend.at[m, h],
                glrecv.at[c],
                ss_gl.at[m, h],
                rs_gl.at[c],
                (r, 4 * q + m, h),
            )

    @pl.loop(0, 8)
    def _(t):
        here = pl.ds(pl.multiple_of(t * 256, 256), 256)
        a = dot(lscr[0], rscr[0, here, :], 1, 1)
        b = dot(lscr[1], rscr[1, here, :], 1, 1)
        for u in range(2):
            at = pl.ds(pl.multiple_of((t * 2 + u) * NP, NP), NP)
            for k in range(16):
                va = a[k * NP : (k + 1) * NP, u * 128 : (u + 1) * 128]
                vb = b[k * NP : (k + 1) * NP, u * 128 : (u + 1) * 128]
                beo[0, at, k * 128 : (k + 1) * 128] = jnp.where(low, va, vb).astype(BF16)
                beo[1, at, k * 128 : (k + 1) * 128] = jnp.where(low, vb, va).astype(BF16)

    for h in range(2):
        part = dot(beo[h], s12[h], 1, 0)
        for p in range(16):
            dwf[pl.ds(2 * p + h, NP, stride=NP), :] = part[p * NP : (p + 1) * NP]
    for m in range(8):
        dwsend[m] = dwf[m * 128 : (m + 1) * 128, :].astype(BF16)
    pltpu.make_async_copy(dwsend.at[c], dwrecv.at[c], rs_dw.at[c]).start()

    @pl.loop(1, 8)
    def _(t):
        m = lax.rem(c + t, 8)
        far(dwsend.at[m], dwrecv.at[c], ss_dw.at[t], rs_dw.at[c], (r, m, q)).start()

    @pl.loop(0, 8)
    def _(t):
        here = pl.ds(pl.multiple_of(t * 256, 256), 256)
        a = dot(wsplit[0], beo[0, :, here], 0, 0)
        b = dot(wsplit[1], beo[1, :, here], 0, 0)
        for u in range(2):
            lanes = slice(u * 128, (u + 1) * 128)
            o = (a[:, lanes] + pltpu.roll(b[:, lanes], 64, 1)).T
            k = t * 2 + u
            inc_ref[k] = (o[:64] * inv[k]).astype(BF16)
            inc_ref[k + 16] = (o[64:] * inv[k + 16]).astype(BF16)

    for m in range(8):
        arrived(dwrecv.at[m], ss_dw.at[m], rs_dw.at[m])
    total = dwrecv[0].astype(F32)
    for m in range(1, 8):
        total = total + dwrecv[m].astype(F32)
    e1[...] = total
    me = r * 2 + q
    pltpu.make_async_copy(e1.at[pl.ds(pl.multiple_of(me * 8, 8), 8), :], e1recv.at[me], rs_e1.at[me]).start()

    @pl.loop(1, 16)
    def _(t):
        m = lax.rem(me + t, 16)
        far(
            e1.at[pl.ds(pl.multiple_of(m * 8, 8), 8), :],
            e1recv.at[me],
            ss_e1.at[t],
            rs_e1.at[me],
            (m // 2, c, lax.rem(m, 2)),
        ).start()

    for m in range(8):
        arrived(glrecv.at[m], ss_gl.at[0, 0], rs_gl.at[m])
    for m in range(8):
        for h in range(2):
            arrived(grrecv.at[m, h], ss_gr.at[0], rs_gr.at[m, h])
    gl = glrecv[0].astype(F32)
    for m in range(1, 8):
        gl = gl + glrecv[m].astype(F32)
    gr = jnp.zeros((256, NS), F32)
    for m in range(8):
        for h in range(2):
            gr = gr + grrecv[m, h].astype(F32)
    tmp[...] = gr
    fsum = jnp.zeros((128, NCH), F32)
    for k in range(NQ):
        g = jnp.concatenate([gl[k * NP : (k + 1) * NP], tmp[pl.ds(k, NP, stride=NQ), :]], axis=0)
        g = g * mine[k : k + 1, :]
        high = g.astype(BF16)
        rest = (g - high.astype(F32)).astype(BF16)
        g2 = jnp.concatenate([high, rest], axis=0)
        gown[k] = g2
        fsum = fsum + dot(g2, nres[k], 1, 0)
    fsum = fsum[:64] + fsum[64:]
    for m in range(8):
        fsend[m] = fsum[m * 8 : (m + 1) * 8]
    pltpu.make_async_copy(fsend.at[c], frecv.at[c], rs_f.at[c]).start()

    @pl.loop(1, 8)
    def _(t):
        m = lax.rem(c + t, 8)
        far(fsend.at[m], frecv.at[c], ss_f.at[t], rs_f.at[c], (r, m, q)).start()

    w2x = jnp.concatenate([wt[...], wt[...]], axis=0)

    def adjoint(k):
        d = dot(gown[k], w2x, 0, 0)
        at = pl.ds(k, NS, stride=NQ)
        z = both_halves(xh, at)
        scale = rs[at, :]
        m1 = jnp.mean(d, axis=-1, keepdims=True)
        m2 = jnp.mean(d * z, axis=-1, keepdims=True)
        o = d - m1 - z * m2
        oscr[0, at, :] = scale * o[:, :128]
        oscr[1, at, :] = scale * o[:, 128:]

    for k in range(0, 2):
        adjoint(k)

    for m in range(16):
        arrived(e1recv.at[m], ss_e1.at[m], rs_e1.at[m])
    total = e1recv[0]
    for m in range(1, 16):
        total = total + e1recv[m]
    e2[...] = total
    pltpu.make_async_copy(e2, e2recv.at[me], rs_e2.at[me]).start()

    @pl.loop(1, 16)
    def _(t):
        m = lax.rem(me + t, 16)
        far(e2, e2recv.at[me], ss_e2.at[t], rs_e2.at[me], (m // 2, c, lax.rem(m, 2))).start()

    for m in range(8):
        arrived(frecv.at[m], ss_f.at[m], rs_f.at[m])
    total = frecv[0]
    for m in range(1, 8):
        total = total + frecv[m]
    f1[...] = total
    pltpu.make_async_copy(f1, f1recv.at[me], rs_f1.at[me]).start()

    @pl.loop(1, 16)
    def _(t):
        m = lax.rem(me + t, 16)
        far(f1, f1recv.at[me], ss_f1.at[t], rs_f1.at[me], (m // 2, c, lax.rem(m, 2))).start()

    for k in range(2, 5):
        adjoint(k)

    for m in range(16):
        arrived(e2recv.at[m], ss_e2.at[m], rs_e2.at[m])
    for m in range(16):
        e3[m * 8 : (m + 1) * 8, :] = e2recv[m]
    rows = pl.ds(pl.multiple_of(c * 128, 128), 128)
    pltpu.make_async_copy(e3, dwo_ref.at[rows, :], rs_e3.at[c]).start()

    @pl.loop(1, 8)
    def _(t):
        far(e3, dwo_ref.at[rows, :], ss_e3.at[t], rs_e3.at[c], (r, lax.rem(c + t, 8), q)).start()

    for m in range(16):
        arrived(f1recv.at[m], ss_f1.at[m], rs_f1.at[m])
    total = f1recv[0]
    for m in range(1, 16):
        total = total + f1recv[m]
    f2[...] = total
    pltpu.make_async_copy(f2, f2recv.at[c], rs_f2.at[c]).start()

    @pl.loop(1, 8)
    def _(t):
        far(f2, f2recv.at[c], ss_f2.at[t], rs_f2.at[c], (r, lax.rem(c + t, 8), q)).start()

    for k in range(5, 8):
        adjoint(k)

    @pl.loop(0, 8)
    def _(t):
        aadj_ref[pl.ds(t * 16, 16)] = both_halves(oscr, pl.ds(t * 128, 128)).reshape(16, NQ, NCH).astype(BF16)

    for m in range(8):
        arrived(f2recv.at[m], ss_f2.at[m], rs_f2.at[m])
    fa_ref[...] = jnp.concatenate([f2recv[m] for m in range(4)], axis=0).T
    sa_ref[...] = jnp.concatenate([f2recv[m] for m in range(4, 8)], axis=0).T
    for m in range(8):
        arrived(dwo_ref.at[pl.ds(m * 128, 128), :], ss_e3.at[m], rs_e3.at[m])

    @pl.when(q == qd)
    def _():
        @pl.loop(1, 8)
        def _(t):
            sent(msend, ss_mr.at[t], rs_mr.at[0])

    @pl.loop(1, 8)
    def _(t):
        sent(msend, ss_mc.at[t], rs_mc.at[0])
        sent(lsend, ss_l.at[t], rs_l.at[0, 0])
        sent(dwsend.at[0], ss_dw.at[t], rs_dw.at[0])
        sent(fsend.at[0], ss_f.at[t], rs_f.at[0])
        sent(f2, ss_f2.at[t], rs_f2.at[0])
        sent(e3, ss_e3.at[t], rs_e3.at[0])

    @pl.loop(1, 16)
    def _(t):
        sent(rsend, ss_r.at[t], rs_r.at[0, 0])
        sent(grsend.at[0, 0], ss_gr.at[t], rs_gr.at[0, 0])
        sent(f1, ss_f1.at[t], rs_f1.at[0])
        sent(e2, ss_e2.at[t], rs_e2.at[0])
        sent(e2, ss_e1.at[t], rs_e1.at[0])

    @pl.when(c != r)
    def _():
        sent(msend, ss_mc.at[0], rs_mc.at[0])
        sent(rsend, ss_r.at[0], rs_r.at[0, 0])
        sent(grsend.at[0, 0], ss_gr.at[0], rs_gr.at[0, 0])

    @pl.when(q != qd)
    def _():
        sent(lsend, ss_l.at[0], rs_l.at[0, 0])

    for m in range(4):
        for h in range(2):

            @pl.when(jnp.logical_not(jnp.logical_and(4 * q + m == c, q == h)))
            def _(m=m, h=h):
                sent(glsend.at[0, 0], ss_gl.at[m, h], rs_gl.at[0])


def local(x, occ, w1, w2, wo, cot):
    vmem = pl.BlockSpec(memory_space=pltpu.VMEM)
    dma = pltpu.SemaphoreType.DMA
    scratch = [
        pltpu.VMEM((2, 16, NS), BF16),
        pltpu.VMEM((4, 2, 16, NS), BF16),
        pltpu.VMEM((8, 2, 16, NS), BF16),
        pltpu.VMEM((2, 1024, 128), F32),
        pltpu.VMEM((1024, 128), F32),
        pltpu.VMEM((NQ, NS, NCH), BF16),
        pltpu.VMEM((256, NS), F32),
        pltpu.VMEM((256, NS), BF16),
        pltpu.VMEM((256, NS), BF16),
        pltpu.VMEM((2, 4, 256, NS), BF16),
        pltpu.VMEM((2, 8, 256, NS), BF16),
        pltpu.VMEM((64, NCH), BF16),
        pltpu.VMEM((2, HALF, NZ), BF16),
        pltpu.VMEM((1024, NZ), F32),
        pltpu.VMEM((32, 64, NZ), F32),
        pltpu.VMEM((2, PAIRS, NZ), BF16),
        pltpu.VMEM((2, HALF, PAIRS), BF16),
        pltpu.VMEM((2, HALF, 256), BF16),
        pltpu.VMEM((2, PAIRS, 256), BF16),
        pltpu.VMEM((2, HALF, PAIRS), BF16),
        pltpu.VMEM((8, 2, 256, NS), BF16),
        pltpu.VMEM((4, 2, 256, NS), BF16),
        pltpu.VMEM((8, 256, NS), BF16),
        pltpu.VMEM((8, 2, 256, NS), BF16),
        pltpu.VMEM((1024, NZ), F32),
        pltpu.VMEM((8, 128, NZ), BF16),
        pltpu.VMEM((8, 128, NZ), BF16),
        pltpu.VMEM((8, 8, NCH), F32),
        pltpu.VMEM((8, 8, NCH), F32),
        pltpu.VMEM((8, NCH), F32),
        pltpu.VMEM((16, 8, NCH), F32),
        pltpu.VMEM((8, NCH), F32),
        pltpu.VMEM((8, 8, NCH), F32),
        pltpu.VMEM((128, NZ), F32),
        pltpu.VMEM((16, 8, NZ), F32),
        pltpu.VMEM((8, NZ), F32),
        pltpu.VMEM((16, 8, NZ), F32),
        pltpu.VMEM((128, NZ), F32),
        pltpu.VMEM((NQ, 128, NS), BF16),
        pltpu.VMEM((2, 1024, 128), F32),
        dma((8,)),
        dma((4,)),
        dma((8,)),
        dma((8,)),
        dma((8,)),
        dma((2, 4)),
        dma((16,)),
        dma((2, 8)),
        dma((4, 2)),
        dma((8,)),
        dma((16,)),
        dma((8, 2)),
        dma((8,)),
        dma((8,)),
        dma((8,)),
        dma((8,)),
        dma((16,)),
        dma((16,)),
        dma((8,)),
        dma((8,)),
        dma((16,)),
        dma((16,)),
        dma((16,)),
        dma((16,)),
        dma((8,)),
        dma((8,)),
    ]
    return pl.pallas_call(
        kernel,
        out_shape=(
            jax.ShapeDtypeStruct((32, 64, NZ), BF16),
            jax.ShapeDtypeStruct((NS, NQ, NCH), BF16),
            jax.ShapeDtypeStruct((NCH, NP), F32),
            jax.ShapeDtypeStruct((NCH, NP), F32),
            jax.ShapeDtypeStruct((1024, NZ), F32),
        ),
        in_specs=[vmem] * 6,
        out_specs=(vmem,) * 5,
        scratch_shapes=scratch,
        compiler_params=pltpu.CompilerParams(vmem_limit_bytes=56 * 1024 * 1024, has_side_effects=True),
    )(x, occ, w1, w2, wo, cot)


def solution(mesh):
    placed = (
        P("seq", ("row", "col"), None),
        P(None, ("row", "col")),
        P(),
        P(),
        P(),
        P(("row", "seq"), "col", None),
    )
    return jax.shard_map(
        local,
        mesh=mesh,
        in_specs=placed,
        out_specs=(P(("row", "seq"), "col", None), P("seq", ("row", "col"), None), P(), P(), P()),
        check_vma=False,
    )
```

```python
import jax
import jax.numpy as jnp
from jax import lax
from jax.experimental import pallas as pl
from jax.experimental.pallas import tpu as pltpu
from jax.sharding import PartitionSpec as P

F32 = jnp.float32
BF16 = jnp.bfloat16
MESH = pl.DeviceIdType.MESH

NS = 128
NQ = 8
NCH = 256
NP = 32
NZ = 128
HALF = 512
PAIRS = 2048


def dot(a, b, ca, cb):
    return lax.dot_general(a, b, (((ca,), (cb,)), ((), ())), preferred_element_type=F32)


def both_halves(ref, rows):
    return jnp.concatenate([ref[0, rows, :], ref[1, rows, :]], axis=1)


def kernel(
    x_ref,
    occ_ref,
    w1_ref,
    w2_ref,
    wo_ref,
    cot_ref,
    inc_ref,
    aadj_ref,
    fa_ref,
    sa_ref,
    dwo_ref,
    msend,
    mrow,
    mcol,
    xh,
    rs,
    nres,
    tmp,
    lsend,
    rsend,
    lrecv,
    rrecv,
    wt,
    wsplit,
    wide,
    inv,
    s12,
    d2,
    lscr,
    rscr,
    beo,
    grsend,
    grrecv,
    grt,
    grown,
    glp,
    gls,
    gly,
    glz,
    gla,
    glown,
    dwf,
    dwsend,
    dwrecv,
    fsend,
    frecv,
    f1,
    f1recv,
    f2,
    f2recv,
    e1,
    e1recv,
    e2,
    e2recv,
    e3,
    gown,
    oscr,
    ss_mr,
    rs_mr,
    ss_mc,
    rs_mc,
    ss_l,
    rs_lx,
    rs_ly,
    rs_lsx,
    rs_lsy,
    ss_r,
    rs_r,
    ss_gl,
    rs_gs,
    rs_gz,
    rs_ga,
    rs_go,
    ss_gr,
    rs_gr,
    ss_gt,
    rs_gt,
    ss_dw,
    rs_dw,
    ss_f,
    rs_f,
    ss_f1,
    rs_f1,
    ss_f2,
    rs_f2,
    ss_e1,
    rs_e1,
    ss_e2,
    rs_e2,
    ss_e3,
    rs_e3,
):
    r, c, q = lax.axis_index("row"), lax.axis_index("col"), lax.axis_index("seq")
    inner = q == c // 4
    outside = jnp.logical_not(inner)
    diagonal = r == c
    me = r * 2 + q
    core, z = lax.rem(c, 2), c // 2
    parity = lax.rem(z, 2)
    sibling = (r, c + 1 - 2 * core, q)
    beside = (r, (z + 1 - 2 * parity) * 2 + core, q)
    across = (r, lax.rem(z + 3 - 2 * parity, 4) * 2 + core, q)
    turned = (c, r, q)
    opposite = (r, c, 1 - q)
    other = (r, lax.rem(c + 1, 8), q)

    def plane(t):
        m = lax.rem(me + t, 16)
        return m, (m // 2, c, lax.rem(m, 2))

    def line(t):
        m = lax.rem(c + t, 8)
        return m, (r, m, q)

    def far(src, dst, ssem, rsem, dev):
        return pltpu.make_async_remote_copy(
            src_ref=src, dst_ref=dst, send_sem=ssem, recv_sem=rsem, device_id=dev, device_id_type=MESH
        )

    def put(own, src, dst, ssem, rsem, dev):
        @pl.when(own)
        def _():
            pltpu.make_async_copy(src, dst, rsem).start()

        @pl.when(jnp.logical_not(own))
        def _():
            far(src, dst, ssem, rsem, dev).start()

    def arrived(slot, ssem, rsem):
        far(slot, slot, ssem, rsem, other).wait_recv()

    def sent(slot, ssem, rsem):
        far(slot, slot, ssem, rsem, other).wait_send()

    barrier = pltpu.get_barrier_semaphore()

    @pl.loop(1, 16)
    def _(t):
        pl.semaphore_signal(barrier, inc=1, device_id=plane(t)[1], device_id_type=MESH)

    @pl.loop(1, 8)
    def _(t):
        pl.semaphore_signal(barrier, inc=1, device_id=line(t)[1], device_id_type=MESH)

    @pl.when(jnp.logical_not(diagonal))
    def _():
        pl.semaphore_signal(barrier, inc=1, device_id=turned, device_id_type=MESH)

    occ = occ_ref[...].astype(F32)
    occ = jnp.concatenate([occ, jnp.zeros((8, 2 * NS), F32)], axis=0).astype(BF16)
    for h in range(2):
        msend[h] = occ[:, h * NS : (h + 1) * NS]

    @pl.loop(0, 8)
    def _(t):
        xb = x_ref[pl.ds(t * 16, 16)].astype(F32).reshape(128, NCH)
        xc = xb - jnp.mean(xb, axis=-1, keepdims=True)
        rstd = lax.rsqrt(jnp.mean(xc * xc, axis=-1, keepdims=True) + 1e-05)
        z = xc * rstd
        xh[0, pl.ds(t * 128, 128), :] = z[:, :128]
        xh[1, pl.ds(t * 128, 128), :] = z[:, 128:]
        rs[pl.ds(t * 128, 128), :] = jnp.broadcast_to(rstd, (128, 128))

    pl.semaphore_wait(barrier, jnp.where(diagonal, 22, 23))
    put(diagonal, msend, mcol.at[c], ss_mc.at[0], rs_mc.at[c], turned)

    @pl.when(inner)
    def _():
        m = lax.rem(c, 4)
        pltpu.make_async_copy(msend, mrow.at[m], rs_mr.at[m]).start()

        @pl.loop(1, 8)
        def _(t):
            far(msend, mrow.at[m], ss_mr.at[t], rs_mr.at[m], line(t)[1]).start()

    wt[0:NP, :] = w1_ref[...]
    wt[NP:, :] = w2_ref[...]
    mine = msend[q].astype(F32)
    for k in range(NQ):
        n = both_halves(xh, pl.ds(k, NS, stride=NQ)).astype(BF16)
        nres[k] = n
        p = dot(wt[...], n, 1, 1) * mine[k : k + 1, :]
        lsend[k * NP : (k + 1) * NP, :] = p[:NP].astype(BF16)
        tmp[pl.ds(k, NP, stride=NQ), :] = p[NP:]
    rsend[...] = tmp[...].astype(BF16)

    put(diagonal, rsend, rrecv.at[q, c], ss_r.at[0], rs_r.at[q, c], turned)
    put(inner, lsend, lrecv.at[lax.rem(c, 4), q], ss_l.at[0], rs_lx.at[q], opposite)

    wide[...] = wo_ref[...].astype(F32)
    for e in range(NP):
        wsplit[e % 2, (e // 2) * NP : (e // 2 + 1) * NP, :] = wide[pl.ds(e, NP, stride=NP), :].astype(BF16)

    arrived(mcol.at[r], ss_mc.at[0], rs_mc.at[r])

    @pl.loop(1, 8)
    def _(t):
        far(mcol.at[r], mcol.at[r], ss_mc.at[t], rs_mc.at[r], (lax.rem(r + t, 8), c, q)).start()

    arrived(rrecv.at[q, r], ss_r.at[0], rs_r.at[q, r])

    @pl.loop(1, 16)
    def _(t):
        far(rrecv.at[q, r], rrecv.at[q, r], ss_r.at[t], rs_r.at[q, r], plane(t)[1]).start()

    xslot = lax.rem(lax.rem(c, 4) + jnp.where(inner, 0, 2), 4)
    yslot = lax.rem(xslot + 2, 4)
    flip = 1 - 2 * core

    def left_on(t):
        h = lax.rem(q + t, 2)
        slot = lrecv.at[xslot, h]
        arrived(slot, ss_l.at[0], rs_lx.at[h])

        @pl.when(inner)
        def _():
            far(slot, slot, ss_l.at[1 + t], rs_lx.at[h], across).start()

        far(slot, slot, ss_l.at[3 + t], rs_ly.at[h], beside).start()
        far(slot, slot, ss_l.at[5 + t], rs_lsx.at[h], sibling).start()

    @pl.when(inner)
    def _():
        left_on(0)
        left_on(1)

    for m in range(4):
        arrived(mrow.at[m], ss_mr.at[m], rs_mr.at[m])
    for m in range(8):

        @pl.when(r != m)
        def _(m=m):
            arrived(mcol.at[m], ss_mc.at[m], rs_mc.at[m])

    count = jnp.zeros((64, 32), F32)
    for h in range(2):
        rows = jnp.concatenate([mrow[m, h].astype(F32)[:NQ] for m in range(4)], axis=0).astype(BF16)
        cols = jnp.concatenate([mcol[m, h].astype(F32)[:NQ] for m in range(8)], axis=0).astype(BF16)
        count = count + dot(cols, rows, 1, 1)
    over = 1.0 / (count + 0.001)
    for k in range(16):
        parts = []
        for i in (k, k + 16):
            column = jnp.broadcast_to(over[:, i : i + 1], (64, NZ))
            inv[i] = column
            parts.append((cot_ref[i].astype(F32) * column).astype(BF16))
        s12[0, k * 128 : k * 128 + 64, :] = parts[0]
        s12[0, k * 128 + 64 : (k + 1) * 128, :] = parts[1]
        s12[1, k * 128 : k * 128 + 64, :] = parts[1]
        s12[1, k * 128 + 64 : (k + 1) * 128, :] = parts[0]

    @pl.when(outside)
    def _():
        left_on(0)
        left_on(1)

    low = lax.broadcasted_iota(jnp.int32, (NP, 128), 1) < 64

    @pl.loop(0, 8)
    def _(t):
        here = pl.ds(pl.multiple_of(t * 256, 256), 256)
        de = dot(wsplit[0], s12[0, here, :], 1, 1)
        do = dot(wsplit[1], s12[1, here, :], 1, 1)
        for u in range(2):
            at = pl.multiple_of((t * 2 + u) * NP, NP)
            for p in range(16):
                a = de[p * NP : (p + 1) * NP, u * 128 : (u + 1) * 128]
                b = do[p * NP : (p + 1) * NP, u * 128 : (u + 1) * 128]
                d2[0, pl.ds(at, NP), p * 128 : (p + 1) * 128] = jnp.where(low, a, b).astype(BF16)
                d2[1, pl.ds(at, NP), p * 128 : (p + 1) * 128] = jnp.where(low, b, a).astype(BF16)

    for t in range(2):
        h = lax.rem(q + t, 2)
        slot = lrecv.at[yslot, h]
        arrived(slot, ss_l.at[0], rs_ly.at[h])
        far(slot, slot, ss_l.at[7 + t], rs_lsy.at[h], sibling).start()

    for h in range(2):
        arrived(lrecv.at[xslot + flip, h], ss_l.at[0], rs_lsx.at[h])
        arrived(lrecv.at[yslot + flip, h], ss_l.at[0], rs_lsy.at[h])
    for h in range(2):
        for m in range(4):
            lscr[m // 2, (m % 2) * 256 : (m % 2 + 1) * 256, h * NS : (h + 1) * NS] = lrecv[m, h]

    @pl.loop(0, 8)
    def _(t):
        here = pl.ds(pl.multiple_of(t * 256, 256), 256)
        a = dot(lscr[0], d2[0, :, here], 0, 0)
        b = dot(lscr[1], d2[1, :, here], 0, 0)
        for u in range(2):
            lanes = slice(u * 128, (u + 1) * 128)
            g = a[:, lanes] + pltpu.roll(b[:, lanes], 64, 1)
            for h in range(2):
                gt = g[h * NS : (h + 1) * NS].T
                at = pl.multiple_of((t * 2 + u) * 16, 16)
                for m in range(8):
                    both = jnp.concatenate([gt[m * 8 : m * 8 + 8], gt[64 + m * 8 : 72 + m * 8]], axis=0)
                    grsend[m, h, pl.ds(at, 16), :] = both.astype(BF16)

    @pl.loop(1, 16)
    def _(t):
        m, dev = plane(t)
        far(grsend.at[m // 2, lax.rem(m, 2)], grrecv.at[t], ss_gr.at[t], rs_gr.at[t], dev).start()

    for h in range(2):
        for m in range(8):

            @pl.when(jnp.logical_or(q != h, r != m))
            def _(h=h, m=m):
                arrived(rrecv.at[h, m], ss_r.at[m], rs_r.at[h, m])

    @pl.loop(0, 16)
    def _(p):
        rows = pl.ds(pl.multiple_of(p * 16, 16), 16)
        for h in range(2):
            got = [rrecv[h, m, rows, :].astype(F32) for m in range(8)]
            one = jnp.concatenate([g[:NQ] for g in got], axis=0).astype(BF16)
            two = jnp.concatenate([g[NQ:] for g in got], axis=0).astype(BF16)
            lanes = slice(h * NS, (h + 1) * NS)
            first = pl.ds(pl.multiple_of(p * 128, 128), 64)
            second = pl.ds(pl.multiple_of(p * 128 + 64, 64), 64)
            rscr[0, first, lanes] = one
            rscr[0, second, lanes] = two
            rscr[1, first, lanes] = two
            rscr[1, second, lanes] = one

    def left_piece(pp, k):
        rows = pl.ds(pl.multiple_of(k * 256, 256), 256)
        g = dot(d2[pp, rows, :], rscr[pp], 1, 0)
        for h in range(2):
            glp[pp * 2 + k, h] = g[:, h * NS : (h + 1) * NS].astype(BF16)

    for pp in range(2):
        left_piece(pp, 1 - core)
        far(glp.at[pp * 2 + 1 - core], gls.at[pp], ss_gl.at[pp], rs_gs.at[pp], sibling).start()
    for pp in range(2):
        left_piece(pp, core)

    @pl.loop(0, 8)
    def _(t):
        here = pl.ds(pl.multiple_of(t * 256, 256), 256)
        a = dot(lscr[0], rscr[0, here, :], 1, 1)
        b = dot(lscr[1], rscr[1, here, :], 1, 1)
        for u in range(2):
            at = pl.ds(pl.multiple_of((t * 2 + u) * NP, NP), NP)
            for k in range(16):
                va = a[k * NP : (k + 1) * NP, u * 128 : (u + 1) * 128]
                vb = b[k * NP : (k + 1) * NP, u * 128 : (u + 1) * 128]
                beo[0, at, k * 128 : (k + 1) * 128] = jnp.where(low, va, vb).astype(BF16)
                beo[1, at, k * 128 : (k + 1) * 128] = jnp.where(low, vb, va).astype(BF16)

    for pp in range(2):
        arrived(gls.at[pp], ss_gl.at[pp], rs_gs.at[pp])
    gly[...] = (glp[yslot].astype(F32) + gls[yslot // 2].astype(F32)).astype(BF16)
    far(gly, glz, ss_gl.at[2], rs_gz.at[0], beside).start()

    for h in range(2):
        part = dot(beo[h], s12[h], 1, 0)
        for p in range(16):
            dwf[pl.ds(2 * p + h, NP, stride=NP), :] = part[p * NP : (p + 1) * NP]
    for m in range(8):
        dwsend[m] = dwf[m * 128 : (m + 1) * 128, :].astype(BF16)
    pltpu.make_async_copy(dwsend.at[c], dwrecv.at[c], rs_dw.at[c]).start()

    @pl.loop(1, 8)
    def _(t):
        m = lax.rem(c + t, 8)
        far(dwsend.at[m], dwrecv.at[c], ss_dw.at[t], rs_dw.at[c], (r, m, q)).start()

    arrived(glz, ss_gl.at[2], rs_gz.at[0])
    gls[xslot // 2] = (
        glp[xslot].astype(F32) + gls[xslot // 2].astype(F32) + glz[...].astype(F32)
    ).astype(BF16)

    @pl.when(outside)
    def _():
        far(gls.at[xslot // 2], gla, ss_gl.at[3], rs_ga.at[0], across).start()

    @pl.loop(0, 8)
    def _(t):
        here = pl.ds(pl.multiple_of(t * 256, 256), 256)
        a = dot(wsplit[0], beo[0, :, here], 0, 0)
        b = dot(wsplit[1], beo[1, :, here], 0, 0)
        for u in range(2):
            lanes = slice(u * 128, (u + 1) * 128)
            o = (a[:, lanes] + pltpu.roll(b[:, lanes], 64, 1)).T
            k = t * 2 + u
            inc_ref[k] = (o[:64] * inv[k]).astype(BF16)
            inc_ref[k + 16] = (o[64:] * inv[k + 16]).astype(BF16)

    @pl.when(inner)
    def _():
        arrived(gla, ss_gl.at[3], rs_ga.at[0])
        glz[...] = (gls[xslot // 2].astype(F32) + gla[...].astype(F32)).astype(BF16)
        pltpu.make_async_copy(glz.at[q], glown, rs_go.at[0]).start()
        far(glz.at[1 - q], glown, ss_gl.at[4], rs_go.at[0], opposite).start()

    total = grsend[r, q].astype(F32)
    for t in range(1, 16):
        arrived(grrecv.at[t], ss_gr.at[t], rs_gr.at[t])
        total = total + grrecv[t].astype(F32)
    grt[...] = total.astype(BF16)
    put(diagonal, grt, grown, ss_gt.at[0], rs_gt.at[0], turned)

    for m in range(8):
        arrived(dwrecv.at[m], ss_dw.at[m], rs_dw.at[m])
    total = dwrecv[0].astype(F32)
    for m in range(1, 8):
        total = total + dwrecv[m].astype(F32)
    e1[...] = total
    pltpu.make_async_copy(e1.at[pl.ds(pl.multiple_of(me * 8, 8), 8), :], e1recv.at[me], rs_e1.at[me]).start()

    @pl.loop(1, 16)
    def _(t):
        m = lax.rem(me + t, 16)
        far(
            e1.at[pl.ds(pl.multiple_of(m * 8, 8), 8), :],
            e1recv.at[me],
            ss_e1.at[t],
            rs_e1.at[me],
            (m // 2, c, lax.rem(m, 2)),
        ).start()

    arrived(glown, ss_gl.at[4], rs_go.at[0])
    arrived(grown, ss_gt.at[0], rs_gt.at[0])
    gl = glown[...].astype(F32)
    tmp[...] = grown[...].astype(F32)
    fsum = jnp.zeros((128, NCH), F32)
    for k in range(NQ):
        g = jnp.concatenate([gl[k * NP : (k + 1) * NP], tmp[pl.ds(k, NP, stride=NQ), :]], axis=0)
        g = g * mine[k : k + 1, :]
        high = g.astype(BF16)
        rest = (g - high.astype(F32)).astype(BF16)
        g2 = jnp.concatenate([high, rest], axis=0)
        gown[k] = g2
        fsum = fsum + dot(g2, nres[k], 1, 0)
    fsum = fsum[:64] + fsum[64:]
    for m in range(8):
        fsend[m] = fsum[m * 8 : (m + 1) * 8]
    pltpu.make_async_copy(fsend.at[c], frecv.at[c], rs_f.at[c]).start()

    @pl.loop(1, 8)
    def _(t):
        m = lax.rem(c + t, 8)
        far(fsend.at[m], frecv.at[c], ss_f.at[t], rs_f.at[c], (r, m, q)).start()

    w2x = jnp.concatenate([wt[...], wt[...]], axis=0)

    def adjoint(k):
        d = dot(gown[k], w2x, 0, 0)
        at = pl.ds(k, NS, stride=NQ)
        z = both_halves(xh, at)
        scale = rs[at, :]
        m1 = jnp.mean(d, axis=-1, keepdims=True)
        m2 = jnp.mean(d * z, axis=-1, keepdims=True)
        o = d - m1 - z * m2
        oscr[0, at, :] = scale * o[:, :128]
        oscr[1, at, :] = scale * o[:, 128:]

    for k in range(0, 2):
        adjoint(k)

    for m in range(16):
        arrived(e1recv.at[m], ss_e1.at[m], rs_e1.at[m])
    total = e1recv[0]
    for m in range(1, 16):
        total = total + e1recv[m]
    e2[...] = total
    pltpu.make_async_copy(e2, e2recv.at[me], rs_e2.at[me]).start()

    @pl.loop(1, 16)
    def _(t):
        m = lax.rem(me + t, 16)
        far(e2, e2recv.at[me], ss_e2.at[t], rs_e2.at[me], (m // 2, c, lax.rem(m, 2))).start()

    for m in range(8):
        arrived(frecv.at[m], ss_f.at[m], rs_f.at[m])
    total = frecv[0]
    for m in range(1, 8):
        total = total + frecv[m]
    f1[...] = total
    pltpu.make_async_copy(f1, f1recv.at[me], rs_f1.at[me]).start()

    @pl.loop(1, 16)
    def _(t):
        m = lax.rem(me + t, 16)
        far(f1, f1recv.at[me], ss_f1.at[t], rs_f1.at[me], (m // 2, c, lax.rem(m, 2))).start()

    for k in range(2, 5):
        adjoint(k)

    for m in range(16):
        arrived(e2recv.at[m], ss_e2.at[m], rs_e2.at[m])
    for m in range(16):
        e3[m * 8 : (m + 1) * 8, :] = e2recv[m]
    rows = pl.ds(pl.multiple_of(c * 128, 128), 128)
    pltpu.make_async_copy(e3, dwo_ref.at[rows, :], rs_e3.at[c]).start()

    @pl.loop(1, 8)
    def _(t):
        far(e3, dwo_ref.at[rows, :], ss_e3.at[t], rs_e3.at[c], (r, lax.rem(c + t, 8), q)).start()

    for m in range(16):
        arrived(f1recv.at[m], ss_f1.at[m], rs_f1.at[m])
    total = f1recv[0]
    for m in range(1, 16):
        total = total + f1recv[m]
    f2[...] = total
    pltpu.make_async_copy(f2, f2recv.at[c], rs_f2.at[c]).start()

    @pl.loop(1, 8)
    def _(t):
        far(f2, f2recv.at[c], ss_f2.at[t], rs_f2.at[c], (r, lax.rem(c + t, 8), q)).start()

    for k in range(5, 8):
        adjoint(k)

    @pl.loop(0, 8)
    def _(t):
        aadj_ref[pl.ds(t * 16, 16)] = both_halves(oscr, pl.ds(t * 128, 128)).reshape(16, NQ, NCH).astype(BF16)

    for m in range(8):
        arrived(f2recv.at[m], ss_f2.at[m], rs_f2.at[m])
    fa_ref[...] = jnp.concatenate([f2recv[m] for m in range(4)], axis=0)
    sa_ref[...] = jnp.concatenate([f2recv[m] for m in range(4, 8)], axis=0)
    for m in range(8):
        arrived(dwo_ref.at[pl.ds(m * 128, 128), :], ss_e3.at[m], rs_e3.at[m])

    @pl.when(inner)
    def _():
        @pl.loop(1, 8)
        def _(t):
            sent(msend, ss_mr.at[t], rs_mr.at[0])

        for t in range(2):
            sent(lsend, ss_l.at[1 + t], rs_lx.at[0])
        sent(glown, ss_gl.at[4], rs_go.at[0])

    @pl.when(outside)
    def _():
        sent(lsend, ss_l.at[0], rs_lx.at[0])
        sent(glz, ss_gl.at[3], rs_ga.at[0])

    for t in range(3, 9):
        sent(lsend, ss_l.at[t], rs_lx.at[0])
    for t in range(3):
        sent(glz, ss_gl.at[t], rs_gz.at[0])

    @pl.loop(1, 8)
    def _(t):
        sent(msend, ss_mc.at[t], rs_mc.at[0])
        sent(dwsend.at[0], ss_dw.at[t], rs_dw.at[0])
        sent(fsend.at[0], ss_f.at[t], rs_f.at[0])
        sent(f2, ss_f2.at[t], rs_f2.at[0])
        sent(e3, ss_e3.at[t], rs_e3.at[0])

    @pl.loop(1, 16)
    def _(t):
        sent(rsend, ss_r.at[t], rs_r.at[0, 0])
        sent(rsend, ss_gr.at[t], rs_gr.at[0])
        sent(f1, ss_f1.at[t], rs_f1.at[0])
        sent(e2, ss_e2.at[t], rs_e2.at[0])
        sent(e2, ss_e1.at[t], rs_e1.at[0])

    @pl.when(jnp.logical_not(diagonal))
    def _():
        sent(msend, ss_mc.at[0], rs_mc.at[0])
        sent(rsend, ss_r.at[0], rs_r.at[0, 0])
        sent(grt, ss_gt.at[0], rs_gt.at[0])


def local(x, occ, w1, w2, wo, cot):
    vmem = pl.BlockSpec(memory_space=pltpu.VMEM)
    dma = pltpu.SemaphoreType.DMA
    scratch = [
        pltpu.VMEM((2, 16, NS), BF16),
        pltpu.VMEM((4, 2, 16, NS), BF16),
        pltpu.VMEM((8, 2, 16, NS), BF16),
        pltpu.VMEM((2, 1024, 128), F32),
        pltpu.VMEM((1024, 128), F32),
        pltpu.VMEM((NQ, NS, NCH), BF16),
        pltpu.VMEM((256, NS), F32),
        pltpu.VMEM((256, NS), BF16),
        pltpu.VMEM((256, NS), BF16),
        pltpu.VMEM((4, 2, 256, NS), BF16),
        pltpu.VMEM((2, 8, 256, NS), BF16),
        pltpu.VMEM((64, NCH), BF16),
        pltpu.VMEM((2, HALF, NZ), BF16),
        pltpu.VMEM((1024, NZ), F32),
        pltpu.VMEM((32, 64, NZ), F32),
        pltpu.VMEM((2, PAIRS, NZ), BF16),
        pltpu.VMEM((2, HALF, PAIRS), BF16),
        pltpu.VMEM((2, HALF, 256), BF16),
        pltpu.VMEM((2, PAIRS, 256), BF16),
        pltpu.VMEM((2, HALF, PAIRS), BF16),
        pltpu.VMEM((8, 2, 256, NS), BF16),
        pltpu.VMEM((16, 256, NS), BF16),
        pltpu.VMEM((256, NS), BF16),
        pltpu.VMEM((256, NS), BF16),
        pltpu.VMEM((4, 2, 256, NS), BF16),
        pltpu.VMEM((2, 2, 256, NS), BF16),
        pltpu.VMEM((2, 256, NS), BF16),
        pltpu.VMEM((2, 256, NS), BF16),
        pltpu.VMEM((2, 256, NS), BF16),
        pltpu.VMEM((256, NS), BF16),
        pltpu.VMEM((1024, NZ), F32),
        pltpu.VMEM((8, 128, NZ), BF16),
        pltpu.VMEM((8, 128, NZ), BF16),
        pltpu.VMEM((8, 8, NCH), F32),
        pltpu.VMEM((8, 8, NCH), F32),
        pltpu.VMEM((8, NCH), F32),
        pltpu.VMEM((16, 8, NCH), F32),
        pltpu.VMEM((8, NCH), F32),
        pltpu.VMEM((8, 8, NCH), F32),
        pltpu.VMEM((128, NZ), F32),
        pltpu.VMEM((16, 8, NZ), F32),
        pltpu.VMEM((8, NZ), F32),
        pltpu.VMEM((16, 8, NZ), F32),
        pltpu.VMEM((128, NZ), F32),
        pltpu.VMEM((NQ, 128, NS), BF16),
        pltpu.VMEM((2, 1024, 128), F32),
        dma((8,)),
        dma((4,)),
        dma((8,)),
        dma((8,)),
        dma((9,)),
        dma((2,)),
        dma((2,)),
        dma((2,)),
        dma((2,)),
        dma((16,)),
        dma((2, 8)),
        dma((5,)),
        dma((2,)),
        dma((1,)),
        dma((1,)),
        dma((1,)),
        dma((16,)),
        dma((16,)),
        dma((1,)),
        dma((1,)),
        dma((8,)),
        dma((8,)),
        dma((8,)),
        dma((8,)),
        dma((16,)),
        dma((16,)),
        dma((8,)),
        dma((8,)),
        dma((16,)),
        dma((16,)),
        dma((16,)),
        dma((16,)),
        dma((8,)),
        dma((8,)),
    ]
    inc, aadj, fa, sa, dwo = pl.pallas_call(
        kernel,
        out_shape=(
            jax.ShapeDtypeStruct((32, 64, NZ), BF16),
            jax.ShapeDtypeStruct((NS, NQ, NCH), BF16),
            jax.ShapeDtypeStruct((NP, NCH), F32),
            jax.ShapeDtypeStruct((NP, NCH), F32),
            jax.ShapeDtypeStruct((1024, NZ), F32),
        ),
        in_specs=[vmem] * 6,
        out_specs=(vmem,) * 5,
        scratch_shapes=scratch,
        compiler_params=pltpu.CompilerParams(vmem_limit_bytes=56 * 1024 * 1024, has_side_effects=True, collective_id=0),
    )(x, occ.T, w1.T, w2.T, wo, cot)
    return inc, aadj, fa.T, sa.T, dwo


def solution(mesh):
    placed = (
        P("seq", ("row", "col"), None),
        P(None, ("row", "col")),
        P(),
        P(),
        P(),
        P(("row", "seq"), "col", None),
    )
    return jax.shard_map(
        local,
        mesh=mesh,
        in_specs=placed,
        out_specs=(P(("row", "seq"), "col", None), P("seq", ("row", "col"), None), P(), P(), P()),
        check_vma=False,
    )
```

```python
import jax
import jax.numpy as jnp
from jax import lax
from jax.experimental import pallas as pl
from jax.experimental.pallas import tpu as pltpu
from jax.sharding import PartitionSpec as P

F32 = jnp.float32
BF16 = jnp.bfloat16
MESH = pl.DeviceIdType.MESH

NS = 128
NQ = 8
NCH = 256
NP = 32
NZ = 128
HALF = 512
PAIRS = 2048


def dot(a, b, ca, cb):
    return lax.dot_general(a, b, (((ca,), (cb,)), ((), ())), preferred_element_type=F32)


def both_halves(ref, rows):
    return jnp.concatenate([ref[0, rows, :], ref[1, rows, :]], axis=1)


def kernel(
    x_ref,
    occ_ref,
    w1_ref,
    w2_ref,
    wo_hbm,
    cot_hbm,
    inc_hbm,
    aadj_ref,
    fa_ref,
    sa_ref,
    dwo_ref,
    wo_ref,
    cot_ref,
    inc_ref,
    msend,
    mrow,
    mcol,
    xh,
    rs,
    nres,
    tmp,
    lsend,
    rsend,
    lrecv,
    rrecv,
    wt,
    wsplit,
    wide,
    inv,
    s12,
    d2,
    lscr,
    lturn,
    wturn,
    rscr,
    beo,
    grsend,
    grrecv,
    grt,
    grown,
    glp,
    gls,
    glown,
    dwf,
    dwsend,
    dwrecv,
    fsend,
    frecv,
    f1,
    f1recv,
    f2,
    f2recv,
    e1,
    e1recv,
    e2,
    e3,
    gown,
    oscr,
    io_sem,
    ss_mr,
    rs_mr,
    ss_mc,
    rs_mc,
    ss_l,
    rs_l,
    rs_ls,
    ss_r,
    rs_r,
    ss_gl,
    rs_gs,
    rs_go,
    ss_gr,
    rs_gr,
    ss_gt,
    rs_gt,
    ss_dw,
    rs_dw,
    ss_f,
    rs_f,
    ss_f1,
    rs_f1,
    ss_f2,
    rs_f2,
    ss_e1,
    rs_e1,
    ss_e2,
    rs_e2,
    ss_e3,
    rs_e3,
):
    r, c, q = lax.axis_index("row"), lax.axis_index("col"), lax.axis_index("seq")
    inner = q == c // 4
    diagonal = r == c
    me = r * 2 + q
    core, z = lax.rem(c, 2), c // 2
    sibling = (r, c + 1 - 2 * core, q)
    turned = (c, r, q)
    other = (r, lax.rem(c + 1, 8), q)

    def plane(t):
        m = lax.rem(me + t, 16)
        return m, (m // 2, c, lax.rem(m, 2))

    def line(t):
        m = lax.rem(c + t, 8)
        return m, (r, m, q)

    def far(src, dst, ssem, rsem, dev):
        return pltpu.make_async_remote_copy(
            src_ref=src, dst_ref=dst, send_sem=ssem, recv_sem=rsem, device_id=dev, device_id_type=MESH
        )

    def put(own, src, dst, ssem, rsem, dev):
        @pl.when(own)
        def _():
            pltpu.make_async_copy(src, dst, rsem).start()

        @pl.when(jnp.logical_not(own))
        def _():
            far(src, dst, ssem, rsem, dev).start()

    def arrived(slot, ssem, rsem):
        far(slot, slot, ssem, rsem, other).wait_recv()

    def sent(slot, ssem, rsem):
        far(slot, slot, ssem, rsem, other).wait_send()

    load_wo = pltpu.make_async_copy(wo_hbm, wo_ref, io_sem.at[0])
    load_cot = pltpu.make_async_copy(cot_hbm, cot_ref, io_sem.at[1])
    save_inc = pltpu.make_async_copy(inc_ref, inc_hbm, io_sem.at[2])
    load_wo.start()
    load_cot.start()

    barrier = pltpu.get_barrier_semaphore()

    @pl.loop(1, 16)
    def _(t):
        pl.semaphore_signal(barrier, inc=1, device_id=plane(t)[1], device_id_type=MESH)

    @pl.loop(1, 8)
    def _(t):
        pl.semaphore_signal(barrier, inc=1, device_id=line(t)[1], device_id_type=MESH)

    y0, x0 = q * 2 + r // 4, lax.rem(r, 4)
    across = (r, lax.rem(z + 3 - 2 * lax.rem(z, 2), 4) * 2 + core, 1 - q)

    def at(y, x):
        return (lax.rem(y, 2) * 4 + x, c, y // 2)

    def along_x(t):
        return at(y0, lax.rem(x0 + t, 4))

    def along_y(t):
        return at(lax.rem(y0 + t, 4), x0)

    def along_z(t):
        return (r, lax.rem(z + t, 4) * 2 + core, q)

    def block(dy, dx, first, last):
        y, x = lax.rem(y0 + dy, 4), lax.rem(x0 + dx, 4)
        h, m = y // 2, lax.rem(y, 2) * 4 + x
        return rrecv.at[h, m, first:last, :], rs_r.at[h, m, first // 128]

    def mask_to(t):
        return (lax.rem(r + t, 8), r, q)

    def mask_from(t):
        return (c, lax.rem(c + t, 8), q)

    @pl.loop(1, 4)
    def _(t):
        dev = (r, lax.rem(z + t, 4) * 2 + core, 1 - q)
        pl.semaphore_signal(barrier, inc=1, device_id=dev, device_id_type=MESH)

    @pl.loop(1, 8)
    def _(t):
        pl.semaphore_signal(barrier, inc=1, device_id=mask_to(t), device_id_type=MESH)
        pl.semaphore_signal(barrier, inc=1, device_id=mask_from(t), device_id_type=MESH)

    @pl.when(jnp.logical_not(diagonal))
    def _():
        for dev in (mask_to(0), mask_from(0), turned):
            pl.semaphore_signal(barrier, inc=1, device_id=dev, device_id_type=MESH)

    occ = occ_ref[...].astype(F32)
    msend[...] = jnp.concatenate([occ[:, :NS], occ[:, NS:]], axis=0).astype(BF16)

    @pl.loop(0, 8)
    def _(t):
        xb = x_ref[pl.ds(t * 16, 16)].astype(F32).reshape(128, NCH)
        xc = xb - jnp.mean(xb, axis=-1, keepdims=True)
        rstd = lax.rsqrt(jnp.mean(xc * xc, axis=-1, keepdims=True) + 1e-05)
        z = xc * rstd
        xh[0, pl.ds(t * 128, 128), :] = z[:, :128]
        xh[1, pl.ds(t * 128, 128), :] = z[:, 128:]
        rs[pl.ds(t * 128, 128), :] = jnp.broadcast_to(rstd, (128, 128))

    pl.semaphore_wait(barrier, jnp.where(diagonal, 39, 42))
    put(diagonal, msend, mcol.at[c], ss_mc.at[0], rs_mc.at[c], mask_to(0))

    @pl.loop(1, 8)
    def _(t):
        far(msend, mcol.at[c], ss_mc.at[t], rs_mc.at[c], mask_to(t)).start()

    @pl.when(inner)
    def _():
        m = lax.rem(c, 4)
        pltpu.make_async_copy(msend, mrow.at[m], rs_mr.at[m]).start()

        @pl.loop(1, 8)
        def _(t):
            far(msend, mrow.at[m], ss_mr.at[t], rs_mr.at[m], line(t)[1]).start()

    wt[0:NP, :] = w1_ref[...]
    wt[NP:, :] = w2_ref[...]
    mine = msend[...].astype(F32)
    mine = jnp.where(q == 0, mine[:NQ], mine[NQ:])
    for k in range(NQ):
        n = both_halves(xh, pl.ds(k, NS, stride=NQ)).astype(BF16)
        nres[k] = n
        p = dot(wt[...], n, 1, 1) * mine[k : k + 1, :]
        lsend[k * NP : (k + 1) * NP, :] = p[:NP].astype(BF16)
        tmp[pl.ds(k, NP, stride=NQ), :] = p[NP:]
    rsend[...] = tmp[...].astype(BF16)

    mine_of_line = lax.rem(jnp.where(inner, z, z + 3 - 2 * lax.rem(z, 2)), 2)
    seq_of_line = jnp.where(inner, q, 1 - q)
    given = lrecv.at[mine_of_line * 2 + core, seq_of_line]
    given_mark = rs_l.at[mine_of_line, seq_of_line]

    def left_along():
        for t in range(1, 4):
            far(given, given, ss_l.at[t], given_mark, along_z(t)).start()
        far(given, given, ss_l.at[4], rs_ls.at[mine_of_line, seq_of_line], sibling).start()

    @pl.when(inner)
    def _():
        lrecv[lax.rem(c, 4), q] = lsend[...]
        left_along()

    @pl.when(jnp.logical_not(inner))
    def _():
        far(lsend, lrecv.at[lax.rem(c, 4), q], ss_l.at[0], rs_l.at[lax.rem(c, 4) // 2, q], across).start()

    put(diagonal, rsend, rrecv.at[q, c], ss_r.at[0], rs_r.at[q, c, 0], turned)

    load_wo.wait()
    wide[...] = wo_ref[...].astype(F32)
    for e in range(NP):
        wsplit[(e % 2) * HALF + (e // 2) * NP : (e % 2) * HALF + (e // 2 + 1) * NP, :] = wide[pl.ds(e, NP, stride=NP), :].astype(BF16)

    wturn[...] = wsplit[...].T

    @pl.when(jnp.logical_not(inner))
    def _():
        arrived(given, ss_l.at[0], given_mark)
        left_along()

    came, mark = block(0, 0, 0, 256)
    arrived(came, ss_r.at[0], mark)
    for t in range(1, 4):
        far(came, came, ss_r.at[t], mark, along_x(t)).start()
        far(came, came, ss_r.at[3 + t], mark, along_y(t)).start()

    for m in range(4):
        arrived(mrow.at[m], ss_mr.at[m], rs_mr.at[m])
    for m in range(8):
        arrived(mcol.at[m], ss_mc.at[m], rs_mc.at[m])

    count = jnp.zeros((64, 32), F32)
    across_lo = jnp.zeros((16, 128), F32)
    across_hi = jnp.zeros((16, 128), F32)
    for h in range(2):
        rows = jnp.concatenate([mrow[m].astype(F32)[h * NQ : (h + 1) * NQ] for m in range(4)], axis=0).astype(BF16)
        groups = [mcol[m].astype(F32)[h * NQ : (h + 1) * NQ] for m in range(8)]
        cols = jnp.concatenate(groups, axis=0).astype(BF16)
        twice = jnp.concatenate([g for g in groups for _ in range(2)], axis=0).astype(BF16)
        count = count + dot(cols, rows, 1, 1)
        across_lo = across_lo + dot(rows[:16], twice, 1, 1)
        across_hi = across_hi + dot(rows[16:], twice, 1, 1)
    lane = lax.broadcasted_iota(jnp.int32, (NP, 128), 1)
    low = lax.rem(lane // 8, 2) == 0
    inv[...] = 1.0 / (jnp.where(low[:16], across_lo, across_hi) + 0.001)
    over = 1.0 / (count + 0.001)
    load_cot.wait()
    for k in range(16):
        lo, hi = [
            cot_ref[i].astype(F32) * jnp.broadcast_to(over[:, i : i + 1], (64, NZ)) for i in (k, k + 16)
        ]
        pairs = [(lo[m * 8 : m * 8 + 8], hi[m * 8 : m * 8 + 8]) for m in range(8)]
        here = slice(k * 128, (k + 1) * 128)
        s12[0, here, :] = jnp.concatenate([g for a, b in pairs for g in (a, b)], axis=0).astype(BF16)
        s12[1, here, :] = jnp.concatenate([g for a, b in pairs for g in (b, a)], axis=0).astype(BF16)

    def outer_adjoint(t):
        here = pl.ds(pl.multiple_of(t * 256, 256), 256)
        even, odd = wsplit[:HALF], wsplit[HALF:]
        plain, turned_s = s12[0, here, :], s12[1, here, :]
        halves = (
            (dot(even, plain, 1, 1), dot(odd, turned_s, 1, 1)),
            (dot(even, turned_s, 1, 1), dot(odd, plain, 1, 1)),
        )
        for u in range(2):
            for half, (a, b) in enumerate(halves):
                at = pl.ds(pl.multiple_of(half * HALF + (t * 2 + u) * NP, NP), NP)
                for p in range(16):
                    va = a[p * NP : (p + 1) * NP, u * 128 : (u + 1) * 128]
                    vb = b[p * NP : (p + 1) * NP, u * 128 : (u + 1) * 128]
                    d2[at, p * 128 : (p + 1) * 128] = jnp.where(low, va, vb).astype(BF16)

    pl.loop(0, 4)(outer_adjoint)

    for t in range(1, 4):
        zt = lax.rem(z + t, 4)
        in_half = zt // 2 == q
        pp = lax.rem(jnp.where(in_half, zt, zt + 3 - 2 * lax.rem(zt, 2)), 2)
        h = jnp.where(in_half, q, 1 - q)
        slot = lrecv.at[pp * 2 + core, h]
        arrived(slot, ss_l.at[0], rs_l.at[pp, h])
        far(slot, slot, ss_l.at[4 + t], rs_ls.at[pp, h], sibling).start()

    for t in range(1, 4):
        whole, mark = block(0, t, 0, 256)
        arrived(whole, ss_r.at[0], mark)
        half, mark = block(0, t, 0, 128)
        for u in range(1, 4):
            far(half, half, ss_r.at[3 + t * 3 + u], mark, along_y(u)).start()
        whole, mark = block(t, 0, 0, 256)
        arrived(whole, ss_r.at[0], mark)
        half, mark = block(t, 0, 128, 256)
        for u in range(1, 4):
            far(half, half, ss_r.at[12 + t * 3 + u], mark, along_x(u)).start()

    pl.loop(4, 8)(outer_adjoint)

    for pp in range(2):
        for h in range(2):
            arrived(lrecv.at[pp * 2 + 1 - core, h], ss_l.at[0], rs_ls.at[pp, h])
    for h in range(2):
        for m in range(4):
            lscr[m * 256 : (m + 1) * 256, h * NS : (h + 1) * NS] = lrecv[m, h]
            lturn[h * NS : (h + 1) * NS, m * 256 : (m + 1) * 256] = lrecv[m, h].T

    @pl.loop(0, 8)
    def _(t):
        here = pl.ds(pl.multiple_of(t * 256, 256), 256)
        a = dot(lturn[...], d2[:, here], 1, 0).astype(BF16)
        for u in range(2):
            at = pl.ds(pl.multiple_of((t * 2 + u) * 16, 16), 16)
            for h in range(2):
                gt = a[h * NS : (h + 1) * NS, u * 128 : (u + 1) * 128].T
                for m in range(8):
                    grsend[m, h, at, :] = gt[m * 16 : (m + 1) * 16]

    @pl.loop(1, 16)
    def _(t):
        m, dev = plane(t)
        far(grsend.at[m // 2, lax.rem(m, 2)], grrecv.at[t], ss_gr.at[t], rs_gr.at[t], dev).start()

    for t in range(1, 4):
        for u in range(1, 4):
            for first in (0, 128):
                half, mark = block(t, u, first, first + 128)
                arrived(half, ss_r.at[0], mark)

    @pl.loop(0, 16)
    def _(p):
        rows = pl.ds(pl.multiple_of(p * 16, 16), 16)
        for h in range(2):
            lanes = slice(h * NS, (h + 1) * NS)
            for m in range(8):
                at = pl.ds(pl.multiple_of(p * 128 + m * 16, 16), 16)
                v = rrecv[h, m, rows, :]
                w = v.astype(F32)
                rscr[0, at, lanes] = v
                rscr[1, at, lanes] = jnp.concatenate([w[8:], w[:8]], axis=0).astype(BF16)

    def outer_product(t):
        here = pl.ds(pl.multiple_of(t * 256, 256), 256)
        a = dot(lscr[...], rscr[0, here, :], 1, 1)
        b = dot(lscr[...], rscr[1, here, :], 1, 1)
        for u in range(2):
            lanes = slice(u * 128, (u + 1) * 128)
            even = pl.ds(pl.multiple_of((t * 2 + u) * NP, NP), NP)
            odd = pl.ds(pl.multiple_of(HALF + (t * 2 + u) * NP, NP), NP)
            for k in range(16):
                lo = slice(k * NP, (k + 1) * NP)
                hi = slice(HALF + k * NP, HALF + (k + 1) * NP)
                beo[even, k * 128 : (k + 1) * 128] = jnp.where(low, a[lo, lanes], b[hi, lanes]).astype(BF16)
                beo[odd, k * 128 : (k + 1) * 128] = jnp.where(low, b[lo, lanes], a[hi, lanes]).astype(BF16)

    pl.loop(0, 4)(outer_product)

    pl.loop(4, 8)(outer_product)

    part = dot(beo[...], s12[0], 1, 0)
    for h in range(2):
        for p in range(16):
            dwf[pl.ds(2 * p + h, NP, stride=NP), :] = part[h * HALF + p * NP : h * HALF + (p + 1) * NP]
    for m in range(8):
        dwsend[m] = dwf[m * 128 : (m + 1) * 128, :].astype(BF16)
    pltpu.make_async_copy(dwsend.at[c], dwrecv.at[c], rs_dw.at[c]).start()

    @pl.loop(1, 8)
    def _(t):
        m = lax.rem(c + t, 8)
        far(dwsend.at[m], dwrecv.at[c], ss_dw.at[t], rs_dw.at[c], (r, m, q)).start()

    def left_piece(pp, k):
        rows = pl.ds(pl.multiple_of((pp * 2 + k) * 256, 256), 256)
        g = dot(d2[rows, :], rscr[0], 1, 0)
        for h in range(2):
            glp[pp * 2 + k, h] = g[:, h * NS : (h + 1) * NS].astype(BF16)

    for pp in range(2):
        left_piece(pp, 1 - core)
        far(glp.at[pp * 2 + 1 - core], gls.at[pp], ss_gl.at[pp], rs_gs.at[pp], sibling).start()
    for pp in range(2):
        left_piece(pp, core)

    def update(t):
        here = pl.ds(pl.multiple_of(t * 256, 256), 256)
        a = dot(wturn[...], beo[:, here], 1, 0)
        for u in range(2):
            k = t * 2 + u
            o = (a[:, u * 128 : (u + 1) * 128] * inv[pl.ds(k, 1), :]).astype(BF16).T.astype(F32)
            inc_ref[k] = jnp.concatenate([o[m * 16 : m * 16 + 8] for m in range(8)], axis=0).astype(BF16)
            inc_ref[k + 16] = jnp.concatenate([o[m * 16 + 8 : m * 16 + 16] for m in range(8)], axis=0).astype(BF16)

    pl.loop(0, 4)(update)

    for pp in range(2):
        arrived(gls.at[pp], ss_gl.at[pp], rs_gs.at[pp])
        m = pp * 2 + core
        for h in range(2):
            glp[m, h] = (glp[m, h].astype(F32) + gls[pp, h].astype(F32)).astype(BF16)
            put(
                jnp.logical_and(2 * q + pp == z, q == h),
                glp.at[m, h],
                glown.at[z],
                ss_gl.at[2 + pp * 2 + h],
                rs_go.at[z],
                (r, 4 * q + m, h),
            )

    total = grsend[r, q].astype(F32)
    for t in range(1, 16):
        arrived(grrecv.at[t], ss_gr.at[t], rs_gr.at[t])
        total = total + grrecv[t].astype(F32)
    grt[...] = total.astype(BF16)
    put(diagonal, grt, grown, ss_gt.at[0], rs_gt.at[0], turned)

    pl.loop(4, 8)(update)
    save_inc.start()

    for m in range(8):
        arrived(dwrecv.at[m], ss_dw.at[m], rs_dw.at[m])
    total = dwrecv[0].astype(F32)
    for m in range(1, 8):
        total = total + dwrecv[m].astype(F32)
    e1[...] = total

    @pl.loop(1, 16)
    def _(t):
        m, dev = plane(t)
        far(e1.at[pl.ds(pl.multiple_of(m * 8, 8), 8), :], e1recv.at[t], ss_e1.at[t], rs_e1.at[t], dev).start()

    for m in range(4):
        arrived(glown.at[m], ss_gl.at[2], rs_go.at[m])
    arrived(grown, ss_gt.at[0], rs_gt.at[0])
    gl = glown[0].astype(F32)
    for m in range(1, 4):
        gl = gl + glown[m].astype(F32)
    tmp[...] = grown[...].astype(F32)
    fsum = jnp.zeros((128, NCH), F32)
    for k in range(NQ):
        g = jnp.concatenate([gl[k * NP : (k + 1) * NP], tmp[pl.ds(k, NP, stride=NQ), :]], axis=0)
        g = g * mine[k : k + 1, :]
        high = g.astype(BF16)
        rest = (g - high.astype(F32)).astype(BF16)
        g2 = jnp.concatenate([high, rest], axis=0)
        gown[k] = g2
        fsum = fsum + dot(g2, nres[k], 1, 0)
    fsum = fsum[:64] + fsum[64:]
    for m in range(8):
        fsend[m] = fsum[m * 8 : (m + 1) * 8]
    pltpu.make_async_copy(fsend.at[c], frecv.at[c], rs_f.at[c]).start()

    @pl.loop(1, 8)
    def _(t):
        m = lax.rem(c + t, 8)
        far(fsend.at[m], frecv.at[c], ss_f.at[t], rs_f.at[c], (r, m, q)).start()

    total = e1[pl.ds(pl.multiple_of(me * 8, 8), 8), :]
    for t in range(1, 16):
        arrived(e1recv.at[t], ss_e1.at[t], rs_e1.at[t])
        total = total + e1recv[t]
    e2[...] = total
    e3[pl.ds(pl.multiple_of(me * 8, 8), 8), :] = total

    @pl.loop(1, 16)
    def _(t):
        m, dev = plane(t)
        far(e2, e3.at[pl.ds(pl.multiple_of(me * 8, 8), 8), :], ss_e2.at[t], rs_e2.at[me], dev).start()

    w2x = jnp.concatenate([wt[...], wt[...]], axis=0)

    def adjoint(k):
        d = dot(gown[k], w2x, 0, 0)
        at = pl.ds(k, NS, stride=NQ)
        z = both_halves(xh, at)
        scale = rs[at, :]
        m1 = jnp.mean(d, axis=-1, keepdims=True)
        m2 = jnp.mean(d * z, axis=-1, keepdims=True)
        o = d - m1 - z * m2
        oscr[0, at, :] = scale * o[:, :128]
        oscr[1, at, :] = scale * o[:, 128:]

    for k in range(0, 3):
        adjoint(k)

    for m in range(8):
        arrived(frecv.at[m], ss_f.at[m], rs_f.at[m])
    total = frecv[0]
    for m in range(1, 8):
        total = total + frecv[m]
    f1[...] = total
    pltpu.make_async_copy(f1, f1recv.at[me], rs_f1.at[me]).start()

    @pl.loop(1, 16)
    def _(t):
        m = lax.rem(me + t, 16)
        far(f1, f1recv.at[me], ss_f1.at[t], rs_f1.at[me], (m // 2, c, lax.rem(m, 2))).start()

    for m in range(16):

        @pl.when(me != m)
        def _(m=m):
            arrived(e3.at[m * 8 : (m + 1) * 8, :], ss_e2.at[m], rs_e2.at[m])

    chunk = dwo_ref.at[pl.ds(pl.multiple_of(c * 128, 128), 128), :]
    pltpu.make_async_copy(e3, chunk, rs_e3.at[c]).start()
    far(e3, chunk, ss_e3.at[0], rs_e3.at[c], sibling).start()

    @pl.loop(1, 4)
    def _(t):
        far(e3, chunk, ss_e3.at[t], rs_e3.at[c], (r, lax.rem(z + t, 4) * 2 + core, q)).start()

    for k in range(3, 5):
        adjoint(k)

    for m in range(16):
        arrived(f1recv.at[m], ss_f1.at[m], rs_f1.at[m])
    total = f1recv[0]
    for m in range(1, 16):
        total = total + f1recv[m]
    f2[...] = total
    pltpu.make_async_copy(f2, f2recv.at[c], rs_f2.at[c]).start()

    @pl.loop(1, 8)
    def _(t):
        far(f2, f2recv.at[c], ss_f2.at[t], rs_f2.at[c], (r, lax.rem(c + t, 8), q)).start()

    for k in range(5, 8):
        adjoint(k)

    @pl.loop(0, 8)
    def _(t):
        aadj_ref[pl.ds(t * 16, 16)] = both_halves(oscr, pl.ds(t * 128, 128)).reshape(16, NQ, NCH).astype(BF16)

    for m in range(8):
        arrived(f2recv.at[m], ss_f2.at[m], rs_f2.at[m])
    fa_ref[...] = jnp.concatenate([f2recv[m] for m in range(4)], axis=0)
    sa_ref[...] = jnp.concatenate([f2recv[m] for m in range(4, 8)], axis=0)
    for t in range(1, 4):
        m = lax.rem(z + t, 4) * 2 + core
        chunk = dwo_ref.at[pl.ds(pl.multiple_of(m * 128, 128), 128), :]
        arrived(chunk, ss_e3.at[0], rs_e3.at[m])
        far(chunk, chunk, ss_e3.at[3 + t], rs_e3.at[m], sibling).start()

    for t in range(4):
        m = lax.rem(z + t, 4) * 2 + 1 - core
        arrived(dwo_ref.at[pl.ds(pl.multiple_of(m * 128, 128), 128), :], ss_e3.at[0], rs_e3.at[m])
    arrived(e3, ss_e3.at[0], rs_e3.at[c])
    save_inc.wait()

    @pl.when(inner)
    def _():
        @pl.loop(1, 8)
        def _(t):
            sent(msend, ss_mr.at[t], rs_mr.at[0])

    for t in range(1, 8):
        sent(lsend, ss_l.at[t], rs_l.at[0, 0])
    for t in range(1, 7):
        sent(rsend, ss_r.at[t], rs_r.at[0, 0, 0])
    for t in range(7, 25):
        sent(rsend.at[0:128, :], ss_r.at[t], rs_r.at[0, 0, 0])
    for t in range(2):
        sent(gls.at[0], ss_gl.at[t], rs_gs.at[0])
    for pp in range(2):
        for h in range(2):

            @pl.when(jnp.logical_not(jnp.logical_and(2 * q + pp == z, q == h)))
            def _(pp=pp, h=h):
                sent(lsend, ss_gl.at[2 + pp * 2 + h], rs_go.at[0])

    @pl.when(jnp.logical_not(inner))
    def _():
        sent(lsend, ss_l.at[0], rs_l.at[0, 0])

    for t in range(7):
        sent(e3, ss_e3.at[t], rs_e3.at[0])

    @pl.loop(1, 8)
    def _(t):
        sent(msend, ss_mc.at[t], rs_mc.at[0])
        sent(dwsend.at[0], ss_dw.at[t], rs_dw.at[0])
        sent(fsend.at[0], ss_f.at[t], rs_f.at[0])
        sent(f2, ss_f2.at[t], rs_f2.at[0])

    @pl.loop(1, 16)
    def _(t):
        sent(rsend, ss_gr.at[t], rs_gr.at[0])
        sent(f1, ss_f1.at[t], rs_f1.at[0])
        sent(e2, ss_e2.at[t], rs_e2.at[0])
        sent(e2, ss_e1.at[t], rs_e1.at[0])

    @pl.when(jnp.logical_not(diagonal))
    def _():
        sent(msend, ss_mc.at[0], rs_mc.at[0])
        sent(rsend, ss_r.at[0], rs_r.at[0, 0, 0])
        sent(grt, ss_gt.at[0], rs_gt.at[0])


def hand_over(*refs):
    into = [pltpu.make_async_copy(refs[i], refs[10 + i], refs[15].at[i]) for i in range(5)]
    out = [pltpu.make_async_copy(refs[10 + i], refs[5 + i], refs[16].at[i]) for i in range(5)]
    for copy in into:
        copy.start()
    for i in range(5):
        into[i].wait()
        out[i].start()
    for copy in out:
        copy.wait()


def local(x, occ, w1, w2, wo, cot):
    vmem = pl.BlockSpec(memory_space=pltpu.VMEM)
    hbm = pl.BlockSpec(memory_space=pl.ANY)
    dma = pltpu.SemaphoreType.DMA
    scratch = [
        pltpu.VMEM((1024, NZ), BF16),
        pltpu.VMEM((32, 64, NZ), BF16),
        pltpu.VMEM((32, 64, NZ), BF16),
        pltpu.VMEM((16, NS), BF16),
        pltpu.VMEM((4, 16, NS), BF16),
        pltpu.VMEM((8, 16, NS), BF16),
        pltpu.VMEM((2, 1024, 128), F32),
        pltpu.VMEM((1024, 128), F32),
        pltpu.VMEM((NQ, NS, NCH), BF16),
        pltpu.VMEM((256, NS), F32),
        pltpu.VMEM((256, NS), BF16),
        pltpu.VMEM((256, NS), BF16),
        pltpu.VMEM((4, 2, 256, NS), BF16),
        pltpu.VMEM((2, 8, 256, NS), BF16),
        pltpu.VMEM((64, NCH), BF16),
        pltpu.VMEM((1024, NZ), BF16),
        pltpu.VMEM((1024, NZ), F32),
        pltpu.VMEM((16, 128), F32),
        pltpu.VMEM((2, PAIRS, NZ), BF16),
        pltpu.VMEM((1024, PAIRS), BF16),
        pltpu.VMEM((1024, 256), BF16),
        pltpu.VMEM((256, 1024), BF16),
        pltpu.VMEM((NZ, 1024), BF16),
        pltpu.VMEM((2, PAIRS, 256), BF16),
        pltpu.VMEM((1024, PAIRS), BF16),
        pltpu.VMEM((8, 2, 256, NS), BF16),
        pltpu.VMEM((16, 256, NS), BF16),
        pltpu.VMEM((256, NS), BF16),
        pltpu.VMEM((256, NS), BF16),
        pltpu.VMEM((4, 2, 256, NS), BF16),
        pltpu.VMEM((2, 2, 256, NS), BF16),
        pltpu.VMEM((4, 256, NS), BF16),
        pltpu.VMEM((1024, NZ), F32),
        pltpu.VMEM((8, 128, NZ), BF16),
        pltpu.VMEM((8, 128, NZ), BF16),
        pltpu.VMEM((8, 8, NCH), F32),
        pltpu.VMEM((8, 8, NCH), F32),
        pltpu.VMEM((8, NCH), F32),
        pltpu.VMEM((16, 8, NCH), F32),
        pltpu.VMEM((8, NCH), F32),
        pltpu.VMEM((8, 8, NCH), F32),
        pltpu.VMEM((128, NZ), F32),
        pltpu.VMEM((16, 8, NZ), F32),
        pltpu.VMEM((8, NZ), F32),
        pltpu.VMEM((128, NZ), F32),
        pltpu.VMEM((NQ, 128, NS), BF16),
        pltpu.VMEM((2, 1024, 128), F32),
        dma((3,)),
        dma((8,)),
        dma((4,)),
        dma((8,)),
        dma((8,)),
        dma((8,)),
        dma((2, 2)),
        dma((2, 2)),
        dma((25,)),
        dma((2, 8, 2)),
        dma((6,)),
        dma((2,)),
        dma((4,)),
        dma((16,)),
        dma((16,)),
        dma((1,)),
        dma((1,)),
        dma((8,)),
        dma((8,)),
        dma((8,)),
        dma((8,)),
        dma((16,)),
        dma((16,)),
        dma((8,)),
        dma((8,)),
        dma((16,)),
        dma((16,)),
        dma((16,)),
        dma((16,)),
        dma((8,)),
        dma((8,)),
    ]
    inc, aadj, fa, sa, dwo = pl.pallas_call(
        kernel,
        out_shape=(
            jax.ShapeDtypeStruct((32, 64, NZ), BF16),
            jax.ShapeDtypeStruct((NS, NQ, NCH), BF16),
            jax.ShapeDtypeStruct((NP, NCH), F32),
            jax.ShapeDtypeStruct((NP, NCH), F32),
            jax.ShapeDtypeStruct((1024, NZ), F32),
        ),
        in_specs=[vmem] * 4 + [hbm] * 2,
        out_specs=(hbm,) + (vmem,) * 4,
        scratch_shapes=scratch,
        compiler_params=pltpu.CompilerParams(vmem_limit_bytes=56 * 1024 * 1024, has_side_effects=True, collective_id=0),
    )(x, occ.T, w1.T, w2.T, wo, cot)
    outs = (inc, aadj, fa, sa, dwo)
    inc, aadj, fa, sa, dwo = pl.pallas_call(
        hand_over,
        out_shape=tuple(jax.ShapeDtypeStruct(o.shape, o.dtype) for o in outs),
        in_specs=[hbm] * 5,
        out_specs=(hbm,) * 5,
        scratch_shapes=[pltpu.VMEM(o.shape, o.dtype) for o in outs] + [dma((5,)), dma((5,))],
        compiler_params=pltpu.CompilerParams(vmem_limit_bytes=56 * 1024 * 1024),
    )(*outs)
    return inc, aadj, fa.T, sa.T, dwo


def solution(mesh):
    placed = (
        P("seq", ("row", "col"), None),
        P(None, ("row", "col")),
        P(),
        P(),
        P(),
        P(("row", "seq"), "col", None),
    )
    return jax.shard_map(
        local,
        mesh=mesh,
        in_specs=placed,
        out_specs=(P(("row", "seq"), "col", None), P("seq", ("row", "col"), None), P(), P(), P()),
        check_vma=False,
    )
```

```python
import jax
import jax.numpy as jnp
from jax import lax
from jax.experimental import pallas as pl
from jax.experimental.pallas import tpu as pltpu
from jax.sharding import PartitionSpec as P

F32 = jnp.float32
BF16 = jnp.bfloat16
MESH = pl.DeviceIdType.MESH

NS = 128
NQ = 8
NCH = 256
NP = 32
NZ = 128
HALF = 512
PAIRS = 2048


def dot(a, b, ca, cb):
    return lax.dot_general(a, b, (((ca,), (cb,)), ((), ())), preferred_element_type=F32)


def both_halves(ref, rows):
    return jnp.concatenate([ref[0, rows, :], ref[1, rows, :]], axis=1)


def kernel(
    x_hbm,
    occ_hbm,
    w1_hbm,
    w2_hbm,
    wo_hbm,
    cot_hbm,
    inc_hbm,
    aadj_hbm,
    fa_ref,
    sa_ref,
    dwo_ref,
    x_ref,
    occ_ref,
    w1_ref,
    w2_ref,
    wo_ref,
    cot_ref,
    inc_ref,
    aadj_ref,
    msend,
    mrow,
    mcol,
    xh,
    rs,
    nres,
    tmp,
    lsend,
    rsend,
    lrecv,
    rrecv,
    wt,
    wsplit,
    wide,
    inv,
    over_lanes,
    dpre,
    s12,
    d2,
    lscr,
    lturn,
    wturn,
    rscr,
    beo,
    grsend,
    gra,
    grb,
    grc,
    grt,
    grown,
    glp,
    gls,
    glown,
    dwf,
    dwsend,
    dwrecv,
    fsend,
    frecv,
    f1,
    f1recv,
    f2,
    f2recv,
    e1,
    e1recv,
    e2,
    e3,
    gown,
    oscr,
    io_sem,
    ss_mr,
    rs_mr,
    ss_mc,
    rs_mc,
    ss_l,
    rs_l,
    rs_ls,
    ss_r,
    rs_r,
    ss_gl,
    rs_gs,
    rs_go,
    ss_gr,
    rs_gr,
    ss_gt,
    rs_gt,
    ss_dw,
    rs_dw,
    ss_f,
    rs_f,
    ss_f1,
    rs_f1,
    ss_f2,
    rs_f2,
    ss_e1,
    rs_e1,
    ss_e2,
    rs_e2,
    ss_e3,
    rs_e3,
):
    r, c, q = lax.axis_index("row"), lax.axis_index("col"), lax.axis_index("seq")
    inner = q == c // 4
    diagonal = r == c
    me = r * 2 + q
    core, z = lax.rem(c, 2), c // 2
    sibling = (r, c + 1 - 2 * core, q)
    holder = (
        lax.rem(r // 4 + core, 2) * 4 + lax.rem(lax.rem(r, 4) + 2 - z + r // 2 + 4, 4),
        r,
        q,
    )

    def held(m):
        dz = lax.rem(2 - lax.rem(m, 4) + lax.rem(c, 4) + 4, 4)
        return lax.rem(c // 2 + dz, 4) * 2 + lax.rem(m // 4 + c // 4, 2)

    def holder_row(m):
        dz = lax.rem(m // 2 - c // 2 + 4, 4)
        return lax.rem(c // 4 + lax.rem(m, 2), 2) * 4 + lax.rem(lax.rem(c, 4) + 2 - dz + 4, 4)

    owner = (c, held(r), q)
    other = (r, lax.rem(c + 1, 8), q)

    def plane(t):
        m = lax.rem(me + t, 16)
        return m, (m // 2, c, lax.rem(m, 2))

    def line(t):
        m = lax.rem(c + t, 8)
        return m, (r, m, q)

    def far(src, dst, ssem, rsem, dev):
        return pltpu.make_async_remote_copy(
            src_ref=src, dst_ref=dst, send_sem=ssem, recv_sem=rsem, device_id=dev, device_id_type=MESH
        )

    def put(own, src, dst, ssem, rsem, dev):
        @pl.when(own)
        def _():
            pltpu.make_async_copy(src, dst, rsem).start()

        @pl.when(jnp.logical_not(own))
        def _():
            far(src, dst, ssem, rsem, dev).start()

    def arrived(slot, ssem, rsem):
        far(slot, slot, ssem, rsem, other).wait_recv()

    def sent(slot, ssem, rsem):
        far(slot, slot, ssem, rsem, other).wait_send()

    load_wo = pltpu.make_async_copy(wo_hbm, wo_ref, io_sem.at[0])
    load_cot = pltpu.make_async_copy(cot_hbm, cot_ref, io_sem.at[1])
    save_inc = pltpu.make_async_copy(inc_ref, inc_hbm, io_sem.at[2])
    save_aadj = pltpu.make_async_copy(aadj_ref, aadj_hbm, io_sem.at[7])
    load_x = pltpu.make_async_copy(x_hbm, x_ref, io_sem.at[3])
    load_occ = pltpu.make_async_copy(occ_hbm, occ_ref, io_sem.at[4])
    load_w1 = pltpu.make_async_copy(w1_hbm, w1_ref, io_sem.at[5])
    load_w2 = pltpu.make_async_copy(w2_hbm, w2_ref, io_sem.at[6])
    for load in (load_x, load_occ, load_w1, load_w2, load_wo, load_cot):
        load.start()

    barrier = pltpu.get_barrier_semaphore()

    @pl.loop(1, 16)
    def _(t):
        pl.semaphore_signal(barrier, inc=1, device_id=plane(t)[1], device_id_type=MESH)

    @pl.loop(1, 8)
    def _(t):
        pl.semaphore_signal(barrier, inc=1, device_id=line(t)[1], device_id_type=MESH)

    y0, x0 = q * 2 + r // 4, lax.rem(r, 4)
    across = (r, lax.rem(z + 3 - 2 * lax.rem(z, 2), 4) * 2 + core, 1 - q)

    def at(y, x):
        return (lax.rem(y, 2) * 4 + x, c, y // 2)

    def along_x(t):
        return at(y0, lax.rem(x0 + t, 4))

    def along_y(t):
        return at(lax.rem(y0 + t, 4), x0)

    def along_z(t):
        return (r, lax.rem(z + t, 4) * 2 + core, q)

    def block(dy, dx, first, last):
        y, x = lax.rem(y0 + dy, 4), lax.rem(x0 + dx, 4)
        h, m = y // 2, lax.rem(y, 2) * 4 + x
        return rrecv.at[h, m, first:last, :], rs_r.at[h, m, first // 128]

    def mask_to(t):
        return (lax.rem(r + t, 8), r, q)

    def mask_from(t):
        return (c, lax.rem(c + t, 8), q)

    @pl.loop(1, 4)
    def _(t):
        dev = (r, lax.rem(z + t, 4) * 2 + core, 1 - q)
        pl.semaphore_signal(barrier, inc=1, device_id=dev, device_id_type=MESH)

    @pl.loop(1, 8)
    def _(t):
        pl.semaphore_signal(barrier, inc=1, device_id=mask_to(t), device_id_type=MESH)
        pl.semaphore_signal(barrier, inc=1, device_id=mask_from(t), device_id_type=MESH)

    for dev in (holder, owner):
        pl.semaphore_signal(barrier, inc=1, device_id=dev, device_id_type=MESH)

    @pl.when(jnp.logical_not(diagonal))
    def _():
        for dev in (mask_to(0), mask_from(0)):
            pl.semaphore_signal(barrier, inc=1, device_id=dev, device_id_type=MESH)

    load_occ.wait()
    occ = occ_ref[...].astype(F32)
    msend[...] = jnp.concatenate([occ[:, :NS], occ[:, NS:]], axis=0).astype(BF16)

    load_x.wait()
    @pl.loop(0, 8)
    def _(t):
        xb = x_ref[pl.ds(t * 16, 16)].astype(F32).reshape(128, NCH)
        xc = xb - jnp.mean(xb, axis=-1, keepdims=True)
        rstd = lax.rsqrt(jnp.mean(xc * xc, axis=-1, keepdims=True) + 1e-05)
        z = xc * rstd
        xh[0, pl.ds(t * 128, 128), :] = z[:, :128]
        xh[1, pl.ds(t * 128, 128), :] = z[:, 128:]
        rs[pl.ds(t * 128, 128), :] = jnp.broadcast_to(rstd, (128, 128))

    pl.semaphore_wait(barrier, jnp.where(diagonal, 41, 43))
    put(diagonal, msend, mcol.at[c], ss_mc.at[0], rs_mc.at[c], mask_to(0))

    @pl.loop(1, 8)
    def _(t):
        far(msend, mcol.at[c], ss_mc.at[t], rs_mc.at[c], mask_to(t)).start()

    @pl.when(inner)
    def _():
        m = lax.rem(c, 4)
        pltpu.make_async_copy(msend, mrow.at[m], rs_mr.at[m]).start()

        @pl.loop(1, 8)
        def _(t):
            far(msend, mrow.at[m], ss_mr.at[t], rs_mr.at[m], line(t)[1]).start()

    load_w1.wait()
    load_w2.wait()
    wt[0:NP, :] = w1_ref[...]
    wt[NP:, :] = w2_ref[...]
    mine = msend[...].astype(F32)
    mine = jnp.where(q == 0, mine[:NQ], mine[NQ:])
    for k in range(NQ):
        n = both_halves(xh, pl.ds(k, NS, stride=NQ)).astype(BF16)
        nres[k] = n
        p = dot(wt[...], n, 1, 1) * mine[k : k + 1, :]
        lsend[k * NP : (k + 1) * NP, :] = p[:NP].astype(BF16)
        tmp[pl.ds(k, NP, stride=NQ), :] = p[NP:]
    rsend[...] = tmp[...].astype(BF16)

    mine_of_line = lax.rem(jnp.where(inner, z, z + 3 - 2 * lax.rem(z, 2)), 2)
    seq_of_line = jnp.where(inner, q, 1 - q)
    given = lrecv.at[mine_of_line * 2 + core, seq_of_line]
    given_mark = rs_l.at[mine_of_line, seq_of_line]

    def left_along():
        for t in range(1, 4):
            far(given, given, ss_l.at[t], given_mark, along_z(t)).start()
        far(given, given, ss_l.at[4], rs_ls.at[mine_of_line, seq_of_line], sibling).start()

    @pl.when(inner)
    def _():
        lrecv[lax.rem(c, 4), q] = lsend[...]
        left_along()

    @pl.when(jnp.logical_not(inner))
    def _():
        far(lsend, lrecv.at[lax.rem(c, 4), q], ss_l.at[0], rs_l.at[lax.rem(c, 4) // 2, q], across).start()

    far(rsend, rrecv.at[q, holder[0]], ss_r.at[0], rs_r.at[q, holder[0], 0], holder).start()

    load_wo.wait()
    wide[...] = wo_ref[...].astype(F32)
    for e in range(NP):
        wsplit[(e % 2) * HALF + (e // 2) * NP : (e % 2) * HALF + (e // 2 + 1) * NP, :] = wide[pl.ds(e, NP, stride=NP), :].astype(BF16)

    wturn[...] = wsplit[...].T

    lane = lax.broadcasted_iota(jnp.int32, (NP, 128), 1)
    low = lax.rem(lane // 8, 2) == 0

    def in_turn(lo, hi):
        return jnp.concatenate([v[m * 8 : m * 8 + 8] for m in range(8) for v in (lo, hi)], axis=0).astype(BF16)

    load_cot.wait()
    for k in range(16):
        lo, hi = cot_ref[k].astype(F32), cot_ref[k + 16].astype(F32)
        s12[0, k * 128 : (k + 1) * 128, :] = in_turn(lo, hi)
        s12[1, k * 128 : (k + 1) * 128, :] = in_turn(hi, lo)

    def outer_adjoint(t):
        here = pl.ds(pl.multiple_of(t * 256, 256), 256)
        even, odd = wsplit[:HALF], wsplit[HALF:]
        plain, turned_s = s12[0, here, :], s12[1, here, :]
        halves = (
            (dot(even, plain, 1, 1), dot(odd, turned_s, 1, 1)),
            (dot(even, turned_s, 1, 1), dot(odd, plain, 1, 1)),
        )
        for u in range(2):
            for half, (a, b) in enumerate(halves):
                at = pl.ds(pl.multiple_of(half * HALF + (t * 2 + u) * NP, NP), NP)
                for p in range(16):
                    va = a[p * NP : (p + 1) * NP, u * 128 : (u + 1) * 128]
                    vb = b[p * NP : (p + 1) * NP, u * 128 : (u + 1) * 128]
                    dpre[at, p * 128 : (p + 1) * 128] = jnp.where(low, va, vb)

    pl.loop(0, 4)(outer_adjoint)

    @pl.when(jnp.logical_not(inner))
    def _():
        arrived(given, ss_l.at[0], given_mark)
        left_along()

    came, mark = block(0, 0, 0, 256)
    arrived(came, ss_r.at[0], mark)
    for t in range(1, 4):
        far(came, came, ss_r.at[t], mark, along_x(t)).start()
        far(came, came, ss_r.at[3 + t], mark, along_y(t)).start()

    pl.loop(4, 8)(outer_adjoint)

    for m in range(4):
        arrived(mrow.at[m], ss_mr.at[m], rs_mr.at[m])
    for m in range(8):
        arrived(mcol.at[m], ss_mc.at[m], rs_mc.at[m])

    count = jnp.zeros((64, 32), F32)
    count_lanes = jnp.zeros((32, 128), F32)
    for h in range(2):
        rows = jnp.concatenate([mrow[m].astype(F32)[h * NQ : (h + 1) * NQ] for m in range(4)], axis=0).astype(BF16)
        groups = [mcol[m].astype(F32)[h * NQ : (h + 1) * NQ] for m in range(8)]
        cols = jnp.concatenate(groups, axis=0).astype(BF16)
        twice = jnp.concatenate([g for g in groups for _ in range(2)], axis=0).astype(BF16)
        count = count + dot(cols, rows, 1, 1)
        count_lanes = count_lanes + dot(rows, twice, 1, 1)
    over_lanes[...] = 1.0 / (count_lanes + 0.001)
    inv[...] = jnp.where(low[:16], over_lanes[:16], over_lanes[16:])

    @pl.loop(0, 32)
    def _(i):
        rows = pl.ds(pl.multiple_of(i * NP, NP), NP)
        d2[rows, :] = (dpre[rows, :] * jnp.concatenate([over_lanes[pl.ds(i, 1), :]] * 16, axis=1)).astype(BF16)

    for t in range(1, 4):
        zt = lax.rem(z + t, 4)
        in_half = zt // 2 == q
        pp = lax.rem(jnp.where(in_half, zt, zt + 3 - 2 * lax.rem(zt, 2)), 2)
        h = jnp.where(in_half, q, 1 - q)
        slot = lrecv.at[pp * 2 + core, h]
        arrived(slot, ss_l.at[0], rs_l.at[pp, h])
        far(slot, slot, ss_l.at[4 + t], rs_ls.at[pp, h], sibling).start()

    for t in range(1, 4):
        whole, mark = block(0, t, 0, 256)
        arrived(whole, ss_r.at[0], mark)
        half, mark = block(0, t, 0, 128)
        for u in range(1, 4):
            far(half, half, ss_r.at[3 + t * 3 + u], mark, along_y(u)).start()
        whole, mark = block(t, 0, 0, 256)
        arrived(whole, ss_r.at[0], mark)
        half, mark = block(t, 0, 128, 256)
        for u in range(1, 4):
            far(half, half, ss_r.at[12 + t * 3 + u], mark, along_x(u)).start()

    for pp in range(2):
        for h in range(2):
            arrived(lrecv.at[pp * 2 + 1 - core, h], ss_l.at[0], rs_ls.at[pp, h])
    for h in range(2):
        for m in range(4):
            lscr[m * 256 : (m + 1) * 256, h * NS : (h + 1) * NS] = lrecv[m, h]
            lturn[h * NS : (h + 1) * NS, m * 256 : (m + 1) * 256] = lrecv[m, h].T

    @pl.loop(0, 8)
    def _(t):
        here = pl.ds(pl.multiple_of(t * 256, 256), 256)
        a = dot(lturn[...], d2[:, here], 1, 0).astype(BF16)
        for u in range(2):
            at = pl.ds(pl.multiple_of((t * 2 + u) * 16, 16), 16)
            for h in range(2):
                gt = a[h * NS : (h + 1) * NS, u * 128 : (u + 1) * 128].T
                for m in range(8):
                    row = holder_row(m)
                    grsend[h * 2 + row // 4, lax.rem(row, 4), at, :] = gt[m * 16 : (m + 1) * 16]

    for t in range(1, 4):
        y, x = lax.rem(y0 + t, 4), lax.rem(x0 + t, 4)
        far(grsend.at[y, :, 0:128, :], gra.at[0, t], ss_gr.at[t], rs_gr.at[0, t], along_y(t)).start()
        far(grsend.at[:, x, 128:256, :], gra.at[1, t], ss_gr.at[3 + t], rs_gr.at[1, t], along_x(t)).start()

    over = 1.0 / (count + 0.001)
    for k in range(16):
        lo, hi = [
            cot_ref[i].astype(F32) * jnp.broadcast_to(over[:, i : i + 1], (64, NZ)) for i in (k, k + 16)
        ]
        s12[0, k * 128 : (k + 1) * 128, :] = in_turn(lo, hi)
        s12[1, k * 128 : (k + 1) * 128, :] = in_turn(hi, lo)

    for t in range(1, 4):
        for u in range(1, 4):
            for first in (0, 128):
                half, mark = block(t, u, first, first + 128)
                arrived(half, ss_r.at[0], mark)

    @pl.loop(0, 16)
    def _(p):
        rows = pl.ds(pl.multiple_of(p * 16, 16), 16)
        for h in range(2):
            lanes = slice(h * NS, (h + 1) * NS)
            for m in range(8):
                at = pl.ds(pl.multiple_of(p * 128 + held(m) * 16, 16), 16)
                v = rrecv[h, m, rows, :]
                w = v.astype(F32)
                rscr[0, at, lanes] = v
                rscr[1, at, lanes] = jnp.concatenate([w[8:], w[:8]], axis=0).astype(BF16)

    def outer_product(t):
        here = pl.ds(pl.multiple_of(t * 256, 256), 256)
        a = dot(lscr[:HALF], rscr[0, here, :], 1, 1)
        b = dot(lscr[HALF:], rscr[1, here, :], 1, 1)
        for u in range(2):
            lanes = slice(u * 128, (u + 1) * 128)
            even = pl.ds(pl.multiple_of((t * 2 + u) * NP, NP), NP)
            odd = pl.ds(pl.multiple_of(HALF + (t * 2 + u) * NP, NP), NP)
            for k in range(16):
                lo = a[k * NP : (k + 1) * NP, lanes]
                hi = b[k * NP : (k + 1) * NP, lanes]
                beo[even, k * 128 : (k + 1) * 128] = jnp.where(low, lo, hi).astype(BF16)
                beo[odd, k * 128 : (k + 1) * 128] = jnp.where(low, hi, lo).astype(BF16)

    pl.loop(0, 4)(outer_product)

    pl.loop(4, 8)(outer_product)

    for i in range(2):
        for t in range(1, 4):
            arrived(gra.at[i, t], ss_gr.at[1], rs_gr.at[i, t])
        for n in range(4):
            own = grsend[n, x0, 128:256, :] if i else grsend[y0, n, 0:128, :]
            total = own.astype(F32)
            for t in range(1, 4):
                total = total + gra[i, t, n].astype(F32)
            grb[i, n] = total.astype(BF16)
        for t in range(1, 4):
            if i:
                far(grb.at[i, lax.rem(y0 + t, 4)], grc.at[i, t], ss_gr.at[9 + t], rs_gr.at[2 + i, t], along_y(t)).start()
            else:
                far(grb.at[i, lax.rem(x0 + t, 4)], grc.at[i, t], ss_gr.at[6 + t], rs_gr.at[2 + i, t], along_x(t)).start()

    for h in range(2):
        part = dot(beo[h * HALF : (h + 1) * HALF], s12[h], 1, 0)
        for p in range(16):
            dwf[pl.ds(2 * p + h, NP, stride=NP), :] = part[p * NP : (p + 1) * NP]
    for m in range(8):
        dwsend[m] = dwf[m * 128 : (m + 1) * 128, :].astype(BF16)
    pltpu.make_async_copy(dwsend.at[c], dwrecv.at[c], rs_dw.at[c]).start()

    @pl.loop(1, 8)
    def _(t):
        m = lax.rem(c + t, 8)
        far(dwsend.at[m], dwrecv.at[c], ss_dw.at[t], rs_dw.at[c], (r, m, q)).start()

    def left_piece(pp, k):
        rows = pl.ds(pl.multiple_of((pp * 2 + k) * 256, 256), 256)
        g = dot(d2[rows, :], rscr[0], 1, 0)
        for h in range(2):
            glp[pp * 2 + k, h] = g[:, h * NS : (h + 1) * NS].astype(BF16)

    for pp in range(2):
        left_piece(pp, 1 - core)
        far(glp.at[pp * 2 + 1 - core], gls.at[pp], ss_gl.at[pp], rs_gs.at[pp], sibling).start()
    for pp in range(2):
        left_piece(pp, core)

    for pp in range(2):
        arrived(gls.at[pp], ss_gl.at[pp], rs_gs.at[pp])
        m = pp * 2 + core
        for h in range(2):
            glp[m, h] = (glp[m, h].astype(F32) + gls[pp, h].astype(F32)).astype(BF16)
            put(
                jnp.logical_and(2 * q + pp == z, q == h),
                glp.at[m, h],
                glown.at[z],
                ss_gl.at[2 + pp * 2 + h],
                rs_go.at[z],
                (r, 4 * q + m, h),
            )

    for i in range(2):
        own = grb[i, y0] if i else grb[i, x0]
        total = own.astype(F32)
        for t in range(1, 4):
            arrived(grc.at[i, t], ss_gr.at[7], rs_gr.at[2 + i, t])
            total = total + grc[i, t].astype(F32)
        grt[i * 128 : (i + 1) * 128, :] = total.astype(BF16)
    far(grt, grown, ss_gt.at[0], rs_gt.at[0], owner).start()

    low_rows = lax.rem(lax.broadcasted_iota(jnp.int32, (NZ, 128), 1) // 8, 2) == 0

    def update(t):
        here = pl.ds(pl.multiple_of(t * 256, 256), 256)
        a = dot(wturn[:, :HALF], beo[:HALF, here], 1, 0)
        b = dot(wturn[:, HALF:], beo[HALF:, here], 1, 0)
        for u in range(2):
            k = t * 2 + u
            odd = b[:, u * 128 : (u + 1) * 128]
            odd = jnp.where(low_rows, pltpu.roll(odd, 120, 1), pltpu.roll(odd, 8, 1))
            o = ((a[:, u * 128 : (u + 1) * 128] + odd) * inv[pl.ds(k, 1), :]).astype(BF16).T.astype(F32)
            inc_ref[k] = jnp.concatenate([o[m * 16 : m * 16 + 8] for m in range(8)], axis=0).astype(BF16)
            inc_ref[k + 16] = jnp.concatenate([o[m * 16 + 8 : m * 16 + 16] for m in range(8)], axis=0).astype(BF16)

    pl.loop(0, 4)(update)

    for m in range(8):
        arrived(dwrecv.at[m], ss_dw.at[m], rs_dw.at[m])
    total = dwrecv[0].astype(F32)
    for m in range(1, 8):
        total = total + dwrecv[m].astype(F32)
    e1[...] = total

    @pl.loop(1, 16)
    def _(t):
        m, dev = plane(t)
        far(e1.at[pl.ds(pl.multiple_of(m * 8, 8), 8), :], e1recv.at[t], ss_e1.at[t], rs_e1.at[t], dev).start()

    pl.loop(4, 8)(update)
    save_inc.start()

    for m in range(4):
        arrived(glown.at[m], ss_gl.at[2], rs_go.at[m])
    arrived(grown, ss_gt.at[0], rs_gt.at[0])
    gl = glown[0].astype(F32)
    for m in range(1, 4):
        gl = gl + glown[m].astype(F32)
    tmp[...] = grown[...].astype(F32)
    fsum = jnp.zeros((128, NCH), F32)
    for k in range(NQ):
        g = jnp.concatenate([gl[k * NP : (k + 1) * NP], tmp[pl.ds(k, NP, stride=NQ), :]], axis=0)
        g = g * mine[k : k + 1, :]
        high = g.astype(BF16)
        rest = (g - high.astype(F32)).astype(BF16)
        g2 = jnp.concatenate([high, rest], axis=0)
        gown[k] = g2
        fsum = fsum + dot(g2, nres[k], 1, 0)
    fsum = fsum[:64] + fsum[64:]
    for m in range(8):
        fsend[m] = fsum[m * 8 : (m + 1) * 8]
    pltpu.make_async_copy(fsend.at[c], frecv.at[c], rs_f.at[c]).start()

    @pl.loop(1, 8)
    def _(t):
        m = lax.rem(c + t, 8)
        far(fsend.at[m], frecv.at[c], ss_f.at[t], rs_f.at[c], (r, m, q)).start()

    w2x = jnp.concatenate([wt[...], wt[...]], axis=0)

    def adjoint(k):
        d = dot(gown[k], w2x, 0, 0)
        at = pl.ds(k, NS, stride=NQ)
        z = both_halves(xh, at)
        scale = rs[at, :]
        m1 = jnp.mean(d, axis=-1, keepdims=True)
        m2 = jnp.mean(d * z, axis=-1, keepdims=True)
        o = d - m1 - z * m2
        oscr[0, at, :] = scale * o[:, :128]
        oscr[1, at, :] = scale * o[:, 128:]

    for k in range(NQ):
        adjoint(k)

    @pl.loop(0, 8)
    def _(t):
        aadj_ref[pl.ds(t * 16, 16)] = both_halves(oscr, pl.ds(t * 128, 128)).reshape(16, NQ, NCH).astype(BF16)

    save_aadj.start()

    total = e1[pl.ds(pl.multiple_of(me * 8, 8), 8), :]
    for t in range(1, 16):
        arrived(e1recv.at[t], ss_e1.at[t], rs_e1.at[t])
        total = total + e1recv[t]
    e2[...] = total
    e3[pl.ds(pl.multiple_of(me * 8, 8), 8), :] = total

    @pl.loop(1, 16)
    def _(t):
        m, dev = plane(t)
        far(e2, e3.at[pl.ds(pl.multiple_of(me * 8, 8), 8), :], ss_e2.at[t], rs_e2.at[me], dev).start()

    for m in range(8):
        arrived(frecv.at[m], ss_f.at[m], rs_f.at[m])
    total = frecv[0]
    for m in range(1, 8):
        total = total + frecv[m]
    f1[...] = total
    pltpu.make_async_copy(f1, f1recv.at[me], rs_f1.at[me]).start()

    @pl.loop(1, 16)
    def _(t):
        m = lax.rem(me + t, 16)
        far(f1, f1recv.at[me], ss_f1.at[t], rs_f1.at[me], (m // 2, c, lax.rem(m, 2))).start()

    for m in range(16):

        @pl.when(me != m)
        def _(m=m):
            arrived(e3.at[m * 8 : (m + 1) * 8, :], ss_e2.at[m], rs_e2.at[m])

    chunk = dwo_ref.at[pl.ds(pl.multiple_of(c * 128, 128), 128), :]
    pltpu.make_async_copy(e3, chunk, rs_e3.at[c]).start()
    far(e3, chunk, ss_e3.at[0], rs_e3.at[c], sibling).start()

    @pl.loop(1, 4)
    def _(t):
        far(e3, chunk, ss_e3.at[t], rs_e3.at[c], (r, lax.rem(z + t, 4) * 2 + core, q)).start()

    for m in range(16):
        arrived(f1recv.at[m], ss_f1.at[m], rs_f1.at[m])
    total = f1recv[0]
    for m in range(1, 16):
        total = total + f1recv[m]
    f2[...] = total
    pltpu.make_async_copy(f2, f2recv.at[c], rs_f2.at[c]).start()

    @pl.loop(1, 8)
    def _(t):
        far(f2, f2recv.at[c], ss_f2.at[t], rs_f2.at[c], (r, lax.rem(c + t, 8), q)).start()

    for t in range(1, 4):
        m = lax.rem(z + t, 4) * 2 + core
        chunk = dwo_ref.at[pl.ds(pl.multiple_of(m * 128, 128), 128), :]
        arrived(chunk, ss_e3.at[0], rs_e3.at[m])
        far(chunk, chunk, ss_e3.at[3 + t], rs_e3.at[m], sibling).start()

    for m in range(8):
        arrived(f2recv.at[m], ss_f2.at[m], rs_f2.at[m])
    fa_ref[...] = jnp.concatenate([f2recv[m] for m in range(4)], axis=0)
    sa_ref[...] = jnp.concatenate([f2recv[m] for m in range(4, 8)], axis=0)
    for t in range(4):
        m = lax.rem(z + t, 4) * 2 + 1 - core
        arrived(dwo_ref.at[pl.ds(pl.multiple_of(m * 128, 128), 128), :], ss_e3.at[0], rs_e3.at[m])
    arrived(e3, ss_e3.at[0], rs_e3.at[c])
    save_inc.wait()
    save_aadj.wait()

    @pl.when(inner)
    def _():
        @pl.loop(1, 8)
        def _(t):
            sent(msend, ss_mr.at[t], rs_mr.at[0])

    for t in range(1, 8):
        sent(lsend, ss_l.at[t], rs_l.at[0, 0])
    for t in range(1, 7):
        sent(rsend, ss_r.at[t], rs_r.at[0, 0, 0])
    for t in range(7, 25):
        sent(rsend.at[0:128, :], ss_r.at[t], rs_r.at[0, 0, 0])
    for t in range(2):
        sent(gls.at[0], ss_gl.at[t], rs_gs.at[0])
    for pp in range(2):
        for h in range(2):

            @pl.when(jnp.logical_not(jnp.logical_and(2 * q + pp == z, q == h)))
            def _(pp=pp, h=h):
                sent(lsend, ss_gl.at[2 + pp * 2 + h], rs_go.at[0])

    @pl.when(jnp.logical_not(inner))
    def _():
        sent(lsend, ss_l.at[0], rs_l.at[0, 0])

    for t in range(7):
        sent(e3, ss_e3.at[t], rs_e3.at[0])

    @pl.loop(1, 8)
    def _(t):
        sent(msend, ss_mc.at[t], rs_mc.at[0])
        sent(dwsend.at[0], ss_dw.at[t], rs_dw.at[0])
        sent(fsend.at[0], ss_f.at[t], rs_f.at[0])
        sent(f2, ss_f2.at[t], rs_f2.at[0])

    @pl.loop(1, 16)
    def _(t):
        sent(f1, ss_f1.at[t], rs_f1.at[0])
        sent(e2, ss_e2.at[t], rs_e2.at[0])
        sent(e2, ss_e1.at[t], rs_e1.at[0])

    @pl.when(jnp.logical_not(diagonal))
    def _():
        sent(msend, ss_mc.at[0], rs_mc.at[0])

    sent(rsend, ss_r.at[0], rs_r.at[0, 0, 0])
    sent(grt, ss_gt.at[0], rs_gt.at[0])
    for t in range(1, 7):
        sent(gra.at[0, 1], ss_gr.at[t], rs_gr.at[0, 1])
    for t in range(7, 13):
        sent(grc.at[0, 1], ss_gr.at[t], rs_gr.at[0, 1])


def hand_over(*refs):
    into = [pltpu.make_async_copy(refs[i], refs[10 + i], refs[15].at[i]) for i in range(5)]
    out = [pltpu.make_async_copy(refs[10 + i], refs[5 + i], refs[16].at[i]) for i in range(5)]
    for copy in into:
        copy.start()
    for i in range(5):
        into[i].wait()
        out[i].start()
    for copy in out:
        copy.wait()


def local(x, occ, w1, w2, wo, cot):
    vmem = pl.BlockSpec(memory_space=pltpu.VMEM)
    hbm = pl.BlockSpec(memory_space=pl.ANY)
    dma = pltpu.SemaphoreType.DMA
    scratch = [
        pltpu.VMEM((NS, NQ, NCH), BF16),
        pltpu.VMEM((NQ, 2 * NS), jnp.int32),
        pltpu.VMEM((NP, NCH), BF16),
        pltpu.VMEM((NP, NCH), BF16),
        pltpu.VMEM((1024, NZ), BF16),
        pltpu.VMEM((32, 64, NZ), BF16),
        pltpu.VMEM((32, 64, NZ), BF16),
        pltpu.VMEM((NS, NQ, NCH), BF16),
        pltpu.VMEM((16, NS), BF16),
        pltpu.VMEM((4, 16, NS), BF16),
        pltpu.VMEM((8, 16, NS), BF16),
        pltpu.VMEM((2, 1024, 128), F32),
        pltpu.VMEM((1024, 128), F32),
        pltpu.VMEM((NQ, NS, NCH), BF16),
        pltpu.VMEM((256, NS), F32),
        pltpu.VMEM((256, NS), BF16),
        pltpu.VMEM((256, NS), BF16),
        pltpu.VMEM((4, 2, 256, NS), BF16),
        pltpu.VMEM((2, 8, 256, NS), BF16),
        pltpu.VMEM((64, NCH), BF16),
        pltpu.VMEM((1024, NZ), BF16),
        pltpu.VMEM((1024, NZ), F32),
        pltpu.VMEM((16, 128), F32),
        pltpu.VMEM((32, 128), F32),
        pltpu.VMEM((1024, PAIRS), F32),
        pltpu.VMEM((2, PAIRS, NZ), BF16),
        pltpu.VMEM((1024, PAIRS), BF16),
        pltpu.VMEM((1024, 256), BF16),
        pltpu.VMEM((256, 1024), BF16),
        pltpu.VMEM((NZ, 1024), BF16),
        pltpu.VMEM((2, PAIRS, 256), BF16),
        pltpu.VMEM((1024, PAIRS), BF16),
        pltpu.VMEM((4, 4, 256, NS), BF16),
        pltpu.VMEM((2, 4, 4, 128, NS), BF16),
        pltpu.VMEM((2, 4, 128, NS), BF16),
        pltpu.VMEM((2, 4, 128, NS), BF16),
        pltpu.VMEM((256, NS), BF16),
        pltpu.VMEM((256, NS), BF16),
        pltpu.VMEM((4, 2, 256, NS), BF16),
        pltpu.VMEM((2, 2, 256, NS), BF16),
        pltpu.VMEM((4, 256, NS), BF16),
        pltpu.VMEM((1024, NZ), F32),
        pltpu.VMEM((8, 128, NZ), BF16),
        pltpu.VMEM((8, 128, NZ), BF16),
        pltpu.VMEM((8, 8, NCH), F32),
        pltpu.VMEM((8, 8, NCH), F32),
        pltpu.VMEM((8, NCH), F32),
        pltpu.VMEM((16, 8, NCH), F32),
        pltpu.VMEM((8, NCH), F32),
        pltpu.VMEM((8, 8, NCH), F32),
        pltpu.VMEM((128, NZ), F32),
        pltpu.VMEM((16, 8, NZ), F32),
        pltpu.VMEM((8, NZ), F32),
        pltpu.VMEM((128, NZ), F32),
        pltpu.VMEM((NQ, 128, NS), BF16),
        pltpu.VMEM((2, 1024, 128), F32),
        dma((8,)),
        dma((8,)),
        dma((4,)),
        dma((8,)),
        dma((8,)),
        dma((8,)),
        dma((2, 2)),
        dma((2, 2)),
        dma((25,)),
        dma((2, 8, 2)),
        dma((6,)),
        dma((2,)),
        dma((4,)),
        dma((13,)),
        dma((4, 4)),
        dma((1,)),
        dma((1,)),
        dma((8,)),
        dma((8,)),
        dma((8,)),
        dma((8,)),
        dma((16,)),
        dma((16,)),
        dma((8,)),
        dma((8,)),
        dma((16,)),
        dma((16,)),
        dma((16,)),
        dma((16,)),
        dma((8,)),
        dma((8,)),
    ]
    inc, aadj, fa, sa, dwo = pl.pallas_call(
        kernel,
        out_shape=(
            jax.ShapeDtypeStruct((32, 64, NZ), BF16),
            jax.ShapeDtypeStruct((NS, NQ, NCH), BF16),
            jax.ShapeDtypeStruct((NP, NCH), F32),
            jax.ShapeDtypeStruct((NP, NCH), F32),
            jax.ShapeDtypeStruct((1024, NZ), F32),
        ),
        in_specs=[hbm] * 6,
        out_specs=(hbm, hbm, vmem, vmem, vmem),
        scratch_shapes=scratch,
        compiler_params=pltpu.CompilerParams(vmem_limit_bytes=60 * 1024 * 1024, has_side_effects=True, collective_id=0),
    )(x, occ.T, w1.T, w2.T, wo, cot)
    outs = (inc, aadj, fa, sa, dwo)
    inc, aadj, fa, sa, dwo = pl.pallas_call(
        hand_over,
        out_shape=tuple(jax.ShapeDtypeStruct(o.shape, o.dtype) for o in outs),
        in_specs=[hbm] * 5,
        out_specs=(hbm,) * 5,
        scratch_shapes=[pltpu.VMEM(o.shape, o.dtype) for o in outs] + [dma((5,)), dma((5,))],
        compiler_params=pltpu.CompilerParams(vmem_limit_bytes=60 * 1024 * 1024),
    )(*outs)
    return inc, aadj, fa.T, sa.T, dwo


def solution(mesh):
    placed = (
        P("seq", ("row", "col"), None),
        P(None, ("row", "col")),
        P(),
        P(),
        P(),
        P(("row", "seq"), "col", None),
    )
    return jax.shard_map(
        local,
        mesh=mesh,
        in_specs=placed,
        out_specs=(P(("row", "seq"), "col", None), P("seq", ("row", "col"), None), P(), P(), P()),
        check_vma=False,
    )
```

```python
import jax
import jax.numpy as jnp
from jax import lax
from jax.experimental import pallas as pl
from jax.experimental.pallas import tpu as pltpu
from jax.sharding import PartitionSpec as P

F32 = jnp.float32
BF16 = jnp.bfloat16
MESH = pl.DeviceIdType.MESH

NS = 128
NQ = 8
NCH = 256
NP = 32
NZ = 128
HALF = 512
PAIRS = 2048


def dot(a, b, ca, cb):
    return lax.dot_general(a, b, (((ca,), (cb,)), ((), ())), preferred_element_type=F32)


def both_halves(ref, rows):
    return jnp.concatenate([ref[0, rows, :], ref[1, rows, :]], axis=1)


def kernel(
    x_hbm,
    occ_hbm,
    w1_hbm,
    w2_hbm,
    wo_hbm,
    cot_hbm,
    inc_hbm,
    aadj_hbm,
    fa_hbm,
    sa_hbm,
    dwo_hbm,
    x_ref,
    occ_ref,
    w1_ref,
    w2_ref,
    wo_ref,
    cot_ref,
    inc_ref,
    aadj_ref,
    fa_ref,
    sa_ref,
    dwo_ref,
    msend,
    mrow,
    mcol,
    xh,
    rs,
    nres,
    tmp,
    lsend,
    rsend,
    lrecv,
    rrecv,
    wt,
    wsplit,
    wide,
    inv,
    over_lanes,
    dpre,
    s12,
    d2,
    lscr,
    lturn,
    wturn,
    rscr,
    beo,
    grsend,
    gra,
    grb,
    grc,
    grt,
    grown,
    glp,
    gls,
    glown,
    dwf,
    dwsend,
    dwrecv,
    fsend,
    frecv,
    f1,
    f1recv,
    f2,
    f2recv,
    e1,
    e1recv,
    e2,
    e3,
    gown,
    oscr,
    io_sem,
    ss,
    rs_mr,
    rs_mc,
    rs_l,
    rs_ls,
    rs_r,
    rs_gs,
    rs_go,
    rs_gr,
    rs_gt,
    rs_dw,
    rs_f,
    rs_f1,
    rs_f2,
    rs_e1,
    rs_e2,
    rs_e3,
):
    r, c, q = lax.axis_index("row"), lax.axis_index("col"), lax.axis_index("seq")
    inner = q == c // 4
    diagonal = r == c
    me = r * 2 + q
    core, z = lax.rem(c, 2), c // 2
    sibling = (r, c + 1 - 2 * core, q)
    holder = (
        lax.rem(r // 4 + core, 2) * 4 + lax.rem(lax.rem(r, 4) + 2 - z + r // 2 + 4, 4),
        r,
        q,
    )

    def held(m):
        dz = lax.rem(2 - lax.rem(m, 4) + lax.rem(c, 4) + 4, 4)
        return lax.rem(c // 2 + dz, 4) * 2 + lax.rem(m // 4 + c // 4, 2)

    def holder_row(m):
        dz = lax.rem(m // 2 - c // 2 + 4, 4)
        return lax.rem(c // 4 + lax.rem(m, 2), 2) * 4 + lax.rem(lax.rem(c, 4) + 2 - dz + 4, 4)

    owner = (c, held(r), q)
    other = (r, lax.rem(c + 1, 8), q)

    def plane(t):
        m = lax.rem(me + t, 16)
        return m, (m // 2, c, lax.rem(m, 2))

    def line(t):
        m = lax.rem(c + t, 8)
        return m, (r, m, q)

    def far(src, dst, ssem, rsem, dev):
        return pltpu.make_async_remote_copy(
            src_ref=src, dst_ref=dst, send_sem=ssem, recv_sem=rsem, device_id=dev, device_id_type=MESH
        )

    def put(own, src, dst, ssem, rsem, dev):
        @pl.when(own)
        def _():
            pltpu.make_async_copy(src, dst, rsem).start()

        @pl.when(jnp.logical_not(own))
        def _():
            far(src, dst, ssem, rsem, dev).start()

    def arrived(size, mark):
        far(size, size, ss.at[0], mark, other).wait_recv()

    def sent(size, step):
        far(size, size, ss.at[step], rs_r.at[0], other).wait_send()

    load_wo = pltpu.make_async_copy(wo_hbm, wo_ref, io_sem.at[0])
    load_cot = pltpu.make_async_copy(cot_hbm, cot_ref, io_sem.at[1])
    save_fa = pltpu.make_async_copy(fa_ref, fa_hbm, io_sem.at[16])
    save_sa = pltpu.make_async_copy(sa_ref, sa_hbm, io_sem.at[17])
    save_inc = pltpu.make_async_copy(inc_ref, inc_hbm, io_sem.at[2])
    save_aadj = pltpu.make_async_copy(aadj_ref, aadj_hbm, io_sem.at[7])

    def save_chunk(m):
        rows = pl.ds(pl.multiple_of(m * 128, 128), 128)
        return pltpu.make_async_copy(dwo_ref.at[rows, :], dwo_hbm.at[rows, :], io_sem.at[8 + m])

    load_x = pltpu.make_async_copy(x_hbm, x_ref, io_sem.at[3])
    load_occ = pltpu.make_async_copy(occ_hbm, occ_ref, io_sem.at[4])
    load_w1 = pltpu.make_async_copy(w1_hbm, w1_ref, io_sem.at[5])
    load_w2 = pltpu.make_async_copy(w2_hbm, w2_ref, io_sem.at[6])
    for load in (load_x, load_occ, load_w1, load_w2, load_wo, load_cot):
        load.start()

    barrier = pltpu.get_barrier_semaphore()

    def mask_to(t):
        return (lax.rem(r + t, 8), r, q)

    def mask_from(t):
        return (c, lax.rem(c + t, 8), q)

    @pl.loop(1, 8)
    def _(t):
        pl.semaphore_signal(barrier, inc=1, device_id=mask_to(t), device_id_type=MESH)
        pl.semaphore_signal(barrier, inc=1, device_id=mask_from(t), device_id_type=MESH)

    @pl.loop(1, 16)
    def _(t):
        pl.semaphore_signal(barrier, inc=1, device_id=plane(t)[1], device_id_type=MESH)

    @pl.loop(1, 8)
    def _(t):
        pl.semaphore_signal(barrier, inc=1, device_id=line(t)[1], device_id_type=MESH)

    y0, x0 = q * 2 + r // 4, lax.rem(r, 4)
    across = (r, lax.rem(z + 3 - 2 * lax.rem(z, 2), 4) * 2 + core, 1 - q)

    def at(y, x):
        return (lax.rem(y, 2) * 4 + x, c, y // 2)

    def along_x(t):
        return at(y0, lax.rem(x0 + t, 4))

    def along_y(t):
        return at(lax.rem(y0 + t, 4), x0)

    def along_z(t):
        return (r, lax.rem(z + t, 4) * 2 + core, q)

    def block(dy, dx, first, last):
        y, x = lax.rem(y0 + dy, 4), lax.rem(x0 + dx, 4)
        h, m = y // 2, lax.rem(y, 2) * 4 + x
        return rrecv.at[h, m, first:last, :]

    @pl.loop(1, 4)
    def _(t):
        dev = (r, lax.rem(z + t, 4) * 2 + core, 1 - q)
        pl.semaphore_signal(barrier, inc=1, device_id=dev, device_id_type=MESH)

    for dev in (holder, owner):
        pl.semaphore_signal(barrier, inc=1, device_id=dev, device_id_type=MESH)

    @pl.when(jnp.logical_not(diagonal))
    def _():
        for dev in (mask_to(0), mask_from(0)):
            pl.semaphore_signal(barrier, inc=1, device_id=dev, device_id_type=MESH)

    load_occ.wait()
    occ = occ_ref[...].astype(F32)
    msend[...] = jnp.concatenate([occ[:, :NS], occ[:, NS:]], axis=0).astype(BF16)

    load_x.wait()
    @pl.loop(0, 8)
    def _(t):
        xb = x_ref[pl.ds(t * 16, 16)].astype(F32).reshape(128, NCH)
        xc = xb - jnp.mean(xb, axis=-1, keepdims=True)
        rstd = lax.rsqrt(jnp.mean(xc * xc, axis=-1, keepdims=True) + 1e-05)
        z = xc * rstd
        xh[0, pl.ds(t * 128, 128), :] = z[:, :128]
        xh[1, pl.ds(t * 128, 128), :] = z[:, 128:]
        rs[pl.ds(t * 128, 128), :] = jnp.broadcast_to(rstd, (128, 128))

    load_w1.wait()
    load_w2.wait()
    wt[0:NP, :] = w1_ref[...]
    wt[NP:, :] = w2_ref[...]
    mine = msend[...].astype(F32)
    mine = jnp.where(q == 0, mine[:NQ], mine[NQ:])
    for k in range(NQ):
        n = both_halves(xh, pl.ds(k, NS, stride=NQ)).astype(BF16)
        nres[k] = n
        p = dot(wt[...], n, 1, 1) * mine[k : k + 1, :]
        lsend[k * NP : (k + 1) * NP, :] = p[:NP].astype(BF16)
        tmp[pl.ds(k, NP, stride=NQ), :] = p[NP:]
    rsend[...] = tmp[...].astype(BF16)

    pl.semaphore_wait(barrier, jnp.where(diagonal, 41, 43))

    mine_of_line = lax.rem(jnp.where(inner, z, z + 3 - 2 * lax.rem(z, 2)), 2)
    seq_of_line = jnp.where(inner, q, 1 - q)
    given = lrecv.at[mine_of_line * 2 + core, seq_of_line]
    given_mark = rs_l.at[mine_of_line, seq_of_line]

    def left_along():
        for t in range(1, 4):
            far(given, given, ss.at[2], given_mark, along_z(t)).start()
        far(given, given, ss.at[2], rs_ls.at[0], sibling).start()

    @pl.when(inner)
    def _():
        lrecv[lax.rem(c, 4), q] = lsend[...]
        left_along()

    @pl.when(jnp.logical_not(inner))
    def _():
        far(lsend, lrecv.at[lax.rem(c, 4), q], ss.at[2], rs_l.at[lax.rem(c, 4) // 2, q], across).start()

    far(rsend, rrecv.at[q, holder[0]], ss.at[3], rs_r.at[0], holder).start()

    put(diagonal, msend, mcol.at[c], ss.at[1], rs_mc.at[0], mask_to(0))

    @pl.loop(1, 8)
    def _(t):
        far(msend, mcol.at[c], ss.at[1], rs_mc.at[0], mask_to(t)).start()

    @pl.when(inner)
    def _():
        m = lax.rem(c, 4)
        pltpu.make_async_copy(msend, mrow.at[m], rs_mr.at[0]).start()

        @pl.loop(1, 8)
        def _(t):
            far(msend, mrow.at[m], ss.at[0], rs_mr.at[0], line(t)[1]).start()

    load_wo.wait()
    wide[...] = wo_ref[...].astype(F32)
    for e in range(NP):
        wsplit[(e % 2) * HALF + (e // 2) * NP : (e % 2) * HALF + (e // 2 + 1) * NP, :] = wide[pl.ds(e, NP, stride=NP), :].astype(BF16)

    wturn[...] = wsplit[...].T

    lane = lax.broadcasted_iota(jnp.int32, (NP, 128), 1)
    low = lax.rem(lane // 8, 2) == 0

    def in_turn(lo, hi):
        return jnp.concatenate([v[m * 8 : m * 8 + 8] for m in range(8) for v in (lo, hi)], axis=0).astype(BF16)

    load_cot.wait()
    for k in range(16):
        lo, hi = cot_ref[k].astype(F32), cot_ref[k + 16].astype(F32)
        s12[0, k * 128 : (k + 1) * 128, :] = in_turn(lo, hi)
        s12[1, k * 128 : (k + 1) * 128, :] = in_turn(hi, lo)

    def outer_adjoint(t):
        here = pl.ds(pl.multiple_of(t * 256, 256), 256)
        even, odd = wsplit[:HALF], wsplit[HALF:]
        plain, turned_s = s12[0, here, :], s12[1, here, :]
        halves = (
            (dot(even, plain, 1, 1), dot(odd, turned_s, 1, 1)),
            (dot(even, turned_s, 1, 1), dot(odd, plain, 1, 1)),
        )
        for u in range(2):
            for half, (a, b) in enumerate(halves):
                at = pl.ds(pl.multiple_of(half * HALF + (t * 2 + u) * NP, NP), NP)
                for p in range(16):
                    va = a[p * NP : (p + 1) * NP, u * 128 : (u + 1) * 128]
                    vb = b[p * NP : (p + 1) * NP, u * 128 : (u + 1) * 128]
                    dpre[at, p * 128 : (p + 1) * 128] = jnp.where(low, va, vb)

    pl.loop(0, 4)(outer_adjoint)

    @pl.when(jnp.logical_not(inner))
    def _():
        arrived(given, given_mark)
        left_along()

    came = block(0, 0, 0, 256)
    arrived(came, rs_r.at[0])
    for t in range(1, 4):
        far(came, came, ss.at[3], rs_r.at[4 - t], along_x(t)).start()
        far(came, came, ss.at[3], rs_r.at[7 - t], along_y(t)).start()

    pl.loop(4, 8)(outer_adjoint)

    arrived(mrow, rs_mr.at[0])
    arrived(mcol, rs_mc.at[0])

    count = jnp.zeros((64, 32), F32)
    count_lanes = jnp.zeros((32, 128), F32)
    for h in range(2):
        rows = jnp.concatenate([mrow[m].astype(F32)[h * NQ : (h + 1) * NQ] for m in range(4)], axis=0).astype(BF16)
        groups = [mcol[m].astype(F32)[h * NQ : (h + 1) * NQ] for m in range(8)]
        cols = jnp.concatenate(groups, axis=0).astype(BF16)
        twice = jnp.concatenate([g for g in groups for _ in range(2)], axis=0).astype(BF16)
        count = count + dot(cols, rows, 1, 1)
        count_lanes = count_lanes + dot(rows, twice, 1, 1)
    over_lanes[...] = 1.0 / (count_lanes + 0.001)
    inv[...] = jnp.where(low[:16], over_lanes[:16], over_lanes[16:])

    @pl.loop(0, 32)
    def _(i):
        rows = pl.ds(pl.multiple_of(i * NP, NP), NP)
        d2[rows, :] = (dpre[rows, :] * jnp.concatenate([over_lanes[pl.ds(i, 1), :]] * 16, axis=1)).astype(BF16)

    for t in range(1, 4):
        zt = lax.rem(z + t, 4)
        in_half = zt // 2 == q
        pp = lax.rem(jnp.where(in_half, zt, zt + 3 - 2 * lax.rem(zt, 2)), 2)
        h = jnp.where(in_half, q, 1 - q)
        slot = lrecv.at[pp * 2 + core, h]
        arrived(slot, rs_l.at[pp, h])
        far(slot, slot, ss.at[2], rs_ls.at[0], sibling).start()

    for t in range(1, 4):
        arrived(block(0, t, 0, 256), rs_r.at[t])
        half = block(0, t, 0, 128)
        for u in range(1, 4):
            far(half, half, ss.at[3], rs_r.at[7], along_y(u)).start()
        arrived(block(t, 0, 0, 256), rs_r.at[3 + t])
        half = block(t, 0, 128, 256)
        for u in range(1, 4):
            far(half, half, ss.at[3], rs_r.at[7], along_x(u)).start()

    def put_right(dy, dx):
        y, x = lax.rem(y0 + dy, 4), lax.rem(x0 + dx, 4)
        h, m = y // 2, lax.rem(y, 2) * 4 + x
        lanes = pl.ds(pl.multiple_of(h * NS, NS), NS)
        first = held(m) * 16
        for p in range(16):
            at = pl.ds(pl.multiple_of(p * 128 + first, 16), 16)
            v = rrecv[h, m, p * 16 : (p + 1) * 16, :]
            w = v.astype(F32)
            rscr[0, at, lanes] = v
            rscr[1, at, lanes] = jnp.concatenate([w[8:], w[:8]], axis=0).astype(BF16)

    put_right(0, 0)
    for t in range(1, 4):
        put_right(0, t)
        put_right(t, 0)

    arrived(lrecv.at[0:2], rs_ls.at[0])
    for h in range(2):
        for m in range(4):
            lscr[m * 256 : (m + 1) * 256, h * NS : (h + 1) * NS] = lrecv[m, h]
            lturn[h * NS : (h + 1) * NS, m * 256 : (m + 1) * 256] = lrecv[m, h].T

    def right_part(t):
        here = pl.ds(pl.multiple_of(t * 256, 256), 256)
        a = dot(lturn[...], d2[:, here], 1, 0).astype(BF16)
        for u in range(2):
            at = pl.ds(pl.multiple_of((t * 2 + u) * 16, 16), 16)
            for h in range(2):
                gt = a[h * NS : (h + 1) * NS, u * 128 : (u + 1) * 128].T
                for m in range(8):
                    row = holder_row(m)
                    grsend[h * 2 + row // 4, lax.rem(row, 4), at, :] = gt[m * 16 : (m + 1) * 16]

    for n in range(4):
        pl.loop(2 * n, 2 * n + 2)(right_part)
        rows = slice(n * 64, (n + 1) * 64)
        for t in range(1, 4):
            y, x = lax.rem(y0 + t, 4), lax.rem(x0 + t, 4)
            part = grsend.at[:, x, rows, :] if n % 2 else grsend.at[y, :, rows, :]
            to = along_x(t) if n % 2 else along_y(t)
            far(part, gra.at[n, t], ss.at[5], rs_gr.at[n], to).start()

    over = 1.0 / (count + 0.001)
    for k in range(16):
        lo, hi = [
            cot_ref[i].astype(F32) * jnp.broadcast_to(over[:, i : i + 1], (64, NZ)) for i in (k, k + 16)
        ]
        s12[0, k * 128 : (k + 1) * 128, :] = in_turn(lo, hi)
        s12[1, k * 128 : (k + 1) * 128, :] = in_turn(hi, lo)

    arrived(grsend.at[0:3, 0:3], rs_r.at[7])
    for t in range(1, 4):
        for u in range(1, 4):
            put_right(t, u)

    def outer_product(t):
        here = pl.ds(pl.multiple_of(t * 256, 256), 256)
        a = dot(lscr[:HALF], rscr[0, here, :], 1, 1)
        b = dot(lscr[HALF:], rscr[1, here, :], 1, 1)
        for u in range(2):
            lanes = slice(u * 128, (u + 1) * 128)
            even = pl.ds(pl.multiple_of((t * 2 + u) * NP, NP), NP)
            odd = pl.ds(pl.multiple_of(HALF + (t * 2 + u) * NP, NP), NP)
            for k in range(16):
                lo = a[k * NP : (k + 1) * NP, lanes]
                hi = b[k * NP : (k + 1) * NP, lanes]
                beo[even, k * 128 : (k + 1) * 128] = jnp.where(low, lo, hi).astype(BF16)
                beo[odd, k * 128 : (k + 1) * 128] = jnp.where(low, hi, lo).astype(BF16)

    pl.loop(0, 4)(outer_product)

    pl.loop(4, 8)(outer_product)

    for h in range(2):
        part = dot(beo[h * HALF : (h + 1) * HALF], s12[h], 1, 0)
        for p in range(16):
            dwf[pl.ds(2 * p + h, NP, stride=NP), :] = part[p * NP : (p + 1) * NP]
    for m in range(8):
        dwsend[m] = dwf[m * 128 : (m + 1) * 128, :].astype(BF16)
    pltpu.make_async_copy(dwsend.at[c], dwrecv.at[c], rs_dw.at[0]).start()

    @pl.loop(1, 8)
    def _(t):
        m = lax.rem(c + t, 8)
        far(dwsend.at[m], dwrecv.at[c], ss.at[8], rs_dw.at[0], (r, m, q)).start()

    for i in range(2):
        for half in range(2):
            part = 2 * half + i
            rows = slice(part * 64, (part + 1) * 64)
            arrived(gra.at[part, 1:4], rs_gr.at[part])
            for n in range(4):
                own = grsend[n, x0, rows, :] if i else grsend[y0, n, rows, :]
                total = own.astype(F32)
                for t in range(1, 4):
                    total = total + gra[part, t, n].astype(F32)
                grb[i, n, half] = total.astype(BF16)
        for t in range(1, 4):
            if i:
                far(grb.at[i, lax.rem(y0 + t, 4)], grc.at[i, t], ss.at[6], rs_gr.at[4 + i], along_y(t)).start()
            else:
                far(grb.at[i, lax.rem(x0 + t, 4)], grc.at[i, t], ss.at[6], rs_gr.at[4 + i], along_x(t)).start()

    def left_piece(pp, k):
        rows = pl.ds(pl.multiple_of((pp * 2 + k) * 256, 256), 256)
        g = dot(d2[rows, :], rscr[0], 1, 0)
        for h in range(2):
            glp[pp * 2 + k, h] = g[:, h * NS : (h + 1) * NS].astype(BF16)

    for pp in range(2):
        left_piece(pp, 1 - core)
        far(glp.at[pp * 2 + 1 - core], gls.at[pp], ss.at[4], rs_gs.at[pp], sibling).start()
    for pp in range(2):
        left_piece(pp, core)

    for pp in range(2):
        arrived(gls.at[pp], rs_gs.at[pp])
        m = pp * 2 + core
        for h in range(2):
            glp[m, h] = (glp[m, h].astype(F32) + gls[pp, h].astype(F32)).astype(BF16)
            put(
                jnp.logical_and(2 * q + pp == z, q == h),
                glp.at[m, h],
                glown.at[z],
                ss.at[4],
                rs_go.at[0],
                (r, 4 * q + m, h),
            )

    low_rows = lax.rem(lax.broadcasted_iota(jnp.int32, (NZ, 128), 1) // 8, 2) == 0

    def update(t):
        here = pl.ds(pl.multiple_of(t * 256, 256), 256)
        a = dot(wturn[:, :HALF], beo[:HALF, here], 1, 0)
        b = dot(wturn[:, HALF:], beo[HALF:, here], 1, 0)
        for u in range(2):
            k = t * 2 + u
            odd = b[:, u * 128 : (u + 1) * 128]
            odd = jnp.where(low_rows, pltpu.roll(odd, 120, 1), pltpu.roll(odd, 8, 1))
            o = ((a[:, u * 128 : (u + 1) * 128] + odd) * inv[pl.ds(k, 1), :]).astype(BF16).T.astype(F32)
            inc_ref[k] = jnp.concatenate([o[m * 16 : m * 16 + 8] for m in range(8)], axis=0).astype(BF16)
            inc_ref[k + 16] = jnp.concatenate([o[m * 16 + 8 : m * 16 + 16] for m in range(8)], axis=0).astype(BF16)

    pl.loop(0, 4)(update)

    for i in range(2):
        own = grb[i, y0] if i else grb[i, x0]
        total = own.astype(F32)
        arrived(grc.at[i, 1:4], rs_gr.at[4 + i])
        for t in range(1, 4):
            total = total + grc[i, t].astype(F32)
        for half in range(2):
            part = 2 * half + i
            grt[part * 64 : (part + 1) * 64, :] = total[half].astype(BF16)
    far(grt, grown, ss.at[7], rs_gt.at[0], owner).start()

    arrived(dwrecv, rs_dw.at[0])
    total = dwrecv[0].astype(F32)
    for m in range(1, 8):
        total = total + dwrecv[m].astype(F32)
    e1[...] = total

    @pl.loop(1, 16)
    def _(t):
        m, dev = plane(t)
        far(e1.at[pl.ds(pl.multiple_of(m * 8, 8), 8), :], e1recv.at[t], ss.at[12], rs_e1.at[0], dev).start()

    pl.loop(4, 8)(update)
    save_inc.start()

    arrived(glown, rs_go.at[0])
    arrived(grown, rs_gt.at[0])
    gl = glown[0].astype(F32)
    for m in range(1, 4):
        gl = gl + glown[m].astype(F32)
    tmp[...] = grown[...].astype(F32)
    fsum = jnp.zeros((128, NCH), F32)
    for k in range(NQ):
        g = jnp.concatenate([gl[k * NP : (k + 1) * NP], tmp[pl.ds(k, NP, stride=NQ), :]], axis=0)
        g = g * mine[k : k + 1, :]
        high = g.astype(BF16)
        rest = (g - high.astype(F32)).astype(BF16)
        g2 = jnp.concatenate([high, rest], axis=0)
        gown[k] = g2
        fsum = fsum + dot(g2, nres[k], 1, 0)
    fsum = fsum[:64] + fsum[64:]
    for m in range(8):
        fsend[m] = fsum[m * 8 : (m + 1) * 8]
    pltpu.make_async_copy(fsend.at[c], frecv.at[c], rs_f.at[0]).start()

    @pl.loop(1, 8)
    def _(t):
        m = lax.rem(c + t, 8)
        far(fsend.at[m], frecv.at[c], ss.at[9], rs_f.at[0], (r, m, q)).start()

    arrived(e1recv.at[1:16], rs_e1.at[0])
    total = e1[pl.ds(pl.multiple_of(me * 8, 8), 8), :]
    for t in range(1, 16):
        total = total + e1recv[t]
    e2[...] = total
    pltpu.make_async_copy(e2, e3.at[pl.ds(pl.multiple_of(me * 8, 8), 8), :], rs_e2.at[0]).start()

    @pl.loop(1, 16)
    def _(t):
        m, dev = plane(t)
        far(e2, e3.at[pl.ds(pl.multiple_of(me * 8, 8), 8), :], ss.at[13], rs_e2.at[0], dev).start()

    w2x = jnp.concatenate([wt[...], wt[...]], axis=0)

    def adjoint(k):
        d = dot(gown[k], w2x, 0, 0)
        at = pl.ds(k, NS, stride=NQ)
        z = both_halves(xh, at)
        scale = rs[at, :]
        m1 = jnp.mean(d, axis=-1, keepdims=True)
        m2 = jnp.mean(d * z, axis=-1, keepdims=True)
        o = d - m1 - z * m2
        oscr[0, at, :] = scale * o[:, :128]
        oscr[1, at, :] = scale * o[:, 128:]

    for k in range(NQ):
        adjoint(k)

    @pl.loop(0, 8)
    def _(t):
        aadj_ref[pl.ds(t * 16, 16)] = both_halves(oscr, pl.ds(t * 128, 128)).reshape(16, NQ, NCH).astype(BF16)

    save_aadj.start()

    arrived(frecv, rs_f.at[0])
    total = frecv[0]
    for m in range(1, 8):
        total = total + frecv[m]
    f1[...] = total
    pltpu.make_async_copy(f1, f1recv.at[me], rs_f1.at[0]).start()

    @pl.loop(1, 16)
    def _(t):
        m = lax.rem(me + t, 16)
        far(f1, f1recv.at[me], ss.at[10], rs_f1.at[0], (m // 2, c, lax.rem(m, 2))).start()

    arrived(e3, rs_e2.at[0])
    chunk = dwo_ref.at[pl.ds(pl.multiple_of(c * 128, 128), 128), :]
    dwo_ref[pl.ds(pl.multiple_of(c * 128, 128), 128), :] = e3[...]
    save_chunk(c).start()
    far(e3, chunk, ss.at[14], rs_e3.at[0], sibling).start()

    for t in range(1, 4):
        far(e3, chunk, ss.at[14], rs_e3.at[4 - t], (r, lax.rem(z + t, 4) * 2 + core, q)).start()

    arrived(f1recv, rs_f1.at[0])
    total = f1recv[0]
    for m in range(1, 16):
        total = total + f1recv[m]
    f2[...] = total
    pltpu.make_async_copy(f2, f2recv.at[c], rs_f2.at[0]).start()

    @pl.loop(1, 8)
    def _(t):
        far(f2, f2recv.at[c], ss.at[11], rs_f2.at[0], (r, lax.rem(c + t, 8), q)).start()

    for t in range(1, 4):
        m = lax.rem(z + t, 4) * 2 + core
        chunk = dwo_ref.at[pl.ds(pl.multiple_of(m * 128, 128), 128), :]
        arrived(chunk, rs_e3.at[t])
        save_chunk(m).start()
        far(chunk, chunk, ss.at[14], rs_e3.at[0], sibling).start()

    arrived(dwo_ref.at[0:512, :], rs_e3.at[0])
    for t in range(4):
        save_chunk(2 * t + 1 - core).start()

    arrived(f2recv, rs_f2.at[0])
    fa_ref[...] = jnp.concatenate([f2recv[m] for m in range(4)], axis=0)
    sa_ref[...] = jnp.concatenate([f2recv[m] for m in range(4, 8)], axis=0)
    save_fa.start()
    save_sa.start()
    for m in range(8):
        save_chunk(m).wait()
    save_inc.wait()
    save_aadj.wait()

    @pl.when(inner)
    def _():
        sent(mcol.at[0:7], 0)
        sent(rrecv.at[0, 0:7], 2)
        sent(rrecv.at[0, 0:7], 4)

    @pl.when(jnp.logical_not(inner))
    def _():
        sent(rrecv.at[0], 2)
        sent(rrecv.at[0], 4)

    @pl.when(diagonal)
    def _():
        sent(mcol.at[0:7], 1)

    @pl.when(jnp.logical_not(diagonal))
    def _():
        sent(mcol, 1)

    sent(rrecv, 3)
    sent(gra.at[0:3], 5)
    sent(gra.at[0, 0:3], 6)
    sent(grt, 7)
    sent(dwrecv.at[0:7], 8)
    sent(frecv.at[0:7], 9)
    sent(f1recv.at[0:15], 10)
    sent(f2recv.at[0:7], 11)
    sent(e1recv.at[0:15], 12)
    sent(e1recv.at[0:15], 13)
    sent(dwo_ref.at[0:896, :], 14)

    save_fa.wait()
    save_sa.wait()


def hand_over(*refs):
    into = [pltpu.make_async_copy(refs[i], refs[10 + i], refs[15].at[i]) for i in range(5)]
    out = [pltpu.make_async_copy(refs[10 + i], refs[5 + i], refs[16].at[i]) for i in range(5)]
    for copy in into:
        copy.start()
    for i in range(5):
        into[i].wait()
        out[i].start()
    for copy in out:
        copy.wait()


def local(x, occ, w1, w2, wo, cot):
    hbm = pl.BlockSpec(memory_space=pl.ANY)
    dma = pltpu.SemaphoreType.DMA
    scratch = [
        pltpu.VMEM((NS, NQ, NCH), BF16),
        pltpu.VMEM((NQ, 2 * NS), jnp.int32),
        pltpu.VMEM((NP, NCH), BF16),
        pltpu.VMEM((NP, NCH), BF16),
        pltpu.VMEM((1024, NZ), BF16),
        pltpu.VMEM((32, 64, NZ), BF16),
        pltpu.VMEM((32, 64, NZ), BF16),
        pltpu.VMEM((NS, NQ, NCH), BF16),
        pltpu.VMEM((NP, NCH), F32),
        pltpu.VMEM((NP, NCH), F32),
        pltpu.VMEM((1024, NZ), F32),
        pltpu.VMEM((16, NS), BF16),
        pltpu.VMEM((4, 16, NS), BF16),
        pltpu.VMEM((8, 16, NS), BF16),
        pltpu.VMEM((2, 1024, 128), F32),
        pltpu.VMEM((1024, 128), F32),
        pltpu.VMEM((NQ, NS, NCH), BF16),
        pltpu.VMEM((256, NS), F32),
        pltpu.VMEM((256, NS), BF16),
        pltpu.VMEM((256, NS), BF16),
        pltpu.VMEM((4, 2, 256, NS), BF16),
        pltpu.VMEM((2, 8, 256, NS), BF16),
        pltpu.VMEM((64, NCH), BF16),
        pltpu.VMEM((1024, NZ), BF16),
        pltpu.VMEM((1024, NZ), F32),
        pltpu.VMEM((16, 128), F32),
        pltpu.VMEM((32, 128), F32),
        pltpu.VMEM((1024, PAIRS), F32),
        pltpu.VMEM((2, PAIRS, NZ), BF16),
        pltpu.VMEM((1024, PAIRS), BF16),
        pltpu.VMEM((1024, 256), BF16),
        pltpu.VMEM((256, 1024), BF16),
        pltpu.VMEM((NZ, 1024), BF16),
        pltpu.VMEM((2, PAIRS, 256), BF16),
        pltpu.VMEM((1024, PAIRS), BF16),
        pltpu.VMEM((4, 4, 256, NS), BF16),
        pltpu.VMEM((4, 4, 4, 64, NS), BF16),
        pltpu.VMEM((2, 4, 2, 64, NS), BF16),
        pltpu.VMEM((2, 4, 2, 64, NS), BF16),
        pltpu.VMEM((256, NS), BF16),
        pltpu.VMEM((256, NS), BF16),
        pltpu.VMEM((4, 2, 256, NS), BF16),
        pltpu.VMEM((2, 2, 256, NS), BF16),
        pltpu.VMEM((4, 256, NS), BF16),
        pltpu.VMEM((1024, NZ), F32),
        pltpu.VMEM((8, 128, NZ), BF16),
        pltpu.VMEM((8, 128, NZ), BF16),
        pltpu.VMEM((8, 8, NCH), F32),
        pltpu.VMEM((8, 8, NCH), F32),
        pltpu.VMEM((8, NCH), F32),
        pltpu.VMEM((16, 8, NCH), F32),
        pltpu.VMEM((8, NCH), F32),
        pltpu.VMEM((8, 8, NCH), F32),
        pltpu.VMEM((128, NZ), F32),
        pltpu.VMEM((16, 8, NZ), F32),
        pltpu.VMEM((8, NZ), F32),
        pltpu.VMEM((128, NZ), F32),
        pltpu.VMEM((NQ, 128, NS), BF16),
        pltpu.VMEM((2, 1024, 128), F32),
        dma((18,)),
        dma((15,)),
        dma((1,)),
        dma((1,)),
        dma((2, 2)),
        dma((1,)),
        dma((8,)),
        dma((2,)),
        dma((1,)),
        dma((6,)),
        dma((1,)),
        dma((1,)),
        dma((1,)),
        dma((1,)),
        dma((1,)),
        dma((1,)),
        dma((1,)),
        dma((4,)),
    ]
    inc, aadj, fa, sa, dwo = pl.pallas_call(
        kernel,
        out_shape=(
            jax.ShapeDtypeStruct((32, 64, NZ), BF16),
            jax.ShapeDtypeStruct((NS, NQ, NCH), BF16),
            jax.ShapeDtypeStruct((NP, NCH), F32),
            jax.ShapeDtypeStruct((NP, NCH), F32),
            jax.ShapeDtypeStruct((1024, NZ), F32),
        ),
        in_specs=[hbm] * 6,
        out_specs=(hbm,) * 5,
        scratch_shapes=scratch,
        compiler_params=pltpu.CompilerParams(vmem_limit_bytes=60 * 1024 * 1024, has_side_effects=True, collective_id=0),
    )(x, occ.T, w1.T, w2.T, wo, cot)
    outs = (inc, aadj, fa, sa, dwo)
    inc, aadj, fa, sa, dwo = pl.pallas_call(
        hand_over,
        out_shape=tuple(jax.ShapeDtypeStruct(o.shape, o.dtype) for o in outs),
        in_specs=[hbm] * 5,
        out_specs=(hbm,) * 5,
        scratch_shapes=[pltpu.VMEM(o.shape, o.dtype) for o in outs] + [dma((5,)), dma((5,))],
        compiler_params=pltpu.CompilerParams(vmem_limit_bytes=60 * 1024 * 1024),
    )(*outs)
    return inc, aadj, fa.T, sa.T, dwo


def solution(mesh):
    placed = (
        P("seq", ("row", "col"), None),
        P(None, ("row", "col")),
        P(),
        P(),
        P(),
        P(("row", "seq"), "col", None),
    )
    return jax.shard_map(
        local,
        mesh=mesh,
        in_specs=placed,
        out_specs=(P(("row", "seq"), "col", None), P("seq", ("row", "col"), None), P(), P(), P()),
        check_vma=False,
    )
```

```python
import jax
import jax.numpy as jnp
from jax import lax
from jax.experimental import pallas as pl
from jax.experimental.pallas import tpu as pltpu
from jax.sharding import PartitionSpec as P

F32 = jnp.float32
BF16 = jnp.bfloat16
MESH = pl.DeviceIdType.MESH

NS = 128
NQ = 8
NCH = 256
NP = 32
NZ = 128
HALF = 512
PAIRS = 2048


def dot(a, b, ca, cb):
    return lax.dot_general(a, b, (((ca,), (cb,)), ((), ())), preferred_element_type=F32)


def both_halves(ref, rows):
    return jnp.concatenate([ref[0, rows, :], ref[1, rows, :]], axis=1)


def kernel(
    x_hbm,
    occ_hbm,
    w1_hbm,
    w2_hbm,
    wo_hbm,
    cot_hbm,
    inc_ref,
    aadj_ref,
    fa_ref,
    sa_ref,
    dwo_ref,
    x_ref,
    occ_ref,
    w1_ref,
    w2_ref,
    wo_ref,
    cot_ref,
    msend,
    mrow,
    mcol,
    xh,
    rs,
    nres,
    tmp,
    lsend,
    rsend,
    lrecv,
    rrecv,
    wt,
    wsplit,
    wide,
    inv,
    over_lanes,
    dpre,
    s12,
    d2,
    lscr,
    lturn,
    wturn,
    rscr,
    beo,
    grsend,
    gra,
    grb,
    grc,
    grt,
    grown,
    glp,
    gls,
    glown,
    dwf,
    dwsend,
    dwrecv,
    fsend,
    frecv,
    f1,
    f1recv,
    f2,
    f2recv,
    e1,
    e1recv,
    e2,
    e3,
    gown,
    oscr,
    io_sem,
    ss,
    rs_mr,
    rs_mc,
    rs_l,
    rs_ls,
    rs_r,
    rs_gs,
    rs_go,
    rs_gr,
    rs_gt,
    rs_dw,
    rs_f,
    rs_f1,
    rs_f2,
    rs_e1,
    rs_e2,
    rs_e3,
):
    r, c, q = lax.axis_index("row"), lax.axis_index("col"), lax.axis_index("seq")
    inner = q == c // 4
    diagonal = r == c
    me = r * 2 + q
    core, z = lax.rem(c, 2), c // 2
    sibling = (r, c + 1 - 2 * core, q)
    holder = (
        lax.rem(r // 4 + core, 2) * 4 + lax.rem(lax.rem(r, 4) + 2 - z + r // 2 + 4, 4),
        r,
        q,
    )

    def held(m):
        dz = lax.rem(2 - lax.rem(m, 4) + lax.rem(c, 4) + 4, 4)
        return lax.rem(c // 2 + dz, 4) * 2 + lax.rem(m // 4 + c // 4, 2)

    def holder_row(m):
        dz = lax.rem(m // 2 - c // 2 + 4, 4)
        return lax.rem(c // 4 + lax.rem(m, 2), 2) * 4 + lax.rem(lax.rem(c, 4) + 2 - dz + 4, 4)

    owner = (c, held(r), q)
    other = (r, lax.rem(c + 1, 8), q)

    def plane(t):
        m = lax.rem(me + t, 16)
        return m, (m // 2, c, lax.rem(m, 2))

    def line(t):
        m = lax.rem(c + t, 8)
        return m, (r, m, q)

    def far(src, dst, ssem, rsem, dev):
        return pltpu.make_async_remote_copy(
            src_ref=src, dst_ref=dst, send_sem=ssem, recv_sem=rsem, device_id=dev, device_id_type=MESH
        )

    def put(own, src, dst, ssem, rsem, dev):
        @pl.when(own)
        def _():
            pltpu.make_async_copy(src, dst, rsem).start()

        @pl.when(jnp.logical_not(own))
        def _():
            far(src, dst, ssem, rsem, dev).start()

    def arrived(size, mark):
        far(size, size, ss.at[0], mark, other).wait_recv()

    def sent(size, step):
        far(size, size, ss.at[step], rs_r.at[0], other).wait_send()

    load_wo = pltpu.make_async_copy(wo_hbm, wo_ref, io_sem.at[0])
    load_cot = pltpu.make_async_copy(cot_hbm, cot_ref, io_sem.at[1])

    load_x = pltpu.make_async_copy(x_hbm, x_ref, io_sem.at[3])
    load_occ = pltpu.make_async_copy(occ_hbm, occ_ref, io_sem.at[4])
    load_w1 = pltpu.make_async_copy(w1_hbm, w1_ref, io_sem.at[5])
    load_w2 = pltpu.make_async_copy(w2_hbm, w2_ref, io_sem.at[6])
    for load in (load_x, load_occ, load_w1, load_w2, load_wo, load_cot):
        load.start()

    barrier = pltpu.get_barrier_semaphore()

    def mask_to(t):
        return (lax.rem(r + t, 8), r, q)

    def mask_from(t):
        return (c, lax.rem(c + t, 8), q)

    @pl.loop(1, 8)
    def _(t):
        pl.semaphore_signal(barrier, inc=1, device_id=mask_to(t), device_id_type=MESH)
        pl.semaphore_signal(barrier, inc=1, device_id=mask_from(t), device_id_type=MESH)

    @pl.loop(1, 16)
    def _(t):
        pl.semaphore_signal(barrier, inc=1, device_id=plane(t)[1], device_id_type=MESH)

    @pl.loop(1, 8)
    def _(t):
        pl.semaphore_signal(barrier, inc=1, device_id=line(t)[1], device_id_type=MESH)

    y0, x0 = q * 2 + r // 4, lax.rem(r, 4)
    across = (r, lax.rem(z + 3 - 2 * lax.rem(z, 2), 4) * 2 + core, 1 - q)

    def at(y, x):
        return (lax.rem(y, 2) * 4 + x, c, y // 2)

    def along_x(t):
        return at(y0, lax.rem(x0 + t, 4))

    def along_y(t):
        return at(lax.rem(y0 + t, 4), x0)

    def along_z(t):
        return (r, lax.rem(z + t, 4) * 2 + core, q)

    def block(dy, dx, first, last):
        y, x = lax.rem(y0 + dy, 4), lax.rem(x0 + dx, 4)
        h, m = y // 2, lax.rem(y, 2) * 4 + x
        return rrecv.at[h, m, first:last, :]

    @pl.loop(1, 4)
    def _(t):
        dev = (r, lax.rem(z + t, 4) * 2 + core, 1 - q)
        pl.semaphore_signal(barrier, inc=1, device_id=dev, device_id_type=MESH)

    for dev in (holder, owner):
        pl.semaphore_signal(barrier, inc=1, device_id=dev, device_id_type=MESH)

    @pl.when(jnp.logical_not(diagonal))
    def _():
        for dev in (mask_to(0), mask_from(0)):
            pl.semaphore_signal(barrier, inc=1, device_id=dev, device_id_type=MESH)

    load_occ.wait()
    occ = occ_ref[...].astype(F32)
    msend[...] = jnp.concatenate([occ[:, :NS], occ[:, NS:]], axis=0).astype(BF16)

    load_x.wait()
    @pl.loop(0, 8)
    def _(t):
        xb = x_ref[pl.ds(t * 16, 16)].astype(F32).reshape(128, NCH)
        xc = xb - jnp.mean(xb, axis=-1, keepdims=True)
        rstd = lax.rsqrt(jnp.mean(xc * xc, axis=-1, keepdims=True) + 1e-05)
        z = xc * rstd
        xh[0, pl.ds(t * 128, 128), :] = z[:, :128]
        xh[1, pl.ds(t * 128, 128), :] = z[:, 128:]
        rs[pl.ds(t * 128, 128), :] = jnp.broadcast_to(rstd, (128, 128))

    load_w1.wait()
    load_w2.wait()
    wt[0:NP, :] = w1_ref[...]
    wt[NP:, :] = w2_ref[...]
    mine = msend[...].astype(F32)
    mine = jnp.where(q == 0, mine[:NQ], mine[NQ:])
    for k in range(NQ):
        n = both_halves(xh, pl.ds(k, NS, stride=NQ)).astype(BF16)
        nres[k] = n
        p = dot(wt[...], n, 1, 1) * mine[k : k + 1, :]
        lsend[k * NP : (k + 1) * NP, :] = p[:NP].astype(BF16)
        tmp[pl.ds(k, NP, stride=NQ), :] = p[NP:]
    rsend[...] = tmp[...].astype(BF16)

    pl.semaphore_wait(barrier, jnp.where(diagonal, 41, 43))

    mine_of_line = lax.rem(jnp.where(inner, z, z + 3 - 2 * lax.rem(z, 2)), 2)
    seq_of_line = jnp.where(inner, q, 1 - q)
    given = lrecv.at[mine_of_line * 2 + core, seq_of_line]
    given_mark = rs_l.at[mine_of_line, seq_of_line]

    def left_along():
        for t in range(1, 4):
            far(given, given, ss.at[2], given_mark, along_z(t)).start()
        far(given, given, ss.at[2], rs_ls.at[0], sibling).start()

    @pl.when(inner)
    def _():
        lrecv[lax.rem(c, 4), q] = lsend[...]
        left_along()

    @pl.when(jnp.logical_not(inner))
    def _():
        far(lsend, lrecv.at[lax.rem(c, 4), q], ss.at[2], rs_l.at[lax.rem(c, 4) // 2, q], across).start()

    far(rsend, rrecv.at[q, holder[0]], ss.at[3], rs_r.at[0], holder).start()

    put(diagonal, msend, mcol.at[c], ss.at[1], rs_mc.at[0], mask_to(0))

    @pl.loop(1, 8)
    def _(t):
        far(msend, mcol.at[c], ss.at[1], rs_mc.at[0], mask_to(t)).start()

    @pl.when(inner)
    def _():
        m = lax.rem(c, 4)
        pltpu.make_async_copy(msend, mrow.at[m], rs_mr.at[0]).start()

        @pl.loop(1, 8)
        def _(t):
            far(msend, mrow.at[m], ss.at[0], rs_mr.at[0], line(t)[1]).start()

    load_wo.wait()
    wide[...] = wo_ref[...].astype(F32)
    for e in range(NP):
        wsplit[(e % 2) * HALF + (e // 2) * NP : (e % 2) * HALF + (e // 2 + 1) * NP, :] = wide[pl.ds(e, NP, stride=NP), :].astype(BF16)

    wturn[...] = wsplit[...].T

    lane = lax.broadcasted_iota(jnp.int32, (NP, 128), 1)
    low = lax.rem(lane // 8, 2) == 0

    def in_turn(lo, hi):
        return jnp.concatenate([v[m * 8 : m * 8 + 8] for m in range(8) for v in (lo, hi)], axis=0).astype(BF16)

    load_cot.wait()
    for k in range(16):
        lo, hi = cot_ref[k].astype(F32), cot_ref[k + 16].astype(F32)
        s12[0, k * 128 : (k + 1) * 128, :] = in_turn(lo, hi)
        s12[1, k * 128 : (k + 1) * 128, :] = in_turn(hi, lo)

    def outer_adjoint(t):
        here = pl.ds(pl.multiple_of(t * 256, 256), 256)
        even, odd = wsplit[:HALF], wsplit[HALF:]
        plain, turned_s = s12[0, here, :], s12[1, here, :]
        halves = (
            (dot(even, plain, 1, 1), dot(odd, turned_s, 1, 1)),
            (dot(even, turned_s, 1, 1), dot(odd, plain, 1, 1)),
        )
        for u in range(2):
            for half, (a, b) in enumerate(halves):
                at = pl.ds(pl.multiple_of(half * HALF + (t * 2 + u) * NP, NP), NP)
                for p in range(16):
                    va = a[p * NP : (p + 1) * NP, u * 128 : (u + 1) * 128]
                    vb = b[p * NP : (p + 1) * NP, u * 128 : (u + 1) * 128]
                    dpre[at, p * 128 : (p + 1) * 128] = jnp.where(low, va, vb)

    pl.loop(0, 4)(outer_adjoint)

    @pl.when(jnp.logical_not(inner))
    def _():
        arrived(given, given_mark)
        left_along()

    came = block(0, 0, 0, 256)
    arrived(came, rs_r.at[0])
    for t in range(1, 4):
        far(came, came, ss.at[3], rs_r.at[4 - t], along_x(t)).start()
        far(came, came, ss.at[3], rs_r.at[7 - t], along_y(t)).start()

    pl.loop(4, 8)(outer_adjoint)

    arrived(mrow, rs_mr.at[0])
    arrived(mcol, rs_mc.at[0])

    count = jnp.zeros((64, 32), F32)
    count_lanes = jnp.zeros((32, 128), F32)
    for h in range(2):
        rows = jnp.concatenate([mrow[m].astype(F32)[h * NQ : (h + 1) * NQ] for m in range(4)], axis=0).astype(BF16)
        groups = [mcol[m].astype(F32)[h * NQ : (h + 1) * NQ] for m in range(8)]
        cols = jnp.concatenate(groups, axis=0).astype(BF16)
        twice = jnp.concatenate([g for g in groups for _ in range(2)], axis=0).astype(BF16)
        count = count + dot(cols, rows, 1, 1)
        count_lanes = count_lanes + dot(rows, twice, 1, 1)
    over_lanes[...] = 1.0 / (count_lanes + 0.001)
    inv[...] = jnp.where(low[:16], over_lanes[:16], over_lanes[16:])

    @pl.loop(0, 32)
    def _(i):
        rows = pl.ds(pl.multiple_of(i * NP, NP), NP)
        d2[rows, :] = (dpre[rows, :] * jnp.concatenate([over_lanes[pl.ds(i, 1), :]] * 16, axis=1)).astype(BF16)

    for t in range(1, 4):
        zt = lax.rem(z + t, 4)
        in_half = zt // 2 == q
        pp = lax.rem(jnp.where(in_half, zt, zt + 3 - 2 * lax.rem(zt, 2)), 2)
        h = jnp.where(in_half, q, 1 - q)
        slot = lrecv.at[pp * 2 + core, h]
        arrived(slot, rs_l.at[pp, h])
        far(slot, slot, ss.at[2], rs_ls.at[0], sibling).start()

    for t in range(1, 4):
        arrived(block(0, t, 0, 256), rs_r.at[t])
        half = block(0, t, 0, 128)
        for u in range(1, 4):
            far(half, half, ss.at[3], rs_r.at[7], along_y(u)).start()
        arrived(block(t, 0, 0, 256), rs_r.at[3 + t])
        half = block(t, 0, 128, 256)
        for u in range(1, 4):
            far(half, half, ss.at[3], rs_r.at[7], along_x(u)).start()

    def put_right(dy, dx):
        y, x = lax.rem(y0 + dy, 4), lax.rem(x0 + dx, 4)
        h, m = y // 2, lax.rem(y, 2) * 4 + x
        lanes = pl.ds(pl.multiple_of(h * NS, NS), NS)
        first = held(m) * 16
        for p in range(16):
            at = pl.ds(pl.multiple_of(p * 128 + first, 16), 16)
            v = rrecv[h, m, p * 16 : (p + 1) * 16, :]
            w = v.astype(F32)
            rscr[0, at, lanes] = v
            rscr[1, at, lanes] = jnp.concatenate([w[8:], w[:8]], axis=0).astype(BF16)

    put_right(0, 0)
    for t in range(1, 4):
        put_right(0, t)
        put_right(t, 0)

    arrived(lrecv.at[0:2], rs_ls.at[0])
    for h in range(2):
        for m in range(4):
            lscr[m * 256 : (m + 1) * 256, h * NS : (h + 1) * NS] = lrecv[m, h]
            lturn[h * NS : (h + 1) * NS, m * 256 : (m + 1) * 256] = lrecv[m, h].T

    def right_part(t):
        here = pl.ds(pl.multiple_of(t * 256, 256), 256)
        a = dot(lturn[...], d2[:, here], 1, 0).astype(BF16)
        for u in range(2):
            at = pl.ds(pl.multiple_of((t * 2 + u) * 16, 16), 16)
            for h in range(2):
                gt = a[h * NS : (h + 1) * NS, u * 128 : (u + 1) * 128].T
                for m in range(8):
                    row = holder_row(m)
                    grsend[h * 2 + row // 4, lax.rem(row, 4), at, :] = gt[m * 16 : (m + 1) * 16]

    for n in range(4):
        pl.loop(2 * n, 2 * n + 2)(right_part)
        rows = slice(n * 64, (n + 1) * 64)
        for t in range(1, 4):
            y, x = lax.rem(y0 + t, 4), lax.rem(x0 + t, 4)
            part = grsend.at[:, x, rows, :] if n % 2 else grsend.at[y, :, rows, :]
            to = along_x(t) if n % 2 else along_y(t)
            far(part, gra.at[n, t], ss.at[5], rs_gr.at[n], to).start()

    over = 1.0 / (count + 0.001)
    for k in range(16):
        lo, hi = [
            cot_ref[i].astype(F32) * jnp.broadcast_to(over[:, i : i + 1], (64, NZ)) for i in (k, k + 16)
        ]
        s12[0, k * 128 : (k + 1) * 128, :] = in_turn(lo, hi)
        s12[1, k * 128 : (k + 1) * 128, :] = in_turn(hi, lo)

    arrived(grsend.at[0:3, 0:3], rs_r.at[7])
    for t in range(1, 4):
        for u in range(1, 4):
            put_right(t, u)

    def outer_product(t):
        here = pl.ds(pl.multiple_of(t * 256, 256), 256)
        a = dot(lscr[:HALF], rscr[0, here, :], 1, 1)
        b = dot(lscr[HALF:], rscr[1, here, :], 1, 1)
        for u in range(2):
            lanes = slice(u * 128, (u + 1) * 128)
            even = pl.ds(pl.multiple_of((t * 2 + u) * NP, NP), NP)
            odd = pl.ds(pl.multiple_of(HALF + (t * 2 + u) * NP, NP), NP)
            for k in range(16):
                lo = a[k * NP : (k + 1) * NP, lanes]
                hi = b[k * NP : (k + 1) * NP, lanes]
                beo[even, k * 128 : (k + 1) * 128] = jnp.where(low, lo, hi).astype(BF16)
                beo[odd, k * 128 : (k + 1) * 128] = jnp.where(low, hi, lo).astype(BF16)

    pl.loop(0, 4)(outer_product)

    pl.loop(4, 8)(outer_product)

    for h in range(2):
        part = dot(beo[h * HALF : (h + 1) * HALF], s12[h], 1, 0)
        for p in range(16):
            dwf[pl.ds(2 * p + h, NP, stride=NP), :] = part[p * NP : (p + 1) * NP]
    for m in range(8):
        dwsend[m] = dwf[m * 128 : (m + 1) * 128, :].astype(BF16)
    pltpu.make_async_copy(dwsend.at[c], dwrecv.at[c], rs_dw.at[0]).start()

    @pl.loop(1, 8)
    def _(t):
        m = lax.rem(c + t, 8)
        far(dwsend.at[m], dwrecv.at[c], ss.at[8], rs_dw.at[0], (r, m, q)).start()

    for i in range(2):
        for half in range(2):
            part = 2 * half + i
            rows = slice(part * 64, (part + 1) * 64)
            arrived(gra.at[part, 1:4], rs_gr.at[part])
            for n in range(4):
                own = grsend[n, x0, rows, :] if i else grsend[y0, n, rows, :]
                total = own.astype(F32)
                for t in range(1, 4):
                    total = total + gra[part, t, n].astype(F32)
                grb[i, n, half] = total.astype(BF16)
        for t in range(1, 4):
            if i:
                far(grb.at[i, lax.rem(y0 + t, 4)], grc.at[i, t], ss.at[6], rs_gr.at[4 + i], along_y(t)).start()
            else:
                far(grb.at[i, lax.rem(x0 + t, 4)], grc.at[i, t], ss.at[6], rs_gr.at[4 + i], along_x(t)).start()

    def left_piece(pp, k):
        rows = pl.ds(pl.multiple_of((pp * 2 + k) * 256, 256), 256)
        g = dot(d2[rows, :], rscr[0], 1, 0)
        for h in range(2):
            glp[pp * 2 + k, h] = g[:, h * NS : (h + 1) * NS].astype(BF16)

    for pp in range(2):
        left_piece(pp, 1 - core)
        far(glp.at[pp * 2 + 1 - core], gls.at[pp], ss.at[4], rs_gs.at[pp], sibling).start()
    for pp in range(2):
        left_piece(pp, core)

    for pp in range(2):
        arrived(gls.at[pp], rs_gs.at[pp])
        m = pp * 2 + core
        for h in range(2):
            glp[m, h] = (glp[m, h].astype(F32) + gls[pp, h].astype(F32)).astype(BF16)
            put(
                jnp.logical_and(2 * q + pp == z, q == h),
                glp.at[m, h],
                glown.at[z],
                ss.at[4],
                rs_go.at[0],
                (r, 4 * q + m, h),
            )

    low_rows = lax.rem(lax.broadcasted_iota(jnp.int32, (NZ, 128), 1) // 8, 2) == 0

    def update(t):
        here = pl.ds(pl.multiple_of(t * 256, 256), 256)
        a = dot(wturn[:, :HALF], beo[:HALF, here], 1, 0)
        b = dot(wturn[:, HALF:], beo[HALF:, here], 1, 0)
        for u in range(2):
            k = t * 2 + u
            odd = b[:, u * 128 : (u + 1) * 128]
            odd = jnp.where(low_rows, pltpu.roll(odd, 120, 1), pltpu.roll(odd, 8, 1))
            o = ((a[:, u * 128 : (u + 1) * 128] + odd) * inv[pl.ds(k, 1), :]).astype(BF16).T.astype(F32)
            inc_ref[k] = jnp.concatenate([o[m * 16 : m * 16 + 8] for m in range(8)], axis=0).astype(BF16)
            inc_ref[k + 16] = jnp.concatenate([o[m * 16 + 8 : m * 16 + 16] for m in range(8)], axis=0).astype(BF16)

    pl.loop(0, 4)(update)

    for i in range(2):
        own = grb[i, y0] if i else grb[i, x0]
        total = own.astype(F32)
        arrived(grc.at[i, 1:4], rs_gr.at[4 + i])
        for t in range(1, 4):
            total = total + grc[i, t].astype(F32)
        for half in range(2):
            part = 2 * half + i
            grt[part * 64 : (part + 1) * 64, :] = total[half].astype(BF16)
    far(grt, grown, ss.at[7], rs_gt.at[0], owner).start()

    arrived(dwrecv, rs_dw.at[0])
    total = dwrecv[0].astype(F32)
    for m in range(1, 8):
        total = total + dwrecv[m].astype(F32)
    e1[...] = total

    @pl.loop(1, 16)
    def _(t):
        m, dev = plane(t)
        far(e1.at[pl.ds(pl.multiple_of(m * 8, 8), 8), :], e1recv.at[t], ss.at[12], rs_e1.at[0], dev).start()

    pl.loop(4, 8)(update)

    arrived(glown, rs_go.at[0])
    arrived(grown, rs_gt.at[0])
    gl = glown[0].astype(F32)
    for m in range(1, 4):
        gl = gl + glown[m].astype(F32)
    tmp[...] = grown[...].astype(F32)
    fsum = jnp.zeros((128, NCH), F32)
    for k in range(NQ):
        g = jnp.concatenate([gl[k * NP : (k + 1) * NP], tmp[pl.ds(k, NP, stride=NQ), :]], axis=0)
        g = g * mine[k : k + 1, :]
        high = g.astype(BF16)
        rest = (g - high.astype(F32)).astype(BF16)
        g2 = jnp.concatenate([high, rest], axis=0)
        gown[k] = g2
        fsum = fsum + dot(g2, nres[k], 1, 0)
    fsum = fsum[:64] + fsum[64:]
    for m in range(8):
        fsend[m] = fsum[m * 8 : (m + 1) * 8]
    pltpu.make_async_copy(fsend.at[c], frecv.at[c], rs_f.at[0]).start()

    @pl.loop(1, 8)
    def _(t):
        m = lax.rem(c + t, 8)
        far(fsend.at[m], frecv.at[c], ss.at[9], rs_f.at[0], (r, m, q)).start()

    arrived(e1recv.at[1:16], rs_e1.at[0])
    total = e1[pl.ds(pl.multiple_of(me * 8, 8), 8), :]
    for t in range(1, 16):
        total = total + e1recv[t]
    e2[...] = total
    pltpu.make_async_copy(e2, e3.at[pl.ds(pl.multiple_of(me * 8, 8), 8), :], rs_e2.at[0]).start()

    @pl.loop(1, 16)
    def _(t):
        m, dev = plane(t)
        far(e2, e3.at[pl.ds(pl.multiple_of(me * 8, 8), 8), :], ss.at[13], rs_e2.at[0], dev).start()

    w2x = jnp.concatenate([wt[...], wt[...]], axis=0)

    def adjoint(k):
        d = dot(gown[k], w2x, 0, 0)
        at = pl.ds(k, NS, stride=NQ)
        z = both_halves(xh, at)
        scale = rs[at, :]
        m1 = jnp.mean(d, axis=-1, keepdims=True)
        m2 = jnp.mean(d * z, axis=-1, keepdims=True)
        o = d - m1 - z * m2
        oscr[0, at, :] = scale * o[:, :128]
        oscr[1, at, :] = scale * o[:, 128:]

    for k in range(NQ):
        adjoint(k)

    @pl.loop(0, 8)
    def _(t):
        aadj_ref[pl.ds(t * 16, 16)] = both_halves(oscr, pl.ds(t * 128, 128)).reshape(16, NQ, NCH).astype(BF16)


    arrived(frecv, rs_f.at[0])
    total = frecv[0]
    for m in range(1, 8):
        total = total + frecv[m]
    f1[...] = total
    pltpu.make_async_copy(f1, f1recv.at[me], rs_f1.at[0]).start()

    @pl.loop(1, 16)
    def _(t):
        m = lax.rem(me + t, 16)
        far(f1, f1recv.at[me], ss.at[10], rs_f1.at[0], (m // 2, c, lax.rem(m, 2))).start()

    arrived(e3, rs_e2.at[0])
    chunk = dwo_ref.at[pl.ds(pl.multiple_of(c * 128, 128), 128), :]
    dwo_ref[pl.ds(pl.multiple_of(c * 128, 128), 128), :] = e3[...]
    far(e3, chunk, ss.at[14], rs_e3.at[0], sibling).start()

    for t in range(1, 4):
        far(e3, chunk, ss.at[14], rs_e3.at[4 - t], (r, lax.rem(z + t, 4) * 2 + core, q)).start()

    arrived(f1recv, rs_f1.at[0])
    total = f1recv[0]
    for m in range(1, 16):
        total = total + f1recv[m]
    f2[...] = total
    pltpu.make_async_copy(f2, f2recv.at[c], rs_f2.at[0]).start()

    @pl.loop(1, 8)
    def _(t):
        far(f2, f2recv.at[c], ss.at[11], rs_f2.at[0], (r, lax.rem(c + t, 8), q)).start()

    for t in range(1, 4):
        m = lax.rem(z + t, 4) * 2 + core
        chunk = dwo_ref.at[pl.ds(pl.multiple_of(m * 128, 128), 128), :]
        arrived(chunk, rs_e3.at[t])
        far(chunk, chunk, ss.at[14], rs_e3.at[0], sibling).start()

    arrived(dwo_ref.at[0:512, :], rs_e3.at[0])

    arrived(f2recv, rs_f2.at[0])
    fa_ref[...] = jnp.concatenate([f2recv[m] for m in range(4)], axis=0)
    sa_ref[...] = jnp.concatenate([f2recv[m] for m in range(4, 8)], axis=0)

    @pl.when(inner)
    def _():
        sent(mcol.at[0:7], 0)
        sent(rrecv.at[0, 0:7], 2)
        sent(rrecv.at[0, 0:7], 4)

    @pl.when(jnp.logical_not(inner))
    def _():
        sent(rrecv.at[0], 2)
        sent(rrecv.at[0], 4)

    @pl.when(diagonal)
    def _():
        sent(mcol.at[0:7], 1)

    @pl.when(jnp.logical_not(diagonal))
    def _():
        sent(mcol, 1)

    sent(rrecv, 3)
    sent(gra.at[0:3], 5)
    sent(gra.at[0, 0:3], 6)
    sent(grt, 7)
    sent(dwrecv.at[0:7], 8)
    sent(frecv.at[0:7], 9)
    sent(f1recv.at[0:15], 10)
    sent(f2recv.at[0:7], 11)
    sent(e1recv.at[0:15], 12)
    sent(e1recv.at[0:15], 13)
    sent(dwo_ref.at[0:896, :], 14)


def hand_over(*refs):
    copies = [pltpu.make_async_copy(refs[i], refs[5 + i], refs[10].at[i]) for i in range(5)]
    for copy in copies:
        copy.start()
    for copy in copies:
        copy.wait()


def local(x, occ, w1, w2, wo, cot):
    hbm = pl.BlockSpec(memory_space=pl.ANY)
    vmem = pl.BlockSpec(memory_space=pltpu.VMEM)
    dma = pltpu.SemaphoreType.DMA
    scratch = [
        pltpu.VMEM((NS, NQ, NCH), BF16),
        pltpu.VMEM((NQ, 2 * NS), jnp.int32),
        pltpu.VMEM((NP, NCH), BF16),
        pltpu.VMEM((NP, NCH), BF16),
        pltpu.VMEM((1024, NZ), BF16),
        pltpu.VMEM((32, 64, NZ), BF16),
        pltpu.VMEM((16, NS), BF16),
        pltpu.VMEM((4, 16, NS), BF16),
        pltpu.VMEM((8, 16, NS), BF16),
        pltpu.VMEM((2, 1024, 128), F32),
        pltpu.VMEM((1024, 128), F32),
        pltpu.VMEM((NQ, NS, NCH), BF16),
        pltpu.VMEM((256, NS), F32),
        pltpu.VMEM((256, NS), BF16),
        pltpu.VMEM((256, NS), BF16),
        pltpu.VMEM((4, 2, 256, NS), BF16),
        pltpu.VMEM((2, 8, 256, NS), BF16),
        pltpu.VMEM((64, NCH), BF16),
        pltpu.VMEM((1024, NZ), BF16),
        pltpu.VMEM((1024, NZ), F32),
        pltpu.VMEM((16, 128), F32),
        pltpu.VMEM((32, 128), F32),
        pltpu.VMEM((1024, PAIRS), F32),
        pltpu.VMEM((2, PAIRS, NZ), BF16),
        pltpu.VMEM((1024, PAIRS), BF16),
        pltpu.VMEM((1024, 256), BF16),
        pltpu.VMEM((256, 1024), BF16),
        pltpu.VMEM((NZ, 1024), BF16),
        pltpu.VMEM((2, PAIRS, 256), BF16),
        pltpu.VMEM((1024, PAIRS), BF16),
        pltpu.VMEM((4, 4, 256, NS), BF16),
        pltpu.VMEM((4, 4, 4, 64, NS), BF16),
        pltpu.VMEM((2, 4, 2, 64, NS), BF16),
        pltpu.VMEM((2, 4, 2, 64, NS), BF16),
        pltpu.VMEM((256, NS), BF16),
        pltpu.VMEM((256, NS), BF16),
        pltpu.VMEM((4, 2, 256, NS), BF16),
        pltpu.VMEM((2, 2, 256, NS), BF16),
        pltpu.VMEM((4, 256, NS), BF16),
        pltpu.VMEM((1024, NZ), F32),
        pltpu.VMEM((8, 128, NZ), BF16),
        pltpu.VMEM((8, 128, NZ), BF16),
        pltpu.VMEM((8, 8, NCH), F32),
        pltpu.VMEM((8, 8, NCH), F32),
        pltpu.VMEM((8, NCH), F32),
        pltpu.VMEM((16, 8, NCH), F32),
        pltpu.VMEM((8, NCH), F32),
        pltpu.VMEM((8, 8, NCH), F32),
        pltpu.VMEM((128, NZ), F32),
        pltpu.VMEM((16, 8, NZ), F32),
        pltpu.VMEM((8, NZ), F32),
        pltpu.VMEM((128, NZ), F32),
        pltpu.VMEM((NQ, 128, NS), BF16),
        pltpu.VMEM((2, 1024, 128), F32),
        dma((7,)),
        dma((15,)),
        dma((1,)),
        dma((1,)),
        dma((2, 2)),
        dma((1,)),
        dma((8,)),
        dma((2,)),
        dma((1,)),
        dma((6,)),
        dma((1,)),
        dma((1,)),
        dma((1,)),
        dma((1,)),
        dma((1,)),
        dma((1,)),
        dma((1,)),
        dma((4,)),
    ]
    inc, aadj, fa, sa, dwo = pl.pallas_call(
        kernel,
        out_shape=(
            pltpu.VMEM((32, 64, NZ), BF16),
            pltpu.VMEM((NS, NQ, NCH), BF16),
            pltpu.VMEM((NP, NCH), F32),
            pltpu.VMEM((NP, NCH), F32),
            pltpu.VMEM((1024, NZ), F32),
        ),
        in_specs=[hbm] * 6,
        out_specs=(vmem,) * 5,
        scratch_shapes=scratch,
        compiler_params=pltpu.CompilerParams(vmem_limit_bytes=60 * 1024 * 1024, has_side_effects=True, collective_id=0),
    )(x, occ.T, w1.T, w2.T, wo, cot)
    outs = [pltpu.with_memory_space_constraint(o, pltpu.VMEM) for o in (inc, aadj, fa, sa, dwo)]
    inc, aadj, fa, sa, dwo = pl.pallas_call(
        hand_over,
        out_shape=tuple(jax.ShapeDtypeStruct(o.shape, o.dtype) for o in outs),
        in_specs=[vmem] * 5,
        out_specs=(hbm,) * 5,
        scratch_shapes=[dma((5,))],
    )(*outs)
    return inc, aadj, fa.T, sa.T, dwo


def solution(mesh):
    placed = (
        P("seq", ("row", "col"), None),
        P(None, ("row", "col")),
        P(),
        P(),
        P(),
        P(("row", "seq"), "col", None),
    )
    return jax.shard_map(
        local,
        mesh=mesh,
        in_specs=placed,
        out_specs=(P(("row", "seq"), "col", None), P("seq", ("row", "col"), None), P(), P(), P()),
        check_vma=False,
    )
```

```python
import jax
import jax.numpy as jnp
from jax import lax
from jax.experimental import pallas as pl
from jax.experimental.pallas import tpu as pltpu
from jax.sharding import PartitionSpec as P

F32 = jnp.float32
BF16 = jnp.bfloat16
MESH = pl.DeviceIdType.MESH

NS = 128
NQ = 8
NCH = 256
NP = 32
NZ = 128
HALF = 512
PAIRS = 2048


def dot(a, b, ca, cb):
    return lax.dot_general(a, b, (((ca,), (cb,)), ((), ())), preferred_element_type=F32)


def both_halves(ref, rows):
    return jnp.concatenate([ref[0, rows, :], ref[1, rows, :]], axis=1)


def kernel(
    x_hbm,
    occ_hbm,
    w1_hbm,
    w2_hbm,
    wo_hbm,
    cot_hbm,
    inc_ref,
    aadj_ref,
    fa_ref,
    sa_ref,
    dwo_ref,
    x_ref,
    occ_ref,
    w1_ref,
    w2_ref,
    wo_ref,
    cot_ref,
    msend,
    mrow,
    mcol,
    xh,
    rs,
    nres,
    tmp,
    lsend,
    rsend,
    lrecv,
    rrecv,
    wt,
    wsplit,
    wide,
    inv,
    over_lanes,
    dpre,
    s12,
    d2,
    lscr,
    lturn,
    wturn,
    rscr,
    beo,
    grsend,
    gra,
    grb,
    grc,
    grt,
    grown,
    glp,
    gls,
    glown,
    dwf,
    dwsend,
    dwrecv,
    fsend,
    frecv,
    f1,
    f1recv,
    f2,
    f2recv,
    e1,
    e1recv,
    e2,
    e3,
    e3out,
    gown,
    oscr,
    io_sem,
    ss,
    rs_mr,
    rs_mc,
    rs_l,
    rs_ls,
    rs_r,
    rs_gs,
    rs_go,
    rs_gr,
    rs_gt,
    rs_dw,
    rs_f,
    rs_f1,
    rs_f2,
    rs_e1,
    rs_e2,
    rs_e3,
):
    r, c, q = lax.axis_index("row"), lax.axis_index("col"), lax.axis_index("seq")
    inner = q == c // 4
    diagonal = r == c
    me = r * 2 + q
    core, z = lax.rem(c, 2), c // 2
    sibling = (r, c + 1 - 2 * core, q)
    def place(col, m, h):
        dz = lax.rem(m // 2 - col // 2 + 4, 4)
        down = lax.rem(m, 2) * (1 + 2 * (dz // 2))
        return lax.rem(col // 4 + 2 * h + down, 4), lax.rem(lax.rem(col, 4) + 6 - dz, 4)

    def held(y, x):
        dz = lax.rem(6 - x + lax.rem(c, 4), 4)
        down = lax.rem(y - c // 4 + 4, 4)
        odd = lax.rem(down, 2)
        return lax.rem(c // 2 + dz, 4) * 2 + odd, lax.rem(down // 2 + odd * (dz // 2), 2)

    holder_y, holder_x = place(r, c, q)
    holder_slot = (holder_y // 2, lax.rem(holder_y, 2) * 4 + holder_x)
    holder = (holder_slot[1], r, holder_slot[0])
    y0, x0 = q * 2 + r // 4, lax.rem(r, 4)
    owner = (c, *held(y0, x0))
    other = (r, lax.rem(c + 1, 8), q)

    def plane(t):
        m = lax.rem(me + t, 16)
        return m, (m // 2, c, lax.rem(m, 2))

    def line(t):
        m = lax.rem(c + t, 8)
        return m, (r, m, q)

    def far(src, dst, ssem, rsem, dev):
        return pltpu.make_async_remote_copy(
            src_ref=src, dst_ref=dst, send_sem=ssem, recv_sem=rsem, device_id=dev, device_id_type=MESH
        )

    def put(own, src, dst, ssem, rsem, dev):
        @pl.when(own)
        def _():
            pltpu.make_async_copy(src, dst, rsem).start()

        @pl.when(jnp.logical_not(own))
        def _():
            far(src, dst, ssem, rsem, dev).start()

    def arrived(size, mark):
        far(size, size, ss.at[0], mark, other).wait_recv()

    def sent(size, step):
        far(size, size, ss.at[step], rs_r.at[0], other).wait_send()

    load_wo = pltpu.make_async_copy(wo_hbm, wo_ref, io_sem.at[0])
    load_cot = pltpu.make_async_copy(cot_hbm, cot_ref, io_sem.at[1])

    load_x = pltpu.make_async_copy(x_hbm, x_ref, io_sem.at[3])
    load_occ = pltpu.make_async_copy(occ_hbm, occ_ref, io_sem.at[4])
    load_w1 = pltpu.make_async_copy(w1_hbm, w1_ref, io_sem.at[5])
    load_w2 = pltpu.make_async_copy(w2_hbm, w2_ref, io_sem.at[6])
    for load in (load_x, load_occ, load_w1, load_w2, load_wo, load_cot):
        load.start()

    barrier = pltpu.get_barrier_semaphore()

    def mask_to(t):
        return (lax.rem(r + t, 8), r, q)

    def mask_from(t):
        return (c, lax.rem(c + t, 8), q)

    @pl.loop(1, 8)
    def _(t):
        pl.semaphore_signal(barrier, inc=1, device_id=mask_to(t), device_id_type=MESH)
        pl.semaphore_signal(barrier, inc=1, device_id=mask_from(t), device_id_type=MESH)

    @pl.loop(1, 16)
    def _(t):
        pl.semaphore_signal(barrier, inc=1, device_id=plane(t)[1], device_id_type=MESH)

    @pl.loop(1, 8)
    def _(t):
        pl.semaphore_signal(barrier, inc=1, device_id=line(t)[1], device_id_type=MESH)

    across = (r, lax.rem(z + 3 - 2 * lax.rem(z, 2), 4) * 2 + core, 1 - q)

    def at(y, x):
        return (lax.rem(y, 2) * 4 + x, c, y // 2)

    def along_x(t):
        return at(y0, lax.rem(x0 + t, 4))

    def along_y(t):
        return at(lax.rem(y0 + t, 4), x0)

    def along_z(t):
        return (r, lax.rem(z + t, 4) * 2 + core, q)

    def block(dy, dx, first, last):
        y, x = lax.rem(y0 + dy, 4), lax.rem(x0 + dx, 4)
        h, m = y // 2, lax.rem(y, 2) * 4 + x
        return rrecv.at[h, m, first:last, :]

    @pl.loop(1, 4)
    def _(t):
        dev = (r, lax.rem(z + t, 4) * 2 + core, 1 - q)
        pl.semaphore_signal(barrier, inc=1, device_id=dev, device_id_type=MESH)

    for dev in (holder, owner):
        pl.semaphore_signal(barrier, inc=1, device_id=dev, device_id_type=MESH)

    @pl.when(jnp.logical_not(diagonal))
    def _():
        for dev in (mask_to(0), mask_from(0)):
            pl.semaphore_signal(barrier, inc=1, device_id=dev, device_id_type=MESH)

    load_occ.wait()
    occ = occ_ref[...].astype(F32)
    msend[...] = jnp.concatenate([occ[:, :NS], occ[:, NS:]], axis=0).astype(BF16)

    load_x.wait()
    @pl.loop(0, 8)
    def _(t):
        xb = x_ref[pl.ds(t * 16, 16)].astype(F32).reshape(128, NCH)
        xc = xb - jnp.mean(xb, axis=-1, keepdims=True)
        rstd = lax.rsqrt(jnp.mean(xc * xc, axis=-1, keepdims=True) + 1e-05)
        z = xc * rstd
        xh[0, pl.ds(t * 128, 128), :] = z[:, :128]
        xh[1, pl.ds(t * 128, 128), :] = z[:, 128:]
        rs[pl.ds(t * 128, 128), :] = jnp.broadcast_to(rstd, (128, 128))

    load_w1.wait()
    load_w2.wait()
    wt[0:NP, :] = w1_ref[...]
    wt[NP:, :] = w2_ref[...]
    mine = msend[...].astype(F32)
    mine = jnp.where(q == 0, mine[:NQ], mine[NQ:])
    for k in range(NQ):
        n = both_halves(xh, pl.ds(k, NS, stride=NQ)).astype(BF16)
        nres[k] = n
        p = dot(wt[...], n, 1, 1) * mine[k : k + 1, :]
        lsend[k * NP : (k + 1) * NP, :] = p[:NP].astype(BF16)
        tmp[pl.ds(k, NP, stride=NQ), :] = p[NP:]
    rsend[...] = tmp[...].astype(BF16)

    pl.semaphore_wait(barrier, jnp.where(diagonal, 41, 43))

    mine_of_line = lax.rem(jnp.where(inner, z, z + 3 - 2 * lax.rem(z, 2)), 2)
    seq_of_line = jnp.where(inner, q, 1 - q)
    given = lrecv.at[mine_of_line * 2 + core, seq_of_line]
    given_mark = rs_l.at[mine_of_line, seq_of_line]

    def left_along():
        for t in range(1, 4):
            far(given, given, ss.at[2], given_mark, along_z(t)).start()
        far(given, given, ss.at[2], rs_ls.at[0], sibling).start()

    @pl.when(inner)
    def _():
        lrecv[lax.rem(c, 4), q] = lsend[...]
        left_along()

    @pl.when(jnp.logical_not(inner))
    def _():
        far(lsend, lrecv.at[lax.rem(c, 4), q], ss.at[2], rs_l.at[lax.rem(c, 4) // 2, q], across).start()

    far(rsend, rrecv.at[holder_slot[0], holder_slot[1]], ss.at[3], rs_r.at[0], holder).start()

    put(diagonal, msend, mcol.at[c], ss.at[1], rs_mc.at[0], mask_to(0))

    @pl.loop(1, 8)
    def _(t):
        far(msend, mcol.at[c], ss.at[1], rs_mc.at[0], mask_to(t)).start()

    @pl.when(inner)
    def _():
        m = lax.rem(c, 4)
        pltpu.make_async_copy(msend, mrow.at[m], rs_mr.at[0]).start()

        @pl.loop(1, 8)
        def _(t):
            far(msend, mrow.at[m], ss.at[0], rs_mr.at[0], line(t)[1]).start()

    load_wo.wait()
    wide[...] = wo_ref[...].astype(F32)
    for e in range(NP):
        wsplit[(e % 2) * HALF + (e // 2) * NP : (e % 2) * HALF + (e // 2 + 1) * NP, :] = wide[pl.ds(e, NP, stride=NP), :].astype(BF16)

    wturn[...] = wsplit[...].T

    lane = lax.broadcasted_iota(jnp.int32, (NP, 128), 1)
    low = lax.rem(lane // 8, 2) == 0

    def in_turn(lo, hi):
        return jnp.concatenate([v[m * 8 : m * 8 + 8] for m in range(8) for v in (lo, hi)], axis=0).astype(BF16)

    load_cot.wait()
    for k in range(16):
        lo, hi = cot_ref[k].astype(F32), cot_ref[k + 16].astype(F32)
        s12[0, k * 128 : (k + 1) * 128, :] = in_turn(lo, hi)
        s12[1, k * 128 : (k + 1) * 128, :] = in_turn(hi, lo)

    def outer_adjoint(t):
        here = pl.ds(pl.multiple_of(t * 256, 256), 256)
        even, odd = wsplit[:HALF], wsplit[HALF:]
        plain, turned_s = s12[0, here, :], s12[1, here, :]
        halves = (
            (dot(even, plain, 1, 1), dot(odd, turned_s, 1, 1)),
            (dot(even, turned_s, 1, 1), dot(odd, plain, 1, 1)),
        )
        for u in range(2):
            for half, (a, b) in enumerate(halves):
                at = pl.ds(pl.multiple_of(half * HALF + (t * 2 + u) * NP, NP), NP)
                for p in range(16):
                    va = a[p * NP : (p + 1) * NP, u * 128 : (u + 1) * 128]
                    vb = b[p * NP : (p + 1) * NP, u * 128 : (u + 1) * 128]
                    dpre[at, p * 128 : (p + 1) * 128] = jnp.where(low, va, vb)

    pl.loop(0, 4)(outer_adjoint)

    @pl.when(jnp.logical_not(inner))
    def _():
        arrived(given, given_mark)
        left_along()

    came = block(0, 0, 0, 256)
    arrived(came, rs_r.at[0])
    upper, lower = block(0, 0, 0, 128), block(0, 0, 128, 256)
    for t in range(1, 4):
        far(upper, upper, ss.at[3], rs_r.at[4 - t], along_x(t)).start()
        far(lower, lower, ss.at[3], rs_r.at[7 - t], along_y(t)).start()
    for t in range(1, 4):
        far(upper, upper, ss.at[3], rs_r.at[7], along_y(t)).start()
        far(lower, lower, ss.at[3], rs_r.at[7], along_x(t)).start()

    pl.loop(4, 8)(outer_adjoint)

    arrived(mrow, rs_mr.at[0])
    arrived(mcol, rs_mc.at[0])

    count = jnp.zeros((64, 32), F32)
    count_lanes = jnp.zeros((32, 128), F32)
    for h in range(2):
        rows = jnp.concatenate([mrow[m].astype(F32)[h * NQ : (h + 1) * NQ] for m in range(4)], axis=0).astype(BF16)
        groups = [mcol[m].astype(F32)[h * NQ : (h + 1) * NQ] for m in range(8)]
        cols = jnp.concatenate(groups, axis=0).astype(BF16)
        twice = jnp.concatenate([g for g in groups for _ in range(2)], axis=0).astype(BF16)
        count = count + dot(cols, rows, 1, 1)
        count_lanes = count_lanes + dot(rows, twice, 1, 1)
    over_lanes[...] = 1.0 / (count_lanes + 0.001)
    inv[...] = jnp.where(low[:16], over_lanes[:16], over_lanes[16:])

    @pl.loop(0, 32)
    def _(i):
        rows = pl.ds(pl.multiple_of(i * NP, NP), NP)
        d2[rows, :] = (dpre[rows, :] * jnp.concatenate([over_lanes[pl.ds(i, 1), :]] * 16, axis=1)).astype(BF16)

    for t in range(1, 4):
        zt = lax.rem(z + t, 4)
        in_half = zt // 2 == q
        pp = lax.rem(jnp.where(in_half, zt, zt + 3 - 2 * lax.rem(zt, 2)), 2)
        h = jnp.where(in_half, q, 1 - q)
        slot = lrecv.at[pp * 2 + core, h]
        arrived(slot, rs_l.at[pp, h])
        far(slot, slot, ss.at[2], rs_ls.at[0], sibling).start()

    for t in range(1, 4):
        half = block(0, t, 0, 128)
        arrived(half, rs_r.at[t])
        for u in range(1, 4):
            far(half, half, ss.at[3], rs_r.at[7], along_y(u)).start()
        half = block(t, 0, 128, 256)
        arrived(half, rs_r.at[3 + t])
        for u in range(1, 4):
            far(half, half, ss.at[3], rs_r.at[7], along_x(u)).start()

    def put_right(dy, dx, pairs):
        y, x = lax.rem(y0 + dy, 4), lax.rem(x0 + dx, 4)
        h, m = y // 2, lax.rem(y, 2) * 4 + x
        col, seq = held(y, x)
        lanes = pl.ds(pl.multiple_of(seq * NS, NS), NS)
        first = col * 16
        for p in pairs:
            at = pl.ds(pl.multiple_of(p * 128 + first, 16), 16)
            v = rrecv[h, m, p * 16 : (p + 1) * 16, :]
            w = v.astype(F32)
            rscr[0, at, lanes] = v
            rscr[1, at, lanes] = jnp.concatenate([w[8:], w[:8]], axis=0).astype(BF16)

    put_right(0, 0, range(16))
    for t in range(1, 4):
        put_right(0, t, range(8))
        put_right(t, 0, range(8, 16))

    arrived(lrecv.at[0:2], rs_ls.at[0])
    for h in range(2):
        for m in range(4):
            lscr[m * 256 : (m + 1) * 256, h * NS : (h + 1) * NS] = lrecv[m, h]
            lturn[h * NS : (h + 1) * NS, m * 256 : (m + 1) * 256] = lrecv[m, h].T

    def right_part(t):
        here = pl.ds(pl.multiple_of(t * 256, 256), 256)
        a = dot(lturn[...], d2[:, here], 1, 0).astype(BF16)
        for u in range(2):
            at = pl.ds(pl.multiple_of((t * 2 + u) * 16, 16), 16)
            for h in range(2):
                gt = a[h * NS : (h + 1) * NS, u * 128 : (u + 1) * 128].T
                for m in range(8):
                    y, x = place(c, m, h)
                    grsend[y, x, at, :] = gt[m * 16 : (m + 1) * 16]

    for n in range(4):
        pl.loop(2 * n, 2 * n + 2)(right_part)
        rows = slice(n * 64, (n + 1) * 64)
        for t in range(1, 4):
            y, x = lax.rem(y0 + t, 4), lax.rem(x0 + t, 4)
            part = grsend.at[:, x, rows, :] if n % 2 else grsend.at[y, :, rows, :]
            to = along_x(t) if n % 2 else along_y(t)
            far(part, gra.at[n, t], ss.at[5], rs_gr.at[n], to).start()

    over = 1.0 / (count + 0.001)
    for k in range(16):
        lo, hi = [
            cot_ref[i].astype(F32) * jnp.broadcast_to(over[:, i : i + 1], (64, NZ)) for i in (k, k + 16)
        ]
        s12[0, k * 128 : (k + 1) * 128, :] = in_turn(lo, hi)
        s12[1, k * 128 : (k + 1) * 128, :] = in_turn(hi, lo)

    arrived(grsend.at[0:3], rs_r.at[7])
    for t in range(1, 4):
        put_right(0, t, range(8, 16))
        put_right(t, 0, range(8))
        for u in range(1, 4):
            put_right(t, u, range(16))

    def outer_product(t):
        here = pl.ds(pl.multiple_of(t * 256, 256), 256)
        a = dot(lscr[:HALF], rscr[0, here, :], 1, 1)
        b = dot(lscr[HALF:], rscr[1, here, :], 1, 1)
        for u in range(2):
            lanes = slice(u * 128, (u + 1) * 128)
            even = pl.ds(pl.multiple_of((t * 2 + u) * NP, NP), NP)
            odd = pl.ds(pl.multiple_of(HALF + (t * 2 + u) * NP, NP), NP)
            for k in range(16):
                lo = a[k * NP : (k + 1) * NP, lanes]
                hi = b[k * NP : (k + 1) * NP, lanes]
                beo[even, k * 128 : (k + 1) * 128] = jnp.where(low, lo, hi).astype(BF16)
                beo[odd, k * 128 : (k + 1) * 128] = jnp.where(low, hi, lo).astype(BF16)

    pl.loop(0, 4)(outer_product)

    pl.loop(4, 8)(outer_product)

    for h in range(2):
        part = dot(beo[h * HALF : (h + 1) * HALF], s12[h], 1, 0)
        for p in range(16):
            dwf[pl.ds(2 * p + h, NP, stride=NP), :] = part[p * NP : (p + 1) * NP]
    for m in range(8):
        dwsend[m] = dwf[m * 128 : (m + 1) * 128, :].astype(BF16)
    pltpu.make_async_copy(dwsend.at[c], dwrecv.at[c], rs_dw.at[0]).start()

    @pl.loop(1, 8)
    def _(t):
        m = lax.rem(c + t, 8)
        far(dwsend.at[m], dwrecv.at[c], ss.at[8], rs_dw.at[0], (r, m, q)).start()

    for i in range(2):
        for half in range(2):
            part = 2 * half + i
            rows = slice(part * 64, (part + 1) * 64)
            arrived(gra.at[part, 1:4], rs_gr.at[part])
            for n in range(4):
                own = grsend[n, x0, rows, :] if i else grsend[y0, n, rows, :]
                total = own.astype(F32)
                for t in range(1, 4):
                    total = total + gra[part, t, n].astype(F32)
                grb[i, n, half] = total.astype(BF16)
        for t in range(1, 4):
            if i:
                far(grb.at[i, lax.rem(y0 + t, 4)], grc.at[i, t], ss.at[6], rs_gr.at[4 + i], along_y(t)).start()
            else:
                far(grb.at[i, lax.rem(x0 + t, 4)], grc.at[i, t], ss.at[6], rs_gr.at[4 + i], along_x(t)).start()

    def left_piece(pp, k):
        rows = pl.ds(pl.multiple_of((pp * 2 + k) * 256, 256), 256)
        g = dot(d2[rows, :], rscr[0], 1, 0)
        for h in range(2):
            glp[pp * 2 + k, h] = g[:, h * NS : (h + 1) * NS].astype(BF16)

    for pp in range(2):
        left_piece(pp, 1 - core)
        far(glp.at[pp * 2 + 1 - core], gls.at[pp], ss.at[4], rs_gs.at[pp], sibling).start()
    for pp in range(2):
        left_piece(pp, core)

    for pp in range(2):
        arrived(gls.at[pp], rs_gs.at[pp])
        m = pp * 2 + core
        for h in range(2):
            glp[m, h] = (glp[m, h].astype(F32) + gls[pp, h].astype(F32)).astype(BF16)
            put(
                jnp.logical_and(2 * q + pp == z, q == h),
                glp.at[m, h],
                glown.at[z],
                ss.at[4],
                rs_go.at[0],
                (r, 4 * q + m, h),
            )

    low_rows = lax.rem(lax.broadcasted_iota(jnp.int32, (NZ, 128), 1) // 8, 2) == 0

    def update(t):
        here = pl.ds(pl.multiple_of(t * 256, 256), 256)
        a = dot(wturn[:, :HALF], beo[:HALF, here], 1, 0)
        b = dot(wturn[:, HALF:], beo[HALF:, here], 1, 0)
        for u in range(2):
            k = t * 2 + u
            odd = b[:, u * 128 : (u + 1) * 128]
            odd = jnp.where(low_rows, pltpu.roll(odd, 120, 1), pltpu.roll(odd, 8, 1))
            o = ((a[:, u * 128 : (u + 1) * 128] + odd) * inv[pl.ds(k, 1), :]).astype(BF16).T.astype(F32)
            inc_ref[k] = jnp.concatenate([o[m * 16 : m * 16 + 8] for m in range(8)], axis=0).astype(BF16)
            inc_ref[k + 16] = jnp.concatenate([o[m * 16 + 8 : m * 16 + 16] for m in range(8)], axis=0).astype(BF16)

    pl.loop(0, 2)(update)

    for i in range(2):
        own = grb[i, y0] if i else grb[i, x0]
        total = own.astype(F32)
        arrived(grc.at[i, 1:4], rs_gr.at[4 + i])
        for t in range(1, 4):
            total = total + grc[i, t].astype(F32)
        for half in range(2):
            part = 2 * half + i
            grt[part * 64 : (part + 1) * 64, :] = total[half].astype(BF16)
    far(grt, grown, ss.at[7], rs_gt.at[0], owner).start()

    pl.loop(2, 5)(update)

    arrived(dwrecv, rs_dw.at[0])
    total = dwrecv[0].astype(F32)
    for m in range(1, 8):
        total = total + dwrecv[m].astype(F32)
    e1[...] = total

    @pl.loop(1, 16)
    def _(t):
        m, dev = plane(t)
        far(e1.at[pl.ds(pl.multiple_of(m * 8, 8), 8), :], e1recv.at[t], ss.at[12], rs_e1.at[0], dev).start()

    pl.loop(5, 8)(update)

    arrived(glown, rs_go.at[0])
    arrived(grown, rs_gt.at[0])
    gl = glown[0].astype(F32)
    for m in range(1, 4):
        gl = gl + glown[m].astype(F32)
    tmp[...] = grown[...].astype(F32)
    fsum = jnp.zeros((128, NCH), F32)
    for k in range(NQ):
        g = jnp.concatenate([gl[k * NP : (k + 1) * NP], tmp[pl.ds(k, NP, stride=NQ), :]], axis=0)
        g = g * mine[k : k + 1, :]
        high = g.astype(BF16)
        rest = (g - high.astype(F32)).astype(BF16)
        g2 = jnp.concatenate([high, rest], axis=0)
        gown[k] = g2
        fsum = fsum + dot(g2, nres[k], 1, 0)
    fsum = fsum[:64] + fsum[64:]
    for m in range(8):
        fsend[m] = fsum[m * 8 : (m + 1) * 8]
    pltpu.make_async_copy(fsend.at[c], frecv.at[c], rs_f.at[0]).start()

    @pl.loop(1, 8)
    def _(t):
        m = lax.rem(c + t, 8)
        far(fsend.at[m], frecv.at[c], ss.at[9], rs_f.at[0], (r, m, q)).start()

    arrived(e1recv.at[1:16], rs_e1.at[0])
    total = e1[pl.ds(pl.multiple_of(me * 8, 8), 8), :]
    for t in range(1, 16):
        total = total + e1recv[t]
    e2[...] = total
    pltpu.make_async_copy(e2, e3.at[pl.ds(pl.multiple_of(me * 8, 8), 8), :], rs_e2.at[0]).start()

    @pl.loop(1, 16)
    def _(t):
        m, dev = plane(t)
        far(e2, e3.at[pl.ds(pl.multiple_of(me * 8, 8), 8), :], ss.at[13], rs_e2.at[0], dev).start()

    w2x = jnp.concatenate([wt[...], wt[...]], axis=0)

    def adjoint(k):
        d = dot(gown[k], w2x, 0, 0)
        at = pl.ds(k, NS, stride=NQ)
        z = both_halves(xh, at)
        scale = rs[at, :]
        m1 = jnp.mean(d, axis=-1, keepdims=True)
        m2 = jnp.mean(d * z, axis=-1, keepdims=True)
        o = d - m1 - z * m2
        oscr[0, at, :] = scale * o[:, :128]
        oscr[1, at, :] = scale * o[:, 128:]

    for k in range(NQ):
        adjoint(k)

    @pl.loop(0, 8)
    def _(t):
        aadj_ref[pl.ds(t * 16, 16)] = both_halves(oscr, pl.ds(t * 128, 128)).reshape(16, NQ, NCH).astype(BF16)


    arrived(frecv, rs_f.at[0])
    total = frecv[0]
    for m in range(1, 8):
        total = total + frecv[m]
    f1[...] = total
    pltpu.make_async_copy(f1, f1recv.at[me], rs_f1.at[0]).start()

    @pl.loop(1, 16)
    def _(t):
        m = lax.rem(me + t, 16)
        far(f1, f1recv.at[me], ss.at[10], rs_f1.at[0], (m // 2, c, lax.rem(m, 2))).start()

    arrived(e3, rs_e2.at[0])
    rows = pl.ds(pl.multiple_of(c * 128, 128), 128)
    e3out[rows, :] = e3[...].astype(BF16)
    chunk = e3out.at[rows, :]
    far(chunk, chunk, ss.at[14], rs_e3.at[0], sibling).start()
    for t in range(1, 4):
        far(chunk, chunk, ss.at[14], rs_e3.at[4 - t], along_z(t)).start()

    arrived(f1recv, rs_f1.at[0])
    total = f1recv[0]
    for m in range(1, 16):
        total = total + f1recv[m]
    f2[...] = total
    pltpu.make_async_copy(f2, f2recv.at[c], rs_f2.at[0]).start()

    @pl.loop(1, 8)
    def _(t):
        far(f2, f2recv.at[c], ss.at[11], rs_f2.at[0], (r, lax.rem(c + t, 8), q)).start()

    for t in range(1, 4):
        m = lax.rem(z + t, 4) * 2 + core
        chunk = e3out.at[pl.ds(pl.multiple_of(m * 128, 128), 128), :]
        arrived(chunk, rs_e3.at[t])
        far(chunk, chunk, ss.at[14], rs_e3.at[0], sibling).start()

    arrived(e3out.at[0:512, :], rs_e3.at[0])
    dwo_ref[...] = e3out[...].astype(F32)

    arrived(f2recv, rs_f2.at[0])
    fa_ref[...] = jnp.concatenate([f2recv[m] for m in range(4)], axis=0)
    sa_ref[...] = jnp.concatenate([f2recv[m] for m in range(4, 8)], axis=0)

    @pl.when(inner)
    def _():
        sent(mcol.at[0:7], 0)
        sent(rrecv.at[0, 0:7], 2)
        sent(rrecv.at[0, 0:7], 4)

    @pl.when(jnp.logical_not(inner))
    def _():
        sent(rrecv.at[0], 2)
        sent(rrecv.at[0], 4)

    @pl.when(diagonal)
    def _():
        sent(mcol.at[0:7], 1)

    @pl.when(jnp.logical_not(diagonal))
    def _():
        sent(mcol, 1)

    sent(rrecv, 3)
    sent(gra.at[0:3], 5)
    sent(gra.at[0, 0:3], 6)
    sent(grt, 7)
    sent(dwrecv.at[0:7], 8)
    sent(frecv.at[0:7], 9)
    sent(f1recv.at[0:15], 10)
    sent(f2recv.at[0:7], 11)
    sent(e1recv.at[0:15], 12)
    sent(e1recv.at[0:15], 13)
    sent(e3out.at[0:896, :], 14)


def hand_over(*refs):
    copies = [pltpu.make_async_copy(refs[i], refs[5 + i], refs[10].at[i]) for i in range(5)]
    for copy in copies:
        copy.start()
    for copy in copies:
        copy.wait()


def local(x, occ, w1, w2, wo, cot):
    hbm = pl.BlockSpec(memory_space=pl.ANY)
    vmem = pl.BlockSpec(memory_space=pltpu.VMEM)
    dma = pltpu.SemaphoreType.DMA
    scratch = [
        pltpu.VMEM((NS, NQ, NCH), BF16),
        pltpu.VMEM((NQ, 2 * NS), jnp.int32),
        pltpu.VMEM((NP, NCH), BF16),
        pltpu.VMEM((NP, NCH), BF16),
        pltpu.VMEM((1024, NZ), BF16),
        pltpu.VMEM((32, 64, NZ), BF16),
        pltpu.VMEM((16, NS), BF16),
        pltpu.VMEM((4, 16, NS), BF16),
        pltpu.VMEM((8, 16, NS), BF16),
        pltpu.VMEM((2, 1024, 128), F32),
        pltpu.VMEM((1024, 128), F32),
        pltpu.VMEM((NQ, NS, NCH), BF16),
        pltpu.VMEM((256, NS), F32),
        pltpu.VMEM((256, NS), BF16),
        pltpu.VMEM((256, NS), BF16),
        pltpu.VMEM((4, 2, 256, NS), BF16),
        pltpu.VMEM((2, 8, 256, NS), BF16),
        pltpu.VMEM((64, NCH), BF16),
        pltpu.VMEM((1024, NZ), BF16),
        pltpu.VMEM((1024, NZ), F32),
        pltpu.VMEM((16, 128), F32),
        pltpu.VMEM((32, 128), F32),
        pltpu.VMEM((1024, PAIRS), F32),
        pltpu.VMEM((2, PAIRS, NZ), BF16),
        pltpu.VMEM((1024, PAIRS), BF16),
        pltpu.VMEM((1024, 256), BF16),
        pltpu.VMEM((256, 1024), BF16),
        pltpu.VMEM((NZ, 1024), BF16),
        pltpu.VMEM((2, PAIRS, 256), BF16),
        pltpu.VMEM((1024, PAIRS), BF16),
        pltpu.VMEM((4, 4, 256, NS), BF16),
        pltpu.VMEM((4, 4, 4, 64, NS), BF16),
        pltpu.VMEM((2, 4, 2, 64, NS), BF16),
        pltpu.VMEM((2, 4, 2, 64, NS), BF16),
        pltpu.VMEM((256, NS), BF16),
        pltpu.VMEM((256, NS), BF16),
        pltpu.VMEM((4, 2, 256, NS), BF16),
        pltpu.VMEM((2, 2, 256, NS), BF16),
        pltpu.VMEM((4, 256, NS), BF16),
        pltpu.VMEM((1024, NZ), F32),
        pltpu.VMEM((8, 128, NZ), BF16),
        pltpu.VMEM((8, 128, NZ), BF16),
        pltpu.VMEM((8, 8, NCH), F32),
        pltpu.VMEM((8, 8, NCH), F32),
        pltpu.VMEM((8, NCH), F32),
        pltpu.VMEM((16, 8, NCH), F32),
        pltpu.VMEM((8, NCH), F32),
        pltpu.VMEM((8, 8, NCH), F32),
        pltpu.VMEM((128, NZ), F32),
        pltpu.VMEM((16, 8, NZ), F32),
        pltpu.VMEM((8, NZ), F32),
        pltpu.VMEM((128, NZ), F32),
        pltpu.VMEM((1024, NZ), BF16),
        pltpu.VMEM((NQ, 128, NS), BF16),
        pltpu.VMEM((2, 1024, 128), F32),
        dma((7,)),
        dma((15,)),
        dma((1,)),
        dma((1,)),
        dma((2, 2)),
        dma((1,)),
        dma((8,)),
        dma((2,)),
        dma((1,)),
        dma((6,)),
        dma((1,)),
        dma((1,)),
        dma((1,)),
        dma((1,)),
        dma((1,)),
        dma((1,)),
        dma((1,)),
        dma((4,)),
    ]
    inc, aadj, fa, sa, dwo = pl.pallas_call(
        kernel,
        out_shape=(
            pltpu.VMEM((32, 64, NZ), BF16),
            pltpu.VMEM((NS, NQ, NCH), BF16),
            pltpu.VMEM((NP, NCH), F32),
            pltpu.VMEM((NP, NCH), F32),
            pltpu.VMEM((1024, NZ), F32),
        ),
        in_specs=[hbm] * 6,
        out_specs=(vmem,) * 5,
        scratch_shapes=scratch,
        compiler_params=pltpu.CompilerParams(vmem_limit_bytes=60 * 1024 * 1024, has_side_effects=True, collective_id=0),
    )(x, occ.T, w1.T, w2.T, wo, cot)
    outs = [pltpu.with_memory_space_constraint(o, pltpu.VMEM) for o in (inc, aadj, fa, sa, dwo)]
    inc, aadj, fa, sa, dwo = pl.pallas_call(
        hand_over,
        out_shape=tuple(jax.ShapeDtypeStruct(o.shape, o.dtype) for o in outs),
        in_specs=[vmem] * 5,
        out_specs=(hbm,) * 5,
        scratch_shapes=[dma((5,))],
    )(*outs)
    return inc, aadj, fa.T, sa.T, dwo


def solution(mesh):
    placed = (
        P("seq", ("row", "col"), None),
        P(None, ("row", "col")),
        P(),
        P(),
        P(),
        P(("row", "seq"), "col", None),
    )
    return jax.shard_map(
        local,
        mesh=mesh,
        in_specs=placed,
        out_specs=(P(("row", "seq"), "col", None), P("seq", ("row", "col"), None), P(), P(), P()),
        check_vma=False,
    )
```

```python
import jax
import jax.numpy as jnp
from jax import lax
from jax.experimental import pallas as pl
from jax.experimental.pallas import tpu as pltpu
from jax.sharding import PartitionSpec as P

F32 = jnp.float32
BF16 = jnp.bfloat16
MESH = pl.DeviceIdType.MESH

NS = 128
NQ = 8
NCH = 256
NP = 32
NZ = 128
HALF = 512
PAIRS = 2048


def dot(a, b, ca, cb):
    return lax.dot_general(a, b, (((ca,), (cb,)), ((), ())), preferred_element_type=F32)


def both_halves(ref, rows):
    return jnp.concatenate([ref[0, rows, :], ref[1, rows, :]], axis=1)


def kernel(
    x_hbm,
    occ_hbm,
    w1_hbm,
    w2_hbm,
    wo_hbm,
    cot_hbm,
    inc_ref,
    aadj_ref,
    fa_ref,
    sa_ref,
    dwo_ref,
    x_ref,
    occ_ref,
    w1_ref,
    w2_ref,
    wo_ref,
    cot_ref,
    msend,
    mrow,
    mcol,
    xh,
    rs,
    nres,
    tmp,
    lsend,
    rsend,
    lrecv,
    rrecv,
    wt,
    wsplit,
    wide,
    inv,
    over_lanes,
    dpre,
    s12,
    d2,
    lscr,
    lturn,
    wturn,
    rscr,
    beo,
    grsend,
    gra,
    grb,
    grc,
    grt,
    grown,
    glp,
    gls,
    glown,
    dwf,
    dwsend,
    dwrecv,
    fsend,
    frecv,
    f1,
    f1recv,
    f2,
    f2recv,
    e1,
    e1recv,
    e2,
    e3,
    e3out,
    gown,
    oscr,
    io_sem,
    ss,
    rs_mr,
    rs_mc,
    rs_l,
    rs_ls,
    rs_r,
    rs_gs,
    rs_go,
    rs_gr,
    rs_gt,
    rs_dw,
    rs_f,
    rs_f1,
    rs_f2,
    rs_e1,
    rs_e2,
    rs_e3,
):
    r, c, q = lax.axis_index("row"), lax.axis_index("col"), lax.axis_index("seq")
    inner = q == c // 4
    diagonal = r == c
    me = r * 2 + q
    core, z = lax.rem(c, 2), c // 2
    sibling = (r, c + 1 - 2 * core, q)
    def place(col, m, h):
        dz = lax.rem(m // 2 - col // 2 + 4, 4)
        down = lax.rem(m, 2) * (1 + 2 * (dz // 2))
        return lax.rem(col // 4 + 2 * h + down, 4), lax.rem(lax.rem(col, 4) + 6 - dz, 4)

    def held(y, x):
        dz = lax.rem(6 - x + lax.rem(c, 4), 4)
        down = lax.rem(y - c // 4 + 4, 4)
        odd = lax.rem(down, 2)
        return lax.rem(c // 2 + dz, 4) * 2 + odd, lax.rem(down // 2 + odd * (dz // 2), 2)

    holder_y, holder_x = place(r, c, q)
    holder_slot = (holder_y // 2, lax.rem(holder_y, 2) * 4 + holder_x)
    holder = (holder_slot[1], r, holder_slot[0])
    y0, x0 = q * 2 + r // 4, lax.rem(r, 4)
    owner = (c, *held(y0, x0))
    other = (r, lax.rem(c + 1, 8), q)

    def plane(t):
        m = lax.rem(me + t, 16)
        return m, (m // 2, c, lax.rem(m, 2))

    def line(t):
        m = lax.rem(c + t, 8)
        return m, (r, m, q)

    def far(src, dst, ssem, rsem, dev):
        return pltpu.make_async_remote_copy(
            src_ref=src, dst_ref=dst, send_sem=ssem, recv_sem=rsem, device_id=dev, device_id_type=MESH
        )

    def put(own, src, dst, ssem, rsem, dev):
        @pl.when(own)
        def _():
            pltpu.make_async_copy(src, dst, rsem).start()

        @pl.when(jnp.logical_not(own))
        def _():
            far(src, dst, ssem, rsem, dev).start()

    def arrived(size, mark):
        far(size, size, ss.at[0], mark, other).wait_recv()

    def sent(size, step):
        far(size, size, ss.at[step], rs_r.at[0], other).wait_send()

    load_wo = pltpu.make_async_copy(wo_hbm, wo_ref, io_sem.at[0])
    load_cot = pltpu.make_async_copy(cot_hbm, cot_ref, io_sem.at[1])

    load_x = pltpu.make_async_copy(x_hbm, x_ref, io_sem.at[3])
    load_occ = pltpu.make_async_copy(occ_hbm, occ_ref, io_sem.at[4])
    load_w1 = pltpu.make_async_copy(w1_hbm, w1_ref, io_sem.at[5])
    load_w2 = pltpu.make_async_copy(w2_hbm, w2_ref, io_sem.at[6])
    for load in (load_x, load_occ, load_w1, load_w2, load_wo, load_cot):
        load.start()

    barrier = pltpu.get_barrier_semaphore()

    def mask_to(t):
        return (lax.rem(r + t, 8), r, q)

    def mask_from(t):
        return (c, lax.rem(c + t, 8), q)

    @pl.loop(1, 8)
    def _(t):
        pl.semaphore_signal(barrier, inc=1, device_id=mask_to(t), device_id_type=MESH)
        pl.semaphore_signal(barrier, inc=1, device_id=mask_from(t), device_id_type=MESH)

    @pl.loop(1, 16)
    def _(t):
        pl.semaphore_signal(barrier, inc=1, device_id=plane(t)[1], device_id_type=MESH)

    @pl.loop(1, 8)
    def _(t):
        pl.semaphore_signal(barrier, inc=1, device_id=line(t)[1], device_id_type=MESH)

    across = (r, lax.rem(z + 3 - 2 * lax.rem(z, 2), 4) * 2 + core, 1 - q)

    def at(y, x):
        return (lax.rem(y, 2) * 4 + x, c, y // 2)

    def along_x(t):
        return at(y0, lax.rem(x0 + t, 4))

    def along_y(t):
        return at(lax.rem(y0 + t, 4), x0)

    def along_z(t):
        return (r, lax.rem(z + t, 4) * 2 + core, q)

    def block(dy, dx, first, last):
        y, x = lax.rem(y0 + dy, 4), lax.rem(x0 + dx, 4)
        h, m = y // 2, lax.rem(y, 2) * 4 + x
        return rrecv.at[h, m, first:last, :]

    @pl.loop(1, 4)
    def _(t):
        dev = (r, lax.rem(z + t, 4) * 2 + core, 1 - q)
        pl.semaphore_signal(barrier, inc=1, device_id=dev, device_id_type=MESH)

    for dev in (holder, owner):
        pl.semaphore_signal(barrier, inc=1, device_id=dev, device_id_type=MESH)

    @pl.when(jnp.logical_not(diagonal))
    def _():
        for dev in (mask_to(0), mask_from(0)):
            pl.semaphore_signal(barrier, inc=1, device_id=dev, device_id_type=MESH)

    load_occ.wait()
    occ = occ_ref[...].astype(F32)
    msend[...] = jnp.concatenate([occ[:, :NS], occ[:, NS:]], axis=0).astype(BF16)

    load_x.wait()
    @pl.loop(0, 8)
    def _(t):
        xb = x_ref[pl.ds(t * 16, 16)].astype(F32).reshape(128, NCH)
        xc = xb - jnp.mean(xb, axis=-1, keepdims=True)
        rstd = lax.rsqrt(jnp.mean(xc * xc, axis=-1, keepdims=True) + 1e-05)
        z = xc * rstd
        xh[0, pl.ds(t * 128, 128), :] = z[:, :128]
        xh[1, pl.ds(t * 128, 128), :] = z[:, 128:]
        rs[pl.ds(t * 128, 128), :] = jnp.broadcast_to(rstd, (128, 128))

    load_w1.wait()
    load_w2.wait()
    wt[0:NP, :] = w1_ref[...]
    wt[NP:, :] = w2_ref[...]
    mine = msend[...].astype(F32)
    mine = jnp.where(q == 0, mine[:NQ], mine[NQ:])
    for k in range(NQ):
        n = both_halves(xh, pl.ds(k, NS, stride=NQ)).astype(BF16)
        nres[k] = n
        p = dot(wt[...], n, 1, 1) * mine[k : k + 1, :]
        lsend[k * NP : (k + 1) * NP, :] = p[:NP].astype(BF16)
        tmp[pl.ds(k, NP, stride=NQ), :] = p[NP:]
    rsend[...] = tmp[...].astype(BF16)

    pl.semaphore_wait(barrier, jnp.where(diagonal, 41, 43))

    mine_of_line = lax.rem(jnp.where(inner, z, z + 3 - 2 * lax.rem(z, 2)), 2)
    seq_of_line = jnp.where(inner, q, 1 - q)
    given = lrecv.at[mine_of_line * 2 + core, seq_of_line]
    given_mark = rs_l.at[mine_of_line, seq_of_line]

    def left_along():
        for t in range(1, 4):
            far(given, given, ss.at[2], given_mark, along_z(t)).start()
        far(given, given, ss.at[2], rs_ls.at[0], sibling).start()

    @pl.when(inner)
    def _():
        lrecv[lax.rem(c, 4), q] = lsend[...]
        left_along()

    @pl.when(jnp.logical_not(inner))
    def _():
        far(lsend, lrecv.at[lax.rem(c, 4), q], ss.at[2], rs_l.at[lax.rem(c, 4) // 2, q], across).start()

    far(rsend, rrecv.at[holder_slot[0], holder_slot[1]], ss.at[3], rs_r.at[0], holder).start()

    put(diagonal, msend, mcol.at[c], ss.at[1], rs_mc.at[0], mask_to(0))

    @pl.loop(1, 8)
    def _(t):
        far(msend, mcol.at[c], ss.at[1], rs_mc.at[0], mask_to(t)).start()

    @pl.when(inner)
    def _():
        m = lax.rem(c, 4)
        pltpu.make_async_copy(msend, mrow.at[m], rs_mr.at[0]).start()

        @pl.loop(1, 8)
        def _(t):
            far(msend, mrow.at[m], ss.at[0], rs_mr.at[0], line(t)[1]).start()

    load_wo.wait()
    wide[...] = wo_ref[...].astype(F32)
    for e in range(NP):
        wsplit[(e % 2) * HALF + (e // 2) * NP : (e % 2) * HALF + (e // 2 + 1) * NP, :] = wide[pl.ds(e, NP, stride=NP), :].astype(BF16)

    wturn[...] = wsplit[...].T

    lane = lax.broadcasted_iota(jnp.int32, (NP, 128), 1)
    low = lax.rem(lane // 8, 2) == 0

    def in_turn(lo, hi):
        return jnp.concatenate([v[m * 8 : m * 8 + 8] for m in range(8) for v in (lo, hi)], axis=0).astype(BF16)

    load_cot.wait()
    for k in range(16):
        lo, hi = cot_ref[k].astype(F32), cot_ref[k + 16].astype(F32)
        s12[0, k * 128 : (k + 1) * 128, :] = in_turn(lo, hi)
        s12[1, k * 128 : (k + 1) * 128, :] = in_turn(hi, lo)

    def outer_adjoint(t):
        here = pl.ds(pl.multiple_of(t * 256, 256), 256)
        even, odd = wsplit[:HALF], wsplit[HALF:]
        plain, turned_s = s12[0, here, :], s12[1, here, :]
        halves = (
            (dot(even, plain, 1, 1), dot(odd, turned_s, 1, 1)),
            (dot(even, turned_s, 1, 1), dot(odd, plain, 1, 1)),
        )
        for u in range(2):
            for half, (a, b) in enumerate(halves):
                at = pl.ds(pl.multiple_of(half * HALF + (t * 2 + u) * NP, NP), NP)
                for p in range(16):
                    va = a[p * NP : (p + 1) * NP, u * 128 : (u + 1) * 128]
                    vb = b[p * NP : (p + 1) * NP, u * 128 : (u + 1) * 128]
                    dpre[at, p * 128 : (p + 1) * 128] = jnp.where(low, va, vb)

    pl.loop(0, 4)(outer_adjoint)

    @pl.when(jnp.logical_not(inner))
    def _():
        arrived(given, given_mark)
        left_along()

    came = block(0, 0, 0, 256)
    arrived(came, rs_r.at[0])
    upper, lower = block(0, 0, 0, 128), block(0, 0, 128, 256)
    for t in range(1, 4):
        far(upper, upper, ss.at[3], rs_r.at[4 - t], along_x(t)).start()
        far(lower, lower, ss.at[3], rs_r.at[7 - t], along_y(t)).start()
    for t in range(1, 4):
        far(upper, upper, ss.at[3], rs_r.at[7], along_y(t)).start()
        far(lower, lower, ss.at[3], rs_r.at[7], along_x(t)).start()

    pl.loop(4, 8)(outer_adjoint)

    arrived(mrow, rs_mr.at[0])
    arrived(mcol, rs_mc.at[0])

    count = jnp.zeros((64, 32), F32)
    count_lanes = jnp.zeros((32, 128), F32)
    for h in range(2):
        rows = jnp.concatenate([mrow[m].astype(F32)[h * NQ : (h + 1) * NQ] for m in range(4)], axis=0).astype(BF16)
        groups = [mcol[m].astype(F32)[h * NQ : (h + 1) * NQ] for m in range(8)]
        cols = jnp.concatenate(groups, axis=0).astype(BF16)
        twice = jnp.concatenate([g for g in groups for _ in range(2)], axis=0).astype(BF16)
        count = count + dot(cols, rows, 1, 1)
        count_lanes = count_lanes + dot(rows, twice, 1, 1)
    over_lanes[...] = 1.0 / (count_lanes + 0.001)
    inv[...] = jnp.where(low[:16], over_lanes[:16], over_lanes[16:])

    @pl.loop(0, 32)
    def _(i):
        rows = pl.ds(pl.multiple_of(i * NP, NP), NP)
        d2[rows, :] = (dpre[rows, :] * jnp.concatenate([over_lanes[pl.ds(i, 1), :]] * 16, axis=1)).astype(BF16)

    for t in range(1, 4):
        zt = lax.rem(z + t, 4)
        in_half = zt // 2 == q
        pp = lax.rem(jnp.where(in_half, zt, zt + 3 - 2 * lax.rem(zt, 2)), 2)
        h = jnp.where(in_half, q, 1 - q)
        slot = lrecv.at[pp * 2 + core, h]
        arrived(slot, rs_l.at[pp, h])
        far(slot, slot, ss.at[2], rs_ls.at[0], sibling).start()

    for t in range(1, 4):
        half = block(0, t, 0, 128)
        arrived(half, rs_r.at[t])
        for u in range(1, 4):
            far(half, half, ss.at[3], rs_r.at[7], along_y(u)).start()
        half = block(t, 0, 128, 256)
        arrived(half, rs_r.at[3 + t])
        for u in range(1, 4):
            far(half, half, ss.at[3], rs_r.at[7], along_x(u)).start()

    def put_right(dy, dx, pairs):
        y, x = lax.rem(y0 + dy, 4), lax.rem(x0 + dx, 4)
        h, m = y // 2, lax.rem(y, 2) * 4 + x
        col, seq = held(y, x)
        lanes = pl.ds(pl.multiple_of(seq * NS, NS), NS)
        first = col * 16
        for p in pairs:
            at = pl.ds(pl.multiple_of(p * 128 + first, 16), 16)
            v = rrecv[h, m, p * 16 : (p + 1) * 16, :]
            w = v.astype(F32)
            rscr[0, at, lanes] = v
            rscr[1, at, lanes] = jnp.concatenate([w[8:], w[:8]], axis=0).astype(BF16)

    put_right(0, 0, range(16))
    for t in range(1, 4):
        put_right(0, t, range(8))
        put_right(t, 0, range(8, 16))

    arrived(lrecv.at[0:2], rs_ls.at[0])
    for h in range(2):
        for m in range(4):
            lscr[m * 256 : (m + 1) * 256, h * NS : (h + 1) * NS] = lrecv[m, h]
            lturn[h * NS : (h + 1) * NS, m * 256 : (m + 1) * 256] = lrecv[m, h].T

    def right_part(t):
        a = dot(lturn[...], d2[:, t * 512 : (t + 1) * 512], 1, 0).astype(BF16)
        for u in range(4):
            at = pl.ds((t * 4 + u) * 16, 16)
            for h in range(2):
                gt = a[h * NS : (h + 1) * NS, u * 128 : (u + 1) * 128].T
                for m in range(8):
                    y, x = place(c, m, h)
                    grsend[y, x, at, :] = gt[m * 16 : (m + 1) * 16]

    for n in range(4):
        right_part(n)
        rows = slice(n * 64, (n + 1) * 64)
        for t in range(1, 4):
            y, x = lax.rem(y0 + t, 4), lax.rem(x0 + t, 4)
            part = grsend.at[:, x, rows, :] if n % 2 else grsend.at[y, :, rows, :]
            to = along_x(t) if n % 2 else along_y(t)
            far(part, gra.at[n, t], ss.at[5], rs_gr.at[n], to).start()

    over = 1.0 / (count + 0.001)
    for k in range(16):
        lo, hi = [
            cot_ref[i].astype(F32) * jnp.broadcast_to(over[:, i : i + 1], (64, NZ)) for i in (k, k + 16)
        ]
        s12[0, k * 128 : (k + 1) * 128, :] = in_turn(lo, hi)
        s12[1, k * 128 : (k + 1) * 128, :] = in_turn(hi, lo)

    arrived(grsend.at[0:3], rs_r.at[7])
    for t in range(1, 4):
        put_right(0, t, range(8, 16))
        put_right(t, 0, range(8))
        for u in range(1, 4):
            put_right(t, u, range(16))

    def outer_product(t):
        here = pl.ds(pl.multiple_of(t * 512, 512), 512)
        a = dot(lscr[:HALF], rscr[0, here, :], 1, 1)
        b = dot(lscr[HALF:], rscr[1, here, :], 1, 1)
        for u in range(4):
            lanes = slice(u * 128, (u + 1) * 128)
            even = pl.ds(pl.multiple_of((t * 4 + u) * NP, NP), NP)
            odd = pl.ds(pl.multiple_of(HALF + (t * 4 + u) * NP, NP), NP)
            for k in range(16):
                lo = a[k * NP : (k + 1) * NP, lanes]
                hi = b[k * NP : (k + 1) * NP, lanes]
                beo[even, k * 128 : (k + 1) * 128] = jnp.where(low, lo, hi).astype(BF16)
                beo[odd, k * 128 : (k + 1) * 128] = jnp.where(low, hi, lo).astype(BF16)

    pl.loop(0, 2)(outer_product)

    pl.loop(2, 4)(outer_product)

    for h in range(2):
        part = dot(beo[h * HALF : (h + 1) * HALF], s12[h], 1, 0)
        for p in range(16):
            dwf[pl.ds(2 * p + h, NP, stride=NP), :] = part[p * NP : (p + 1) * NP]
    for m in range(8):
        dwsend[m] = dwf[m * 128 : (m + 1) * 128, :].astype(BF16)
    pltpu.make_async_copy(dwsend.at[c], dwrecv.at[c], rs_dw.at[0]).start()

    @pl.loop(1, 8)
    def _(t):
        m = lax.rem(c + t, 8)
        far(dwsend.at[m], dwrecv.at[c], ss.at[8], rs_dw.at[0], (r, m, q)).start()

    for i in range(2):
        for half in range(2):
            part = 2 * half + i
            rows = slice(part * 64, (part + 1) * 64)
            arrived(gra.at[part, 1:4], rs_gr.at[part])
            for n in range(4):
                own = grsend[n, x0, rows, :] if i else grsend[y0, n, rows, :]
                total = own.astype(F32)
                for t in range(1, 4):
                    total = total + gra[part, t, n].astype(F32)
                grb[i, n, half] = total.astype(BF16)
        for t in range(1, 4):
            if i:
                far(grb.at[i, lax.rem(y0 + t, 4)], grc.at[i, t], ss.at[6], rs_gr.at[4 + i], along_y(t)).start()
            else:
                far(grb.at[i, lax.rem(x0 + t, 4)], grc.at[i, t], ss.at[6], rs_gr.at[4 + i], along_x(t)).start()

    def left_piece(pp, k):
        rows = pl.ds(pl.multiple_of((pp * 2 + k) * 256, 256), 256)
        g = dot(d2[rows, :], rscr[0], 1, 0)
        for h in range(2):
            glp[pp * 2 + k, h] = g[:, h * NS : (h + 1) * NS].astype(BF16)

    for pp in range(2):
        left_piece(pp, 1 - core)
        far(glp.at[pp * 2 + 1 - core], gls.at[pp], ss.at[4], rs_gs.at[pp], sibling).start()
    for pp in range(2):
        left_piece(pp, core)

    for pp in range(2):
        arrived(gls.at[pp], rs_gs.at[pp])
        m = pp * 2 + core
        for h in range(2):
            glp[m, h] = (glp[m, h].astype(F32) + gls[pp, h].astype(F32)).astype(BF16)
            put(
                jnp.logical_and(2 * q + pp == z, q == h),
                glp.at[m, h],
                glown.at[z],
                ss.at[4],
                rs_go.at[0],
                (r, 4 * q + m, h),
            )

    low_rows = lax.rem(lax.broadcasted_iota(jnp.int32, (NZ, 128), 1) // 8, 2) == 0

    def update(t):
        here = pl.ds(pl.multiple_of(t * 256, 256), 256)
        a = dot(wturn[:, :HALF], beo[:HALF, here], 1, 0)
        b = dot(wturn[:, HALF:], beo[HALF:, here], 1, 0)
        for u in range(2):
            k = t * 2 + u
            odd = b[:, u * 128 : (u + 1) * 128]
            odd = jnp.where(low_rows, pltpu.roll(odd, 120, 1), pltpu.roll(odd, 8, 1))
            o = ((a[:, u * 128 : (u + 1) * 128] + odd) * inv[pl.ds(k, 1), :]).astype(BF16).T.astype(F32)
            inc_ref[k] = jnp.concatenate([o[m * 16 : m * 16 + 8] for m in range(8)], axis=0).astype(BF16)
            inc_ref[k + 16] = jnp.concatenate([o[m * 16 + 8 : m * 16 + 16] for m in range(8)], axis=0).astype(BF16)

    pl.loop(0, 2)(update)

    for i in range(2):
        own = grb[i, y0] if i else grb[i, x0]
        total = own.astype(F32)
        arrived(grc.at[i, 1:4], rs_gr.at[4 + i])
        for t in range(1, 4):
            total = total + grc[i, t].astype(F32)
        for half in range(2):
            part = 2 * half + i
            grt[part * 64 : (part + 1) * 64, :] = total[half].astype(BF16)
    far(grt, grown, ss.at[7], rs_gt.at[0], owner).start()

    pl.loop(2, 5)(update)

    arrived(dwrecv, rs_dw.at[0])
    total = dwrecv[0].astype(F32)
    for m in range(1, 8):
        total = total + dwrecv[m].astype(F32)
    e1[...] = total

    @pl.loop(1, 16)
    def _(t):
        m, dev = plane(t)
        far(e1.at[pl.ds(pl.multiple_of(m * 8, 8), 8), :], e1recv.at[t], ss.at[12], rs_e1.at[0], dev).start()

    pl.loop(5, 8)(update)

    arrived(glown, rs_go.at[0])
    arrived(grown, rs_gt.at[0])
    gl = glown[0].astype(F32)
    for m in range(1, 4):
        gl = gl + glown[m].astype(F32)
    tmp[...] = grown[...].astype(F32)
    fsum = jnp.zeros((128, NCH), F32)
    for k in range(NQ):
        g = jnp.concatenate([gl[k * NP : (k + 1) * NP], tmp[pl.ds(k, NP, stride=NQ), :]], axis=0)
        g = g * mine[k : k + 1, :]
        high = g.astype(BF16)
        rest = (g - high.astype(F32)).astype(BF16)
        g2 = jnp.concatenate([high, rest], axis=0)
        gown[k] = g2
        fsum = fsum + dot(g2, nres[k], 1, 0)
    fsum = fsum[:64] + fsum[64:]
    for m in range(8):
        fsend[m] = fsum[m * 8 : (m + 1) * 8]
    pltpu.make_async_copy(fsend.at[c], frecv.at[c], rs_f.at[0]).start()

    @pl.loop(1, 8)
    def _(t):
        m = lax.rem(c + t, 8)
        far(fsend.at[m], frecv.at[c], ss.at[9], rs_f.at[0], (r, m, q)).start()

    arrived(e1recv.at[1:16], rs_e1.at[0])
    total = e1[pl.ds(pl.multiple_of(me * 8, 8), 8), :]
    for t in range(1, 16):
        total = total + e1recv[t]
    e2[...] = total
    pltpu.make_async_copy(e2, e3.at[pl.ds(pl.multiple_of(me * 8, 8), 8), :], rs_e2.at[0]).start()

    @pl.loop(1, 16)
    def _(t):
        m, dev = plane(t)
        far(e2, e3.at[pl.ds(pl.multiple_of(me * 8, 8), 8), :], ss.at[13], rs_e2.at[0], dev).start()

    w2x = jnp.concatenate([wt[...], wt[...]], axis=0)

    def adjoint(k):
        d = dot(gown[k], w2x, 0, 0)
        at = pl.ds(k, NS, stride=NQ)
        z = both_halves(xh, at)
        scale = rs[at, :]
        m1 = jnp.mean(d, axis=-1, keepdims=True)
        m2 = jnp.mean(d * z, axis=-1, keepdims=True)
        o = d - m1 - z * m2
        oscr[0, at, :] = scale * o[:, :128]
        oscr[1, at, :] = scale * o[:, 128:]

    for k in range(NQ):
        adjoint(k)

    @pl.loop(0, 8)
    def _(t):
        aadj_ref[pl.ds(t * 16, 16)] = both_halves(oscr, pl.ds(t * 128, 128)).reshape(16, NQ, NCH).astype(BF16)


    arrived(frecv, rs_f.at[0])
    total = frecv[0]
    for m in range(1, 8):
        total = total + frecv[m]
    f1[...] = total
    pltpu.make_async_copy(f1, f1recv.at[me], rs_f1.at[0]).start()

    @pl.loop(1, 16)
    def _(t):
        m = lax.rem(me + t, 16)
        far(f1, f1recv.at[me], ss.at[10], rs_f1.at[0], (m // 2, c, lax.rem(m, 2))).start()

    arrived(e3, rs_e2.at[0])
    rows = pl.ds(pl.multiple_of(c * 128, 128), 128)
    e3out[rows, :] = e3[...].astype(BF16)
    chunk = e3out.at[rows, :]
    far(chunk, chunk, ss.at[14], rs_e3.at[0], sibling).start()
    for t in range(1, 4):
        far(chunk, chunk, ss.at[14], rs_e3.at[4 - t], along_z(t)).start()

    arrived(f1recv, rs_f1.at[0])
    total = f1recv[0]
    for m in range(1, 16):
        total = total + f1recv[m]
    f2[...] = total
    pltpu.make_async_copy(f2, f2recv.at[c], rs_f2.at[0]).start()

    @pl.loop(1, 8)
    def _(t):
        far(f2, f2recv.at[c], ss.at[11], rs_f2.at[0], (r, lax.rem(c + t, 8), q)).start()

    for t in range(1, 4):
        m = lax.rem(z + t, 4) * 2 + core
        chunk = e3out.at[pl.ds(pl.multiple_of(m * 128, 128), 128), :]
        arrived(chunk, rs_e3.at[t])
        far(chunk, chunk, ss.at[14], rs_e3.at[0], sibling).start()

    arrived(e3out.at[0:512, :], rs_e3.at[0])
    dwo_ref[...] = e3out[...].astype(F32)

    arrived(f2recv, rs_f2.at[0])
    fa_ref[...] = jnp.concatenate([f2recv[m] for m in range(4)], axis=0)
    sa_ref[...] = jnp.concatenate([f2recv[m] for m in range(4, 8)], axis=0)

    @pl.when(inner)
    def _():
        sent(mcol.at[0:7], 0)
        sent(rrecv.at[0, 0:7], 2)
        sent(rrecv.at[0, 0:7], 4)

    @pl.when(jnp.logical_not(inner))
    def _():
        sent(rrecv.at[0], 2)
        sent(rrecv.at[0], 4)

    @pl.when(diagonal)
    def _():
        sent(mcol.at[0:7], 1)

    @pl.when(jnp.logical_not(diagonal))
    def _():
        sent(mcol, 1)

    sent(rrecv, 3)
    sent(gra.at[0:3], 5)
    sent(gra.at[0, 0:3], 6)
    sent(grt, 7)
    sent(dwrecv.at[0:7], 8)
    sent(frecv.at[0:7], 9)
    sent(f1recv.at[0:15], 10)
    sent(f2recv.at[0:7], 11)
    sent(e1recv.at[0:15], 12)
    sent(e1recv.at[0:15], 13)
    sent(e3out.at[0:896, :], 14)


def hand_over(*refs):
    copies = [pltpu.make_async_copy(refs[i], refs[5 + i], refs[10].at[i]) for i in range(5)]
    for copy in copies:
        copy.start()
    for copy in copies:
        copy.wait()


def local(x, occ, w1, w2, wo, cot):
    hbm = pl.BlockSpec(memory_space=pl.ANY)
    vmem = pl.BlockSpec(memory_space=pltpu.VMEM)
    dma = pltpu.SemaphoreType.DMA
    scratch = [
        pltpu.VMEM((NS, NQ, NCH), BF16),
        pltpu.VMEM((NQ, 2 * NS), jnp.int32),
        pltpu.VMEM((NP, NCH), BF16),
        pltpu.VMEM((NP, NCH), BF16),
        pltpu.VMEM((1024, NZ), BF16),
        pltpu.VMEM((32, 64, NZ), BF16),
        pltpu.VMEM((16, NS), BF16),
        pltpu.VMEM((4, 16, NS), BF16),
        pltpu.VMEM((8, 16, NS), BF16),
        pltpu.VMEM((2, 1024, 128), F32),
        pltpu.VMEM((1024, 128), F32),
        pltpu.VMEM((NQ, NS, NCH), BF16),
        pltpu.VMEM((256, NS), F32),
        pltpu.VMEM((256, NS), BF16),
        pltpu.VMEM((256, NS), BF16),
        pltpu.VMEM((4, 2, 256, NS), BF16),
        pltpu.VMEM((2, 8, 256, NS), BF16),
        pltpu.VMEM((64, NCH), BF16),
        pltpu.VMEM((1024, NZ), BF16),
        pltpu.VMEM((1024, NZ), F32),
        pltpu.VMEM((16, 128), F32),
        pltpu.VMEM((32, 128), F32),
        pltpu.VMEM((1024, PAIRS), F32),
        pltpu.VMEM((2, PAIRS, NZ), BF16),
        pltpu.VMEM((1024, PAIRS), BF16),
        pltpu.VMEM((1024, 256), BF16),
        pltpu.VMEM((256, 1024), BF16),
        pltpu.VMEM((NZ, 1024), BF16),
        pltpu.VMEM((2, PAIRS, 256), BF16),
        pltpu.VMEM((1024, PAIRS), BF16),
        pltpu.VMEM((4, 4, 256, NS), BF16),
        pltpu.VMEM((4, 4, 4, 64, NS), BF16),
        pltpu.VMEM((2, 4, 2, 64, NS), BF16),
        pltpu.VMEM((2, 4, 2, 64, NS), BF16),
        pltpu.VMEM((256, NS), BF16),
        pltpu.VMEM((256, NS), BF16),
        pltpu.VMEM((4, 2, 256, NS), BF16),
        pltpu.VMEM((2, 2, 256, NS), BF16),
        pltpu.VMEM((4, 256, NS), BF16),
        pltpu.VMEM((1024, NZ), F32),
        pltpu.VMEM((8, 128, NZ), BF16),
        pltpu.VMEM((8, 128, NZ), BF16),
        pltpu.VMEM((8, 8, NCH), F32),
        pltpu.VMEM((8, 8, NCH), F32),
        pltpu.VMEM((8, NCH), F32),
        pltpu.VMEM((16, 8, NCH), F32),
        pltpu.VMEM((8, NCH), F32),
        pltpu.VMEM((8, 8, NCH), F32),
        pltpu.VMEM((128, NZ), F32),
        pltpu.VMEM((16, 8, NZ), F32),
        pltpu.VMEM((8, NZ), F32),
        pltpu.VMEM((128, NZ), F32),
        pltpu.VMEM((1024, NZ), BF16),
        pltpu.VMEM((NQ, 128, NS), BF16),
        pltpu.VMEM((2, 1024, 128), F32),
        dma((7,)),
        dma((15,)),
        dma((1,)),
        dma((1,)),
        dma((2, 2)),
        dma((1,)),
        dma((8,)),
        dma((2,)),
        dma((1,)),
        dma((6,)),
        dma((1,)),
        dma((1,)),
        dma((1,)),
        dma((1,)),
        dma((1,)),
        dma((1,)),
        dma((1,)),
        dma((4,)),
    ]
    inc, aadj, fa, sa, dwo = pl.pallas_call(
        kernel,
        out_shape=(
            pltpu.VMEM((32, 64, NZ), BF16),
            pltpu.VMEM((NS, NQ, NCH), BF16),
            pltpu.VMEM((NP, NCH), F32),
            pltpu.VMEM((NP, NCH), F32),
            pltpu.VMEM((1024, NZ), F32),
        ),
        in_specs=[hbm] * 6,
        out_specs=(vmem,) * 5,
        scratch_shapes=scratch,
        compiler_params=pltpu.CompilerParams(vmem_limit_bytes=60 * 1024 * 1024, has_side_effects=True, collective_id=0),
    )(x, occ.T, w1.T, w2.T, wo, cot)
    outs = [pltpu.with_memory_space_constraint(o, pltpu.VMEM) for o in (inc, aadj, fa, sa, dwo)]
    inc, aadj, fa, sa, dwo = pl.pallas_call(
        hand_over,
        out_shape=tuple(jax.ShapeDtypeStruct(o.shape, o.dtype) for o in outs),
        in_specs=[vmem] * 5,
        out_specs=(hbm,) * 5,
        scratch_shapes=[dma((5,))],
    )(*outs)
    return inc, aadj, fa.T, sa.T, dwo


def solution(mesh):
    placed = (
        P("seq", ("row", "col"), None),
        P(None, ("row", "col")),
        P(),
        P(),
        P(),
        P(("row", "seq"), "col", None),
    )
    return jax.shard_map(
        local,
        mesh=mesh,
        in_specs=placed,
        out_specs=(P(("row", "seq"), "col", None), P("seq", ("row", "col"), None), P(), P(), P()),
        check_vma=False,
    )
```

```python
import jax
import jax.numpy as jnp
from jax import lax
from jax.experimental import pallas as pl
from jax.experimental.pallas import tpu as pltpu
from jax.sharding import PartitionSpec as P

F32 = jnp.float32
BF16 = jnp.bfloat16
MESH = pl.DeviceIdType.MESH

NS = 128
NQ = 8
NCH = 256
NP = 32
NZ = 128
HALF = 512
PAIRS = 2048


def dot(a, b, ca, cb):
    return lax.dot_general(a, b, (((ca,), (cb,)), ((), ())), preferred_element_type=F32)


def both_halves(ref, rows):
    return jnp.concatenate([ref[0, rows, :], ref[1, rows, :]], axis=1)


def kernel(
    x_hbm,
    occ_hbm,
    w1_hbm,
    w2_hbm,
    wo_hbm,
    cot_hbm,
    inc_ref,
    aadj_ref,
    fa_ref,
    sa_ref,
    dwo_ref,
    x_ref,
    occ_ref,
    w1_ref,
    w2_ref,
    wo_ref,
    cot_ref,
    msend,
    mrow,
    mcol,
    xh,
    rs,
    nres,
    tmp,
    lsend,
    rsend,
    lrecv,
    rrecv,
    wt,
    wsplit,
    wide,
    inv,
    over_lanes,
    dpre,
    s12,
    d2,
    lscr,
    lturn,
    wturn,
    rscr,
    beo,
    grsend,
    gra,
    grb,
    grc,
    grt,
    grown,
    glp,
    gls,
    glown,
    dwf,
    dwsend,
    dwrecv,
    fsend,
    frecv,
    f1,
    f1recv,
    f2,
    f2recv,
    e1,
    e1recv,
    e2,
    e3,
    e3out,
    gown,
    oscr,
    io_sem,
    ss,
    rs_mr,
    rs_mc,
    rs_l,
    rs_ls,
    rs_r,
    rs_gs,
    rs_go,
    rs_gr,
    rs_gt,
    rs_dw,
    rs_f,
    rs_f1,
    rs_f2,
    rs_e1,
    rs_e2,
    rs_e3,
):
    r, c, q = lax.axis_index("row"), lax.axis_index("col"), lax.axis_index("seq")
    inner = q == c // 4
    me = r * 2 + q
    core, z = lax.rem(c, 2), c // 2
    sibling = (r, c + 1 - 2 * core, q)
    def place(col, m, h):
        dz = lax.rem(m // 2 - col // 2 + 4, 4)
        down = lax.rem(m, 2) * (1 + 2 * (dz // 2))
        return lax.rem(col // 4 + 2 * h + down, 4), lax.rem(lax.rem(col, 4) + 6 - dz, 4)

    def held(y, x):
        dz = lax.rem(6 - x + lax.rem(c, 4), 4)
        down = lax.rem(y - c // 4 + 4, 4)
        odd = lax.rem(down, 2)
        return lax.rem(c // 2 + dz, 4) * 2 + odd, lax.rem(down // 2 + odd * (dz // 2), 2)

    holder_y, holder_x = place(r, c, q)
    holder_slot = (holder_y // 2, lax.rem(holder_y, 2) * 4 + holder_x)
    holder = (holder_slot[1], r, holder_slot[0])
    y0, x0 = q * 2 + r // 4, lax.rem(r, 4)
    owner = (c, *held(y0, x0))
    other = (r, lax.rem(c + 1, 8), q)

    def plane(t):
        m = lax.rem(me + t, 16)
        return m, (m // 2, c, lax.rem(m, 2))

    def line(t):
        m = lax.rem(c + t, 8)
        return m, (r, m, q)

    def far(src, dst, ssem, rsem, dev):
        return pltpu.make_async_remote_copy(
            src_ref=src, dst_ref=dst, send_sem=ssem, recv_sem=rsem, device_id=dev, device_id_type=MESH
        )

    def put(own, src, dst, ssem, rsem, dev):
        @pl.when(own)
        def _():
            pltpu.make_async_copy(src, dst, rsem).start()

        @pl.when(jnp.logical_not(own))
        def _():
            far(src, dst, ssem, rsem, dev).start()

    def arrived(size, mark):
        far(size, size, ss.at[0], mark, other).wait_recv()

    def sent(size, step):
        far(size, size, ss.at[step], rs_r.at[0], other).wait_send()

    load_wo = pltpu.make_async_copy(wo_hbm, wo_ref, io_sem.at[0])
    load_cot = pltpu.make_async_copy(cot_hbm, cot_ref, io_sem.at[1])

    load_x = pltpu.make_async_copy(x_hbm, x_ref, io_sem.at[3])
    load_occ = pltpu.make_async_copy(occ_hbm, occ_ref, io_sem.at[4])
    load_w1 = pltpu.make_async_copy(w1_hbm, w1_ref, io_sem.at[5])
    load_w2 = pltpu.make_async_copy(w2_hbm, w2_ref, io_sem.at[6])
    for load in (load_x, load_occ, load_w1, load_w2, load_wo, load_cot):
        load.start()

    barrier = pltpu.get_barrier_semaphore()

    @pl.loop(1, 16)
    def _(t):
        pl.semaphore_signal(barrier, inc=1, device_id=plane(t)[1], device_id_type=MESH)

    @pl.loop(1, 8)
    def _(t):
        pl.semaphore_signal(barrier, inc=1, device_id=line(t)[1], device_id_type=MESH)

    across = (r, lax.rem(z + 3 - 2 * lax.rem(z, 2), 4) * 2 + core, 1 - q)

    def at(y, x):
        return (lax.rem(y, 2) * 4 + x, c, y // 2)

    def along_x(t):
        return at(y0, lax.rem(x0 + t, 4))

    def along_y(t):
        return at(lax.rem(y0 + t, 4), x0)

    def along_z(t):
        return (r, lax.rem(z + t, 4) * 2 + core, q)

    def block(dy, dx, first, last):
        y, x = lax.rem(y0 + dy, 4), lax.rem(x0 + dx, 4)
        h, m = y // 2, lax.rem(y, 2) * 4 + x
        return rrecv.at[h, m, first:last, :]

    @pl.loop(1, 4)
    def _(t):
        dev = (r, lax.rem(z + t, 4) * 2 + core, 1 - q)
        pl.semaphore_signal(barrier, inc=1, device_id=dev, device_id_type=MESH)

    for dev in (holder, owner):
        pl.semaphore_signal(barrier, inc=1, device_id=dev, device_id_type=MESH)

    load_occ.wait()
    occ = occ_ref[...].astype(F32)
    msend[...] = jnp.concatenate([occ[:, :NS], occ[:, NS:]], axis=0).astype(BF16)

    load_x.wait()
    @pl.loop(0, 8)
    def _(t):
        xb = x_ref[pl.ds(t * 16, 16)].astype(F32).reshape(128, NCH)
        xc = xb - jnp.mean(xb, axis=-1, keepdims=True)
        rstd = lax.rsqrt(jnp.mean(xc * xc, axis=-1, keepdims=True) + 1e-05)
        z = xc * rstd
        xh[0, pl.ds(t * 128, 128), :] = z[:, :128]
        xh[1, pl.ds(t * 128, 128), :] = z[:, 128:]
        rs[pl.ds(t * 128, 128), :] = jnp.broadcast_to(rstd, (128, 128))

    load_w1.wait()
    load_w2.wait()
    wt[0:NP, :] = w1_ref[...]
    wt[NP:, :] = w2_ref[...]
    mine = msend[...].astype(F32)
    mine = jnp.where(q == 0, mine[:NQ], mine[NQ:])
    for k in range(NQ):
        n = both_halves(xh, pl.ds(k, NS, stride=NQ)).astype(BF16)
        nres[k] = n
        p = dot(wt[...], n, 1, 1) * mine[k : k + 1, :]
        lsend[k * NP : (k + 1) * NP, :] = p[:NP].astype(BF16)
        tmp[pl.ds(k, NP, stride=NQ), :] = p[NP:]
    rsend[...] = tmp[...].astype(BF16)

    pl.semaphore_wait(barrier, 27)

    mine_of_line = lax.rem(jnp.where(inner, z, z + 3 - 2 * lax.rem(z, 2)), 2)
    seq_of_line = jnp.where(inner, q, 1 - q)
    given = lrecv.at[mine_of_line * 2 + core, seq_of_line]
    given_mark = rs_l.at[mine_of_line, seq_of_line]

    def left_along():
        for t in range(1, 4):
            far(given, given, ss.at[2], given_mark, along_z(t)).start()
        far(given, given, ss.at[2], rs_ls.at[0], sibling).start()

    @pl.when(inner)
    def _():
        lrecv[lax.rem(c, 4), q] = lsend[...]
        left_along()

    @pl.when(jnp.logical_not(inner))
    def _():
        far(lsend, lrecv.at[lax.rem(c, 4), q], ss.at[2], rs_l.at[lax.rem(c, 4) // 2, q], across).start()

    far(rsend, rrecv.at[holder_slot[0], holder_slot[1]], ss.at[3], rs_r.at[0], holder).start()

    @pl.when(q == 0)
    def _():
        far(msend, mcol.at[c], ss.at[1], rs_mc.at[0], holder).start()

    @pl.when(inner)
    def _():
        m = lax.rem(c, 4)
        pltpu.make_async_copy(msend, mrow.at[m], rs_mr.at[0]).start()

        @pl.loop(1, 8)
        def _(t):
            far(msend, mrow.at[m], ss.at[0], rs_mr.at[0], line(t)[1]).start()

    load_wo.wait()
    wide[...] = wo_ref[...].astype(F32)
    for e in range(NP):
        wsplit[(e % 2) * HALF + (e // 2) * NP : (e % 2) * HALF + (e // 2 + 1) * NP, :] = wide[pl.ds(e, NP, stride=NP), :].astype(BF16)

    wturn[...] = wsplit[...].T

    lane = lax.broadcasted_iota(jnp.int32, (NP, 128), 1)
    low = lax.rem(lane // 8, 2) == 0

    def in_turn(lo, hi):
        return jnp.concatenate([v[m * 8 : m * 8 + 8] for m in range(8) for v in (lo, hi)], axis=0).astype(BF16)

    load_cot.wait()
    for k in range(16):
        lo, hi = cot_ref[k].astype(F32), cot_ref[k + 16].astype(F32)
        s12[0, k * 128 : (k + 1) * 128, :] = in_turn(lo, hi)
        s12[1, k * 128 : (k + 1) * 128, :] = in_turn(hi, lo)

    def outer_adjoint(t):
        here = pl.ds(pl.multiple_of(t * 256, 256), 256)
        even, odd = wsplit[:HALF], wsplit[HALF:]
        plain, turned_s = s12[0, here, :], s12[1, here, :]
        halves = (
            (dot(even, plain, 1, 1), dot(odd, turned_s, 1, 1)),
            (dot(even, turned_s, 1, 1), dot(odd, plain, 1, 1)),
        )
        for u in range(2):
            for half, (a, b) in enumerate(halves):
                at = pl.ds(pl.multiple_of(half * HALF + (t * 2 + u) * NP, NP), NP)
                for p in range(16):
                    va = a[p * NP : (p + 1) * NP, u * 128 : (u + 1) * 128]
                    vb = b[p * NP : (p + 1) * NP, u * 128 : (u + 1) * 128]
                    dpre[at, p * 128 : (p + 1) * 128] = jnp.where(low, va, vb)

    pl.loop(0, 4)(outer_adjoint)

    @pl.when(jnp.logical_not(inner))
    def _():
        arrived(given, given_mark)
        left_along()

    mask_of, mask_seq = owner[1], owner[2]

    @pl.when(mask_seq == 0)
    def _():
        came = mcol.at[mask_of]
        arrived(came, rs_mc.at[0])

        @pl.loop(1, 16)
        def _(t):
            far(came, came, ss.at[15], rs_mc.at[1], plane(t)[1]).start()

    came = block(0, 0, 0, 256)
    arrived(came, rs_r.at[0])
    upper, lower = block(0, 0, 0, 128), block(0, 0, 128, 256)
    for t in range(1, 4):
        far(upper, upper, ss.at[3], rs_r.at[4 - t], along_x(t)).start()
        far(lower, lower, ss.at[3], rs_r.at[7 - t], along_y(t)).start()
    for t in range(1, 4):
        far(upper, upper, ss.at[3], rs_r.at[7], along_y(t)).start()
        far(lower, lower, ss.at[3], rs_r.at[7], along_x(t)).start()

    pl.loop(4, 8)(outer_adjoint)

    for t in range(1, 4):
        zt = lax.rem(z + t, 4)
        in_half = zt // 2 == q
        pp = lax.rem(jnp.where(in_half, zt, zt + 3 - 2 * lax.rem(zt, 2)), 2)
        h = jnp.where(in_half, q, 1 - q)
        slot = lrecv.at[pp * 2 + core, h]
        arrived(slot, rs_l.at[pp, h])
        far(slot, slot, ss.at[2], rs_ls.at[0], sibling).start()

    for t in range(1, 4):
        half = block(0, t, 0, 128)
        arrived(half, rs_r.at[t])
        for u in range(1, 4):
            far(half, half, ss.at[3], rs_r.at[7], along_y(u)).start()
        half = block(t, 0, 128, 256)
        arrived(half, rs_r.at[3 + t])
        for u in range(1, 4):
            far(half, half, ss.at[3], rs_r.at[7], along_x(u)).start()

    def put_right(dy, dx, pairs):
        y, x = lax.rem(y0 + dy, 4), lax.rem(x0 + dx, 4)
        h, m = y // 2, lax.rem(y, 2) * 4 + x
        col, seq = held(y, x)
        lanes = pl.ds(pl.multiple_of(seq * NS, NS), NS)
        first = col * 16
        for p in pairs:
            at = pl.ds(pl.multiple_of(p * 128 + first, 16), 16)
            v = rrecv[h, m, p * 16 : (p + 1) * 16, :]
            w = v.astype(F32)
            rscr[0, at, lanes] = v
            rscr[1, at, lanes] = jnp.concatenate([w[8:], w[:8]], axis=0).astype(BF16)

    put_right(0, 0, range(16))
    for t in range(1, 4):
        put_right(0, t, range(8))
        put_right(t, 0, range(8, 16))

    arrived(mrow, rs_mr.at[0])

    @pl.when(mask_seq == 0)
    def _():
        arrived(mcol.at[0:7], rs_mc.at[1])

    @pl.when(mask_seq == 1)
    def _():
        arrived(mcol, rs_mc.at[1])


    count = jnp.zeros((64, 32), F32)
    count_lanes = jnp.zeros((32, 128), F32)
    for h in range(2):
        rows = jnp.concatenate([mrow[m].astype(F32)[h * NQ : (h + 1) * NQ] for m in range(4)], axis=0).astype(BF16)
        groups = [mcol[m].astype(F32)[h * NQ : (h + 1) * NQ] for m in range(8)]
        cols = jnp.concatenate(groups, axis=0).astype(BF16)
        twice = jnp.concatenate([g for g in groups for _ in range(2)], axis=0).astype(BF16)
        count = count + dot(cols, rows, 1, 1)
        count_lanes = count_lanes + dot(rows, twice, 1, 1)
    over_lanes[...] = 1.0 / (count_lanes + 0.001)
    inv[...] = jnp.where(low[:16], over_lanes[:16], over_lanes[16:])

    @pl.loop(0, 32)
    def _(i):
        rows = pl.ds(pl.multiple_of(i * NP, NP), NP)
        d2[rows, :] = (dpre[rows, :] * jnp.concatenate([over_lanes[pl.ds(i, 1), :]] * 16, axis=1)).astype(BF16)

    arrived(lrecv.at[0:2], rs_ls.at[0])
    for h in range(2):
        for m in range(4):
            lscr[m * 256 : (m + 1) * 256, h * NS : (h + 1) * NS] = lrecv[m, h]
            lturn[h * NS : (h + 1) * NS, m * 256 : (m + 1) * 256] = lrecv[m, h].T

    def right_part(t):
        a = dot(lturn[...], d2[:, t * 512 : (t + 1) * 512], 1, 0).astype(BF16)
        for u in range(4):
            at = pl.ds((t * 4 + u) * 16, 16)
            for h in range(2):
                gt = a[h * NS : (h + 1) * NS, u * 128 : (u + 1) * 128].T
                for m in range(8):
                    y, x = place(c, m, h)
                    grsend[y, x, at, :] = gt[m * 16 : (m + 1) * 16]

    for n in range(4):
        right_part(n)
        rows = slice(n * 64, (n + 1) * 64)
        for t in range(1, 4):
            y, x = lax.rem(y0 + t, 4), lax.rem(x0 + t, 4)
            part = grsend.at[:, x, rows, :] if n % 2 else grsend.at[y, :, rows, :]
            to = along_x(t) if n % 2 else along_y(t)
            far(part, gra.at[n, t], ss.at[5], rs_gr.at[n], to).start()

    over = 1.0 / (count + 0.001)
    for k in range(16):
        lo, hi = [
            cot_ref[i].astype(F32) * jnp.broadcast_to(over[:, i : i + 1], (64, NZ)) for i in (k, k + 16)
        ]
        s12[0, k * 128 : (k + 1) * 128, :] = in_turn(lo, hi)
        s12[1, k * 128 : (k + 1) * 128, :] = in_turn(hi, lo)

    arrived(grsend.at[0:3], rs_r.at[7])
    for t in range(1, 4):
        put_right(0, t, range(8, 16))
        put_right(t, 0, range(8))
        for u in range(1, 4):
            put_right(t, u, range(16))

    def outer_product(t):
        here = pl.ds(pl.multiple_of(t * 512, 512), 512)
        a = dot(lscr[:HALF], rscr[0, here, :], 1, 1)
        b = dot(lscr[HALF:], rscr[1, here, :], 1, 1)
        for u in range(4):
            lanes = slice(u * 128, (u + 1) * 128)
            even = pl.ds(pl.multiple_of((t * 4 + u) * NP, NP), NP)
            odd = pl.ds(pl.multiple_of(HALF + (t * 4 + u) * NP, NP), NP)
            for k in range(16):
                lo = a[k * NP : (k + 1) * NP, lanes]
                hi = b[k * NP : (k + 1) * NP, lanes]
                beo[even, k * 128 : (k + 1) * 128] = jnp.where(low, lo, hi).astype(BF16)
                beo[odd, k * 128 : (k + 1) * 128] = jnp.where(low, hi, lo).astype(BF16)

    pl.loop(0, 2)(outer_product)

    pl.loop(2, 4)(outer_product)

    for h in range(2):
        part = dot(beo[h * HALF : (h + 1) * HALF], s12[h], 1, 0)
        for p in range(16):
            dwf[pl.ds(2 * p + h, NP, stride=NP), :] = part[p * NP : (p + 1) * NP]
    for m in range(8):
        dwsend[m] = dwf[m * 128 : (m + 1) * 128, :].astype(BF16)
    pltpu.make_async_copy(dwsend.at[c], dwrecv.at[c], rs_dw.at[0]).start()

    @pl.loop(1, 8)
    def _(t):
        m = lax.rem(c + t, 8)
        far(dwsend.at[m], dwrecv.at[c], ss.at[8], rs_dw.at[0], (r, m, q)).start()

    for i in range(2):
        for half in range(2):
            part = 2 * half + i
            rows = slice(part * 64, (part + 1) * 64)
            arrived(gra.at[part, 1:4], rs_gr.at[part])
            for n in range(4):
                own = grsend[n, x0, rows, :] if i else grsend[y0, n, rows, :]
                total = own.astype(F32)
                for t in range(1, 4):
                    total = total + gra[part, t, n].astype(F32)
                grb[i, n, half] = total.astype(BF16)
        for t in range(1, 4):
            if i:
                far(grb.at[i, lax.rem(y0 + t, 4)], grc.at[i, t], ss.at[6], rs_gr.at[4 + i], along_y(t)).start()
            else:
                far(grb.at[i, lax.rem(x0 + t, 4)], grc.at[i, t], ss.at[6], rs_gr.at[4 + i], along_x(t)).start()

    def left_piece(pp, k):
        rows = pl.ds(pl.multiple_of((pp * 2 + k) * 256, 256), 256)
        g = dot(d2[rows, :], rscr[0], 1, 0)
        for h in range(2):
            glp[pp * 2 + k, h] = g[:, h * NS : (h + 1) * NS].astype(BF16)

    for pp in range(2):
        left_piece(pp, 1 - core)
        far(glp.at[pp * 2 + 1 - core], gls.at[pp], ss.at[4], rs_gs.at[pp], sibling).start()
    for pp in range(2):
        left_piece(pp, core)

    for pp in range(2):
        arrived(gls.at[pp], rs_gs.at[pp])
        m = pp * 2 + core
        for h in range(2):
            glp[m, h] = (glp[m, h].astype(F32) + gls[pp, h].astype(F32)).astype(BF16)
            put(
                jnp.logical_and(2 * q + pp == z, q == h),
                glp.at[m, h],
                glown.at[z],
                ss.at[4],
                rs_go.at[0],
                (r, 4 * q + m, h),
            )

    low_rows = lax.rem(lax.broadcasted_iota(jnp.int32, (NZ, 128), 1) // 8, 2) == 0

    def update(t):
        here = pl.ds(pl.multiple_of(t * 256, 256), 256)
        a = dot(wturn[:, :HALF], beo[:HALF, here], 1, 0)
        b = dot(wturn[:, HALF:], beo[HALF:, here], 1, 0)
        for u in range(2):
            k = t * 2 + u
            odd = b[:, u * 128 : (u + 1) * 128]
            odd = jnp.where(low_rows, pltpu.roll(odd, 120, 1), pltpu.roll(odd, 8, 1))
            o = ((a[:, u * 128 : (u + 1) * 128] + odd) * inv[pl.ds(k, 1), :]).astype(BF16).T.astype(F32)
            inc_ref[k] = jnp.concatenate([o[m * 16 : m * 16 + 8] for m in range(8)], axis=0).astype(BF16)
            inc_ref[k + 16] = jnp.concatenate([o[m * 16 + 8 : m * 16 + 16] for m in range(8)], axis=0).astype(BF16)

    pl.loop(0, 2)(update)

    for i in range(2):
        own = grb[i, y0] if i else grb[i, x0]
        total = own.astype(F32)
        arrived(grc.at[i, 1:4], rs_gr.at[4 + i])
        for t in range(1, 4):
            total = total + grc[i, t].astype(F32)
        for half in range(2):
            part = 2 * half + i
            grt[part * 64 : (part + 1) * 64, :] = total[half].astype(BF16)
    far(grt, grown, ss.at[7], rs_gt.at[0], owner).start()

    pl.loop(2, 5)(update)

    arrived(dwrecv, rs_dw.at[0])
    total = dwrecv[0].astype(F32)
    for m in range(1, 8):
        total = total + dwrecv[m].astype(F32)
    e1[...] = total

    @pl.loop(1, 16)
    def _(t):
        m, dev = plane(t)
        far(e1.at[pl.ds(pl.multiple_of(m * 8, 8), 8), :], e1recv.at[t], ss.at[12], rs_e1.at[0], dev).start()

    pl.loop(5, 8)(update)

    arrived(glown, rs_go.at[0])
    arrived(grown, rs_gt.at[0])
    gl = glown[0].astype(F32)
    for m in range(1, 4):
        gl = gl + glown[m].astype(F32)
    tmp[...] = grown[...].astype(F32)
    fsum = jnp.zeros((128, NCH), F32)
    for k in range(NQ):
        g = jnp.concatenate([gl[k * NP : (k + 1) * NP], tmp[pl.ds(k, NP, stride=NQ), :]], axis=0)
        g = g * mine[k : k + 1, :]
        high = g.astype(BF16)
        rest = (g - high.astype(F32)).astype(BF16)
        g2 = jnp.concatenate([high, rest], axis=0)
        gown[k] = g2
        fsum = fsum + dot(g2, nres[k], 1, 0)
    fsum = fsum[:64] + fsum[64:]
    for m in range(8):
        fsend[m] = fsum[m * 8 : (m + 1) * 8]
    pltpu.make_async_copy(fsend.at[c], frecv.at[c], rs_f.at[0]).start()

    @pl.loop(1, 8)
    def _(t):
        m = lax.rem(c + t, 8)
        far(fsend.at[m], frecv.at[c], ss.at[9], rs_f.at[0], (r, m, q)).start()

    arrived(e1recv.at[1:16], rs_e1.at[0])
    total = e1[pl.ds(pl.multiple_of(me * 8, 8), 8), :]
    for t in range(1, 16):
        total = total + e1recv[t]
    e2[...] = total
    pltpu.make_async_copy(e2, e3.at[pl.ds(pl.multiple_of(me * 8, 8), 8), :], rs_e2.at[0]).start()

    @pl.loop(1, 16)
    def _(t):
        m, dev = plane(t)
        far(e2, e3.at[pl.ds(pl.multiple_of(me * 8, 8), 8), :], ss.at[13], rs_e2.at[0], dev).start()

    w2x = jnp.concatenate([wt[...], wt[...]], axis=0)

    def adjoint(k):
        d = dot(gown[k], w2x, 0, 0)
        at = pl.ds(k, NS, stride=NQ)
        z = both_halves(xh, at)
        scale = rs[at, :]
        m1 = jnp.mean(d, axis=-1, keepdims=True)
        m2 = jnp.mean(d * z, axis=-1, keepdims=True)
        o = d - m1 - z * m2
        oscr[0, at, :] = scale * o[:, :128]
        oscr[1, at, :] = scale * o[:, 128:]

    for k in range(NQ):
        adjoint(k)

    @pl.loop(0, 8)
    def _(t):
        aadj_ref[pl.ds(t * 16, 16)] = both_halves(oscr, pl.ds(t * 128, 128)).reshape(16, NQ, NCH).astype(BF16)


    arrived(frecv, rs_f.at[0])
    total = frecv[0]
    for m in range(1, 8):
        total = total + frecv[m]
    f1[...] = total
    pltpu.make_async_copy(f1, f1recv.at[me], rs_f1.at[0]).start()

    @pl.loop(1, 16)
    def _(t):
        m = lax.rem(me + t, 16)
        far(f1, f1recv.at[me], ss.at[10], rs_f1.at[0], (m // 2, c, lax.rem(m, 2))).start()

    arrived(e3, rs_e2.at[0])
    rows = pl.ds(pl.multiple_of(c * 128, 128), 128)
    e3out[rows, :] = e3[...].astype(BF16)
    chunk = e3out.at[rows, :]
    far(chunk, chunk, ss.at[14], rs_e3.at[0], sibling).start()
    for t in range(1, 4):
        far(chunk, chunk, ss.at[14], rs_e3.at[4 - t], along_z(t)).start()

    arrived(f1recv, rs_f1.at[0])
    total = f1recv[0]
    for m in range(1, 16):
        total = total + f1recv[m]
    f2[...] = total
    pltpu.make_async_copy(f2, f2recv.at[c], rs_f2.at[0]).start()

    @pl.loop(1, 8)
    def _(t):
        far(f2, f2recv.at[c], ss.at[11], rs_f2.at[0], (r, lax.rem(c + t, 8), q)).start()

    for t in range(1, 4):
        m = lax.rem(z + t, 4) * 2 + core
        chunk = e3out.at[pl.ds(pl.multiple_of(m * 128, 128), 128), :]
        arrived(chunk, rs_e3.at[t])
        far(chunk, chunk, ss.at[14], rs_e3.at[0], sibling).start()

    arrived(e3out.at[0:512, :], rs_e3.at[0])
    dwo_ref[...] = e3out[...].astype(F32)

    arrived(f2recv, rs_f2.at[0])
    fa_ref[...] = jnp.concatenate([f2recv[m] for m in range(4)], axis=0)
    sa_ref[...] = jnp.concatenate([f2recv[m] for m in range(4, 8)], axis=0)

    @pl.when(inner)
    def _():
        sent(mcol.at[0:7], 0)
        sent(rrecv.at[0, 0:7], 2)
        sent(rrecv.at[0, 0:7], 4)

    @pl.when(jnp.logical_not(inner))
    def _():
        sent(rrecv.at[0], 2)
        sent(rrecv.at[0], 4)

    @pl.when(q == 0)
    def _():
        sent(msend, 1)

    @pl.when(mask_seq == 0)
    def _():
        sent(e1recv.at[0:15], 15)

    sent(rrecv, 3)
    sent(gra.at[0:3], 5)
    sent(gra.at[0, 0:3], 6)
    sent(grt, 7)
    sent(dwrecv.at[0:7], 8)
    sent(frecv.at[0:7], 9)
    sent(f1recv.at[0:15], 10)
    sent(f2recv.at[0:7], 11)
    sent(e1recv.at[0:15], 12)
    sent(e1recv.at[0:15], 13)
    sent(e3out.at[0:896, :], 14)


def hand_over(*refs):
    copies = [pltpu.make_async_copy(refs[i], refs[5 + i], refs[10].at[i]) for i in range(5)]
    for copy in copies:
        copy.start()
    for copy in copies:
        copy.wait()


def local(x, occ, w1, w2, wo, cot):
    hbm = pl.BlockSpec(memory_space=pl.ANY)
    vmem = pl.BlockSpec(memory_space=pltpu.VMEM)
    dma = pltpu.SemaphoreType.DMA
    scratch = [
        pltpu.VMEM((NS, NQ, NCH), BF16),
        pltpu.VMEM((NQ, 2 * NS), jnp.int32),
        pltpu.VMEM((NP, NCH), BF16),
        pltpu.VMEM((NP, NCH), BF16),
        pltpu.VMEM((1024, NZ), BF16),
        pltpu.VMEM((32, 64, NZ), BF16),
        pltpu.VMEM((16, NS), BF16),
        pltpu.VMEM((4, 16, NS), BF16),
        pltpu.VMEM((8, 16, NS), BF16),
        pltpu.VMEM((2, 1024, 128), F32),
        pltpu.VMEM((1024, 128), F32),
        pltpu.VMEM((NQ, NS, NCH), BF16),
        pltpu.VMEM((256, NS), F32),
        pltpu.VMEM((256, NS), BF16),
        pltpu.VMEM((256, NS), BF16),
        pltpu.VMEM((4, 2, 256, NS), BF16),
        pltpu.VMEM((2, 8, 256, NS), BF16),
        pltpu.VMEM((64, NCH), BF16),
        pltpu.VMEM((1024, NZ), BF16),
        pltpu.VMEM((1024, NZ), F32),
        pltpu.VMEM((16, 128), F32),
        pltpu.VMEM((32, 128), F32),
        pltpu.VMEM((1024, PAIRS), F32),
        pltpu.VMEM((2, PAIRS, NZ), BF16),
        pltpu.VMEM((1024, PAIRS), BF16),
        pltpu.VMEM((1024, 256), BF16),
        pltpu.VMEM((256, 1024), BF16),
        pltpu.VMEM((NZ, 1024), BF16),
        pltpu.VMEM((2, PAIRS, 256), BF16),
        pltpu.VMEM((1024, PAIRS), BF16),
        pltpu.VMEM((4, 4, 256, NS), BF16),
        pltpu.VMEM((4, 4, 4, 64, NS), BF16),
        pltpu.VMEM((2, 4, 2, 64, NS), BF16),
        pltpu.VMEM((2, 4, 2, 64, NS), BF16),
        pltpu.VMEM((256, NS), BF16),
        pltpu.VMEM((256, NS), BF16),
        pltpu.VMEM((4, 2, 256, NS), BF16),
        pltpu.VMEM((2, 2, 256, NS), BF16),
        pltpu.VMEM((4, 256, NS), BF16),
        pltpu.VMEM((1024, NZ), F32),
        pltpu.VMEM((8, 128, NZ), BF16),
        pltpu.VMEM((8, 128, NZ), BF16),
        pltpu.VMEM((8, 8, NCH), F32),
        pltpu.VMEM((8, 8, NCH), F32),
        pltpu.VMEM((8, NCH), F32),
        pltpu.VMEM((16, 8, NCH), F32),
        pltpu.VMEM((8, NCH), F32),
        pltpu.VMEM((8, 8, NCH), F32),
        pltpu.VMEM((128, NZ), F32),
        pltpu.VMEM((16, 8, NZ), F32),
        pltpu.VMEM((8, NZ), F32),
        pltpu.VMEM((128, NZ), F32),
        pltpu.VMEM((1024, NZ), BF16),
        pltpu.VMEM((NQ, 128, NS), BF16),
        pltpu.VMEM((2, 1024, 128), F32),
        dma((7,)),
        dma((16,)),
        dma((1,)),
        dma((2,)),
        dma((2, 2)),
        dma((1,)),
        dma((8,)),
        dma((2,)),
        dma((1,)),
        dma((6,)),
        dma((1,)),
        dma((1,)),
        dma((1,)),
        dma((1,)),
        dma((1,)),
        dma((1,)),
        dma((1,)),
        dma((4,)),
    ]
    inc, aadj, fa, sa, dwo = pl.pallas_call(
        kernel,
        out_shape=(
            pltpu.VMEM((32, 64, NZ), BF16),
            pltpu.VMEM((NS, NQ, NCH), BF16),
            pltpu.VMEM((NP, NCH), F32),
            pltpu.VMEM((NP, NCH), F32),
            pltpu.VMEM((1024, NZ), F32),
        ),
        in_specs=[hbm] * 6,
        out_specs=(vmem,) * 5,
        scratch_shapes=scratch,
        compiler_params=pltpu.CompilerParams(vmem_limit_bytes=60 * 1024 * 1024, has_side_effects=True, collective_id=0),
    )(x, occ.T, w1.T, w2.T, wo, cot)
    outs = [pltpu.with_memory_space_constraint(o, pltpu.VMEM) for o in (inc, aadj, fa, sa, dwo)]
    inc, aadj, fa, sa, dwo = pl.pallas_call(
        hand_over,
        out_shape=tuple(jax.ShapeDtypeStruct(o.shape, o.dtype) for o in outs),
        in_specs=[vmem] * 5,
        out_specs=(hbm,) * 5,
        scratch_shapes=[dma((5,))],
    )(*outs)
    return inc, aadj, fa.T, sa.T, dwo


def solution(mesh):
    placed = (
        P("seq", ("row", "col"), None),
        P(None, ("row", "col")),
        P(),
        P(),
        P(),
        P(("row", "seq"), "col", None),
    )
    return jax.shard_map(
        local,
        mesh=mesh,
        in_specs=placed,
        out_specs=(P(("row", "seq"), "col", None), P("seq", ("row", "col"), None), P(), P(), P()),
        check_vma=False,
    )
```
